32 devices in a mesh: seq: 8 (over z, y), ch: 4 (over x, core).
Axes of the slice: x: 2, y: 2, z: 4, core: 2. Of those that a mesh axis runs over, the one named last changes fastest.
Arguments:
- streams: bfloat16 [3, 1024, 4096], P(None, 'seq', 'ch'), may hold values from -6 to 6
- short_taps: float32 [3, 3, 4096], P(None, None, 'ch'), may hold values from -2.5 to 2.5
- long_filter: float32 [1024, 4096], P('seq', 'ch'), may hold values from -10 to 10
- skip_bias: float32 [4096], P('ch'), may hold values from -2.5 to 2.5
- norm_gain: float32 [4096], P('ch'), may hold values from 0.5 to 1.5
- cotangent: bfloat16 [1024, 4096], P('seq', 'ch'), may hold values from -6 to 6
Outputs:
- normed: bfloat16 [1024, 4096], P('seq', 'ch')
- stream_grads: bfloat16 [3, 1024, 4096], P(None, 'seq', 'ch')
The draws below stay inside these ranges and needn't reach their ends.
All inputs are finite; a program needn't handle non-finite values.
Results may differ from the reference program's by a relative error of at most 0.001.
Values sent between devices are 32-bit elements; how exact they have to be, the bound alone decides.
No kernel may reach another device: no remote copies, remote signals or barrier semaphores. Data moves between devices by JAX's collectives and lax.ppermute only.
A program may use at most 64 MiB of HBM per device.

```python
import jax
import jax.numpy as jnp
from jax import lax

CHANNELS = 4096
TAPS = 3
SEQLEN = 1024


def draw_long_filter(key, part):
    noise_key, select_key, fast_key, slow_key, place_key, drop_key, tail_key = jax.random.split(jax.random.fold_in(key, 17), 7)
    delay_offsets = jnp.arange(SEQLEN, dtype=jnp.float32)[:, None]
    channel_pos = jnp.arange(CHANNELS, dtype=jnp.float32)[None, :]
    random_jitter = jnp.clip(jax.random.normal(noise_key, (SEQLEN, CHANNELS), jnp.float32), -4.0, 4.0)
    tail_jitter = jnp.clip(jax.random.normal(tail_key, (SEQLEN, CHANNELS), jnp.float32), -4.0, 4.0)
    slow_share = 0.5
    rise_factor = 3.0
    selector = jax.random.uniform(select_key, (1, CHANNELS), jnp.float32)
    fast_rate = 1.0 / jax.random.uniform(fast_key, (1, CHANNELS), jnp.float32, 30.0, 50.0)
    slow_rate = jax.random.uniform(slow_key, (1, CHANNELS), jnp.float32, 0.2, 2.0) / SEQLEN
    falloff_speed = jnp.where(selector < slow_share, slow_rate, fast_rate)
    spike_locations = jax.random.uniform(place_key, (4,), jnp.float32, 0.0, 1.0 * SEQLEN)
    damping_multipliers = jax.random.uniform(drop_key, (4,), jnp.float32, 0.5, 0.8)
    spike_logarithm = jnp.sum(jnp.log(damping_multipliers)[None, None, :] * (delay_offsets[:, :, None] >= spike_locations[None, None, :]).astype(jnp.float32), axis=-1)
    signal_power = jnp.sqrt(2.0 * falloff_speed / (1.0 - jnp.exp(-2.0 * falloff_speed * SEQLEN)))
    filter_magnitude = rise_factor ** (channel_pos / (CHANNELS - 1))
    head_part = random_jitter * signal_power * jnp.exp(-falloff_speed * delay_offsets)
    tail_part = tail_jitter * jnp.sqrt(0.25 / SEQLEN)
    return (head_part + tail_part) * filter_magnitude * jnp.exp(spike_logarithm)


def steps_of(rng, dims, cuts, low, high):
    gain = 1.0
    for dim, blocks in cuts:
        heights = jax.random.uniform(jax.random.fold_in(jax.random.fold_in(rng, 6), dim), (blocks,), jnp.float32, low / len(cuts), high / len(cuts))
        gain = gain * jnp.repeat(jnp.exp(heights), dims[dim] // blocks).reshape((-1,) + (1,) * (len(dims) - 1 - dim))
    return gain


def noise(key, dims, deviation, bound, pieces=(), kind=jnp.bfloat16):
    entries = jax.random.normal(key, dims, jnp.float32) * deviation
    if len(pieces) > 0:
        entries = steps_of(key, dims, pieces, -0.22, 0.18) * entries
    return jnp.clip(entries, min=-bound, max=bound).astype(kind)


def setup_inputs(seed: int = 0) -> dict:
    arg_keys = jax.random.split(jax.random.key(seed), 7)
    streams = noise(arg_keys[0], (3, SEQLEN, CHANNELS), 1.0, 6.0, ((1, 8), (2, 4)))
    short_taps = noise(arg_keys[1], (3, TAPS, CHANNELS), 0.6, 2.5, ((2, 4),), jnp.float32)
    long_filter = draw_long_filter(jax.random.fold_in(arg_keys[6], 71), 0)
    skip_bias = noise(arg_keys[3], (CHANNELS,), 0.3, 2.5, ((0, 4),), jnp.float32)
    norm_gain = jnp.clip(1.0 + 0.1 * jax.random.normal(arg_keys[4], (CHANNELS,), jnp.float32), 0.5, 1.5)
    cotangent = noise(arg_keys[5], (SEQLEN, CHANNELS), 1.0, 6.0, ((0, 8), (1, 4)))
    return {"streams": streams, "short_taps": short_taps, "long_filter": long_filter, "skip_bias": skip_bias, "norm_gain": norm_gain, "cotangent": cotangent}


def short_filter(series, tap_table):
    rim_rows = tap_table.shape[1] - 1
    length = series.shape[1]
    padded = jnp.pad(series, ((0, 0), (rim_rows, 0), (0, 0)))
    summed = jnp.zeros_like(series)
    for offset in range(tap_table.shape[1]):
        summed = summed + tap_table[:, offset, None, :] * padded[:, rim_rows - offset:rim_rows - offset + length, :]
    return summed

def short_transpose(series, tap_table):
    rim_rows = tap_table.shape[1] - 1
    length = series.shape[1]
    padded = jnp.pad(series, ((0, 0), (0, rim_rows), (0, 0)))
    summed = jnp.zeros_like(series)
    for offset in range(tap_table.shape[1]):
        summed = summed + tap_table[:, offset, None, :] * padded[:, offset:offset + length, :]
    return summed

def channel_block(inputs):
    stream_part, tap_part, filter_part, bias_part, cot_part = inputs
    length = stream_part.shape[1]
    shorts = short_filter(stream_part.astype(jnp.float32), tap_part)
    short_q, short_k, short_v = (shorts[0], shorts[1], shorts[2])
    gated_input = short_k * short_v
    span = 2 * length
    filter_spec = jnp.fft.rfft(filter_part, n=span, axis=0)
    convolved = jnp.fft.irfft(filter_spec * jnp.fft.rfft(gated_input, n=span, axis=0), n=span, axis=0)[:length]
    direct = convolved + bias_part * gated_input
    mixed_out = short_q * direct
    cot_wide = cot_part.astype(jnp.float32)
    carried = cot_wide * short_q
    correlated = jnp.fft.irfft(jnp.conj(filter_spec) * jnp.fft.rfft(carried, n=span, axis=0), n=span, axis=0)[:length]
    gated_grad = correlated + bias_part * carried
    short_grad = jnp.stack([cot_wide * direct, gated_grad * short_v, gated_grad * short_k])
    return (mixed_out, short_transpose(short_grad, tap_part))

def reference(streams, short_taps, long_filter, skip_bias, norm_gain, cotangent):
    block_width = min(256, CHANNELS)
    block_count = CHANNELS // block_width

    def by_blocks(array):
        shaped = array.reshape(array.shape[:-1] + (block_count, block_width))
        return jnp.moveaxis(shaped, -2, 0)
    mixed_out, grads = lax.map(channel_block, (by_blocks(streams), by_blocks(short_taps), by_blocks(long_filter), by_blocks(skip_bias), by_blocks(cotangent)))
    mixed_out = jnp.moveaxis(mixed_out, 0, -2).reshape(SEQLEN, CHANNELS)
    grads = jnp.moveaxis(grads, 0, -2).reshape(3, SEQLEN, CHANNELS)
    square_mean = lax.optimization_barrier(jnp.mean(mixed_out * mixed_out, axis=1, keepdims=True))
    normed = (mixed_out * lax.rsqrt(square_mean + 1e-06) * norm_gain).astype(jnp.bfloat16)
    return (normed, grads.astype(jnp.bfloat16))
```

```python
import functools
import math

import jax
import jax.numpy as jnp
import numpy as np
from jax import lax
from jax.experimental import pallas as pl
from jax.experimental.pallas import tpu as pltpu
from jax.sharding import PartitionSpec as P

F32 = jnp.float32
BF16 = jnp.bfloat16
PAD_ROWS = 8
VMEM_BYTES = 48 * 1024 * 1024


def shift_along(block, axis, distance):
    devices = range(lax.axis_size(axis))
    route = [(i - distance, i) for i in devices if i - distance in devices]
    return lax.ppermute(block, axis, route)


def params():
    return pltpu.CompilerParams(vmem_limit_bytes=VMEM_BYTES)


def split_table(table):
    high = table.astype(BF16)
    low = (table - high.astype(np.float64)).astype(BF16)
    return high, low


def stage_tables(blocks, rows):
    period = 2 * blocks * rows
    place = np.arange(rows)

    def angles(first, count):
        bins = first + 2 * blocks * np.arange(count)
        turn = 2.0 * np.pi * ((bins[:, None] * place[None, :]) % period) / period
        return np.cos(turn), np.sin(turn)

    tables = np.zeros((blocks, 2 * rows, 2 * rows))
    half = rows // 2
    cos_0, sin_0 = angles(0, half)
    cos_n, sin_n = angles(blocks, half)
    tables[0, :half, :rows] = cos_0
    tables[0, half:rows, rows:] = cos_n
    tables[0, rows : rows + half, :rows] = -sin_0
    tables[0, rows, :rows] = 1.0 - 2.0 * (place % 2)
    tables[0, rows + half :, rows:] = -sin_n
    for first in range(1, blocks):
        cos_k, sin_k = angles(first, rows)
        tables[first] = np.block([[cos_k, sin_k], [-sin_k, cos_k]])
    return split_table(tables) + split_table(np.swapaxes(tables, 1, 2))


def scaled(value, factor):
    if abs(factor) < 1e-12:
        return None
    if abs(factor - 1.0) < 1e-12:
        return value
    if abs(factor + 1.0) < 1e-12:
        return -value
    return value * factor


def total(terms):
    kept = [term for term in terms if term is not None]
    if not kept:
        return None
    result = kept[0]
    for term in kept[1:]:
        result = result + term
    return result


def plus(left, right):
    return total([left, right])


def minus(left, right):
    return total([left, None if right is None else -right])


def store_split(high_ref, low_ref, index, value):
    high = value.astype(BF16)
    high_ref[index] = high
    low_ref[index] = (value - high.astype(F32)).astype(BF16)


def first_stage(x_ref, high_ref, low_ref, tile):
    blocks, rows = x_ref.shape[0], x_ref.shape[1]
    for start in range(0, rows, tile):
        here = slice(start, start + tile)
        there = slice(rows + start, rows + start + tile)
        x = [x_ref[a, here, :] for a in range(blocks)]
        for k in range(blocks // 2 + 1):
            parts = []
            for parity in (0, 1):
                members = range(parity, blocks, 2)
                turn = [math.pi * ((a * k) % (2 * blocks)) / blocks for a in members]
                parts.append(total([scaled(x[a], math.cos(t)) for a, t in zip(members, turn)]))
                parts.append(total([scaled(x[a], math.sin(t)) for a, t in zip(members, turn)]))
            even_c, even_s, odd_c, odd_s = parts
            if k == 0:
                store_split(high_ref, low_ref, (0, here), plus(even_c, odd_c))
                store_split(high_ref, low_ref, (0, there), minus(even_c, odd_c))
                continue
            store_split(high_ref, low_ref, (k, here), plus(even_c, odd_c))
            store_split(high_ref, low_ref, (k, there), -plus(even_s, odd_s))
            if 2 * k != blocks:
                store_split(high_ref, low_ref, (blocks - k, here), minus(even_c, odd_c))
                store_split(high_ref, low_ref, (blocks - k, there), minus(even_s, odd_s))


def last_stage(v_ref, out_ref, tile):
    blocks, rows = v_ref.shape[0], v_ref.shape[1] // 2
    for start in range(0, rows, tile):
        here = slice(start, start + tile)
        there = slice(rows + start, rows + start + tile)
        first = v_ref[0, here, :]
        last = v_ref[0, there, :]
        re = {k: v_ref[k, here, :] for k in range(1, blocks)}
        im = {k: v_ref[k, there, :] for k in range(1, blocks)}
        for parity in (0, 1):
            sign = 1.0 - 2.0 * parity
            base = first + sign * last
            re_sum = {k: re[k] + sign * re[blocks - k] for k in range(1, blocks // 2)}
            im_sum = {k: im[k] - sign * im[blocks - k] for k in range(1, blocks // 2)}
            re_sum[blocks // 2] = re[blocks // 2]
            im_sum[blocks // 2] = im[blocks // 2]
            for a in range(parity, blocks, 2):
                terms = [base]
                for k in range(1, blocks // 2 + 1):
                    turn = math.pi * ((a * k) % (2 * blocks)) / blocks
                    terms.append(scaled(re_sum[k], math.cos(turn)))
                    terms.append(scaled(im_sum[k], -math.sin(turn)))
                value = total(terms)
                out_ref[a, here, :] = value
                if start == 0 and a > 0:
                    out_ref[a - 1, rows : rows + PAD_ROWS, :] = value[:PAD_ROWS]
    out_ref[blocks - 1, rows : rows + PAD_ROWS, :] = jnp.zeros((PAD_ROWS, out_ref.shape[2]), F32)


def dot(left, right):
    return lax.dot_general(left, right, (((1,), (0,)), ((), ())), preferred_element_type=F32)


def exact_dot(table_high, table_low, high, low):
    return dot(table_high, high) + dot(table_high, low) + dot(table_low, high)


def spectrum_kernel(x_ref, gh_ref, gl_ref, spec_ref, high_ref, low_ref):
    blocks, rows = x_ref.shape[0], x_ref.shape[1]
    first_stage(x_ref, high_ref, low_ref, 32)
    scale = 1.0 / (blocks * rows)
    for k in range(blocks):
        spec = exact_dot(gh_ref[k], gl_ref[k], high_ref[k], low_ref[k]) * scale
        spec_ref[k] = spec
        if k == 0:
            for row in (0, rows):
                spec_ref[0, row : row + 1, :] = 0.5 * spec[row : row + 1]


def product_kernel(conjugate, x_ref, spec_ref, gh_ref, gl_ref, th_ref, tl_ref, out_ref, high_ref, low_ref, v_ref):
    blocks, rows = x_ref.shape[0], x_ref.shape[1]
    first_stage(x_ref, high_ref, low_ref, 32)
    sign = -1.0 if conjugate else 1.0
    for k in range(blocks):
        spec = exact_dot(gh_ref[k], gl_ref[k], high_ref[k], low_ref[k])
        x_re, x_im = spec[:rows], spec[rows:]
        h_re, h_im = spec_ref[k, :rows, :], spec_ref[k, rows:, :]
        cross = x_im * h_im
        if k == 0:
            real_row = lax.broadcasted_iota(jnp.int32, cross.shape, 0) == 0
            out_re = x_re * h_re - sign * jnp.where(real_row, 0.0, cross)
            out_im = jnp.where(real_row, cross, x_im * h_re + sign * (x_re * h_im))
        else:
            out_re = x_re * h_re - sign * cross
            out_im = x_im * h_re + sign * (x_re * h_im)
        out = jnp.concatenate([out_re, out_im], axis=0)
        high = out.astype(BF16)
        low = (out - high.astype(F32)).astype(BF16)
        v_ref[k] = exact_dot(th_ref[k], tl_ref[k], high, low)
    last_stage(v_ref, out_ref, 32)


def scratch(blocks, rows, width, inverse):
    shape = (blocks, 2 * rows, width)
    kept = [pltpu.VMEM(shape, BF16), pltpu.VMEM(shape, BF16)]
    return kept + [pltpu.VMEM(shape, F32)] if inverse else kept


def spectrum(x, tables):
    blocks, rows, width = x.shape
    return pl.pallas_call(
        spectrum_kernel,
        out_shape=jax.ShapeDtypeStruct((blocks, 2 * rows, width), F32),
        scratch_shapes=scratch(blocks, rows, width, False),
        compiler_params=params(),
        name="filter_spectrum",
    )(x, tables[0], tables[1])


def through_filter(x, spec, tables, conjugate):
    blocks, rows, width = x.shape
    return pl.pallas_call(
        functools.partial(product_kernel, conjugate),
        out_shape=jax.ShapeDtypeStruct((blocks, rows + PAD_ROWS, width), F32),
        scratch_shapes=scratch(blocks, rows, width, True),
        compiler_params=params(),
        name="correlation" if conjugate else "convolution",
    )(x, spec, *tables)


def row_number(shape):
    return lax.broadcasted_iota(jnp.int32, shape, 0)


def delayed(x, before, distance):
    moved = pltpu.roll(x, distance, 0)
    rows = row_number(x.shape)
    rim = len(before)
    for row in range(distance):
        moved = jnp.where(rows == row, before[rim - distance + row], moved)
    return moved


def advanced(x, after, distance):
    count = x.shape[0]
    moved = pltpu.roll(x, count - distance, 0)
    rows = row_number(x.shape)
    for row in range(distance):
        moved = jnp.where(rows == count - distance + row, after[row], moved)
    return moved


def rows_of(block):
    return [block[row : row + 1] for row in range(block.shape[0])]


def short_filter_after(after, last, taps):
    known = last + after
    return [
        total([taps[j : j + 1] * known[len(last) + row - j] for j in range(taps.shape[0])])
        for row in range(len(after))
    ]


def short_filter(x, before, taps):
    result = taps[0:1] * x
    for j in range(1, taps.shape[0]):
        result = result + taps[j : j + 1] * delayed(x, before, j)
    return result


def short_transpose(x, after, taps):
    result = taps[0:1] * x
    for j in range(1, taps.shape[0]):
        result = result + taps[j : j + 1] * advanced(x, after, j)
    return result


def gate_kernel(streams_ref, before_ref, taps_ref, cot_ref, gated_ref, carried_ref):
    block = gated_ref.shape[2]
    for part in range(gated_ref.shape[0]):
        lanes = slice(part * block, (part + 1) * block)
        short = [
            short_filter(streams_ref[i, :, lanes].astype(F32), rows_of(before_ref[i, :, lanes]), taps_ref[i, :, lanes])
            for i in range(3)
        ]
        gated_ref[part] = short[1] * short[2]
        carried_ref[part] = cot_ref[:, lanes].astype(F32) * short[0]


def gate(streams, before, taps, cotangent, parts):
    _, rows, width = streams.shape
    block = width // parts
    steps = 4
    span = width // steps
    per_step = parts // steps
    rim, count = before.shape[1], taps.shape[1]
    chunk = jax.ShapeDtypeStruct((parts, rows, block), F32)
    return pl.pallas_call(
        gate_kernel,
        grid=(steps,),
        in_specs=[
            pl.BlockSpec((3, rows, span), lambda i: (0, 0, i)),
            pl.BlockSpec((3, rim, span), lambda i: (0, 0, i)),
            pl.BlockSpec((3, count, span), lambda i: (0, 0, i)),
            pl.BlockSpec((rows, span), lambda i: (0, i)),
        ],
        out_specs=[pl.BlockSpec((per_step, rows, block), lambda i: (i, 0, 0))] * 2,
        out_shape=[chunk, chunk],
        compiler_params=params(),
        name="short_filters",
    )(streams, before, taps, cotangent)


def mix_kernel(streams_ref, before_ref, taps_ref, bias_ref, conv_ref, mixed_ref, square_ref):
    step = pl.program_id(0)
    block = conv_ref.shape[2]
    rows = streams_ref.shape[1]
    squares = jnp.zeros((rows, block), F32)
    for part in range(conv_ref.shape[0]):
        lanes = slice(part * block, (part + 1) * block)
        short = [
            short_filter(streams_ref[i, :, lanes].astype(F32), rows_of(before_ref[i, :, lanes]), taps_ref[i, :, lanes])
            for i in range(3)
        ]
        mixed = short[0] * (conv_ref[part, :rows, :] + bias_ref[:, lanes] * (short[1] * short[2]))
        mixed_ref[:, lanes] = mixed
        squares = squares + mixed * mixed
    row_sums = lax.dot_general(
        jnp.ones((8, block), F32),
        squares,
        (((1,), (1,)), ((), ())),
        precision=lax.Precision.HIGHEST,
        preferred_element_type=F32,
    )[0:1]

    @pl.when(step == 0)
    def _():
        square_ref[...] = row_sums

    @pl.when(step > 0)
    def _():
        square_ref[...] += row_sums


def mix(streams, before, taps, bias, conv):
    _, rows, width = streams.shape
    parts, long_rows, block = conv.shape
    steps = 4
    span = width // steps
    per_step = parts // steps
    rim, count = before.shape[1], taps.shape[1]
    return pl.pallas_call(
        mix_kernel,
        grid=(steps,),
        in_specs=[
            pl.BlockSpec((3, rows, span), lambda i: (0, 0, i)),
            pl.BlockSpec((3, rim, span), lambda i: (0, 0, i)),
            pl.BlockSpec((3, count, span), lambda i: (0, 0, i)),
            pl.BlockSpec((1, span), lambda i: (0, i)),
            pl.BlockSpec((per_step, long_rows, block), lambda i: (i, 0, 0)),
        ],
        out_specs=[
            pl.BlockSpec((rows, span), lambda i: (0, i)),
            pl.BlockSpec((1, rows), lambda i: (0, 0)),
        ],
        out_shape=[
            jax.ShapeDtypeStruct((rows, width), F32),
            jax.ShapeDtypeStruct((1, rows), F32),
        ],
        compiler_params=params(),
        name="mixed_squares",
    )(streams, before, taps, bias, conv)


def finish_kernel(
    channels, streams_ref, before_ref, after_ref, taps_ref, bias_ref, gain_ref, cot_ref, mixed_ref, square_ref,
    conv_ref, corr_ref, normed_ref, grads_ref,
):
    block = conv_ref.shape[2]
    rows = streams_ref.shape[1]
    squares = jnp.broadcast_to(square_ref[...], (block, rows)).T
    scaling = lax.rsqrt(squares / channels + 1e-06)
    rim = after_ref.shape[1]
    for part in range(conv_ref.shape[0]):
        lanes = slice(part * block, (part + 1) * block)
        normed_ref[:, lanes] = (mixed_ref[:, lanes] * scaling * gain_ref[:, lanes]).astype(BF16)
        bias = bias_ref[:, lanes]
        x = [streams_ref[i, :, lanes].astype(F32) for i in range(3)]
        after = [rows_of(after_ref[i, :, lanes]) for i in range(4)]
        taps = [taps_ref[i, :, lanes] for i in range(3)]
        cot = cot_ref[:, lanes].astype(F32)

        def short_grads(short, cotangent, conv, corr):
            direct = conv + bias * (short[1] * short[2])
            gated_grad = corr + bias * (cotangent * short[0])
            return (cotangent * direct, gated_grad * short[2], gated_grad * short[1])

        short = [short_filter(x[i], rows_of(before_ref[i, :, lanes]), taps[i]) for i in range(3)]
        short_after = [short_filter_after(after[i], rows_of(x[i][rows - rim :]), taps[i]) for i in range(3)]
        main = short_grads(short, cot, conv_ref[part, :rows, :], corr_ref[part, :rows, :])
        conv_after = rows_of(conv_ref[part, rows : rows + rim, :])
        corr_after = rows_of(corr_ref[part, rows : rows + rim, :])
        tail = [
            short_grads([short_after[i][row] for i in range(3)], after[3][row], conv_after[row], corr_after[row])
            for row in range(rim)
        ]
        for i in range(3):
            above = [tail[row][i] for row in range(rim)]
            grads_ref[i, :, lanes] = short_transpose(main[i], above, taps[i]).astype(BF16)


def finish(channels, streams, before, after, taps, bias, gain, cotangent, mixed, squares, conv, corr):
    _, rows, width = streams.shape
    parts, long_rows, block = conv.shape
    steps = 4
    span = width // steps
    per_step = parts // steps
    rim, count = before.shape[1], taps.shape[1]
    flat = pl.BlockSpec((rows, span), lambda i: (0, i))
    vector = pl.BlockSpec((1, span), lambda i: (0, i))
    chunk = pl.BlockSpec((per_step, long_rows, block), lambda i: (i, 0, 0))
    return pl.pallas_call(
        functools.partial(finish_kernel, float(channels)),
        grid=(steps,),
        in_specs=[
            pl.BlockSpec((3, rows, span), lambda i: (0, 0, i)),
            pl.BlockSpec((3, rim, span), lambda i: (0, 0, i)),
            pl.BlockSpec((4, after.shape[1], span), lambda i: (0, 0, i)),
            pl.BlockSpec((3, count, span), lambda i: (0, 0, i)),
            vector,
            vector,
            flat,
            flat,
            pl.BlockSpec((1, rows), lambda i: (0, 0)),
            chunk,
            chunk,
        ],
        out_specs=[flat, pl.BlockSpec((3, rows, span), lambda i: (0, 0, i))],
        out_shape=[
            jax.ShapeDtypeStruct((rows, width), BF16),
            jax.ShapeDtypeStruct((3, rows, width), BF16),
        ],
        compiler_params=params(),
        name="norm_and_grads",
    )(streams, before, after, taps, bias, gain, cotangent, mixed, squares, conv, corr)


def swap_blocks(blocks):
    return lax.all_to_all(blocks, "seq", split_axis=0, concat_axis=0, tiled=True)


def by_blocks(rows, parts):
    length, width = rows.shape
    return jnp.swapaxes(rows.reshape(length, parts, width // parts), 0, 1)


def local(streams, short_taps, long_filter, skip_bias, norm_gain, cotangent):
    parts = lax.axis_size("seq")
    rows, width = cotangent.shape
    rim = short_taps.shape[1] - 1
    tables = stage_tables(parts, rows)
    edges = jnp.concatenate([streams[:, :rim].astype(F32), cotangent[None, :rim].astype(F32)], axis=0)
    before = shift_along(streams[:, rows - rim :].astype(F32), "seq", 1)
    after = shift_along(edges, "seq", -1)
    bias, gain = skip_bias[None], norm_gain[None]
    gated, carried = gate(streams, before, short_taps, cotangent, parts)
    sent = jnp.concatenate([by_blocks(long_filter, parts), gated, carried], axis=1)
    got = swap_blocks(sent)
    spec = spectrum(got[:, :rows], tables)
    conv = through_filter(got[:, rows : 2 * rows], spec, tables, False)
    corr = through_filter(got[:, 2 * rows :], spec, tables, True)
    back = swap_blocks(jnp.concatenate([conv, corr], axis=1))
    conv, corr = back[:, : rows + PAD_ROWS], back[:, rows + PAD_ROWS :]
    mixed, squares = mix(streams, before, short_taps, bias, conv)
    squares = lax.psum(squares, "ch")
    channels = width * lax.axis_size("ch")
    return tuple(
        finish(
            channels, streams, before, after, short_taps, bias, gain, cotangent, mixed, squares, conv, corr
        )
    )


EXACTNESS = lax.Precision.HIGHEST


def passed_along(block, axis, distance):
    devices = range(lax.axis_size(axis))
    route = [(i - distance, i) for i in devices if i - distance in devices]
    return lax.ppermute(block, axis, route)


def counting(amount):
    return jnp.arange(amount, dtype=jnp.int32)


def angle_pair(left_index, right_index, period, turning):
    product = left_index[:, None] * right_index[None, :] % period
    angles = product.astype(jnp.float32) * (turning * 2.0 * math.pi / period)
    return (jnp.cos(angles), jnp.sin(angles))


def neighbour_rows(edge_rows, offset):
    return passed_along(edge_rows, "seq", offset)


def swap_middle(blocks):
    return lax.all_to_all(blocks, "seq", split_axis=1, concat_axis=0, tiled=True)


def spread_forward(series):
    length, series_count, chan_width = series.shape
    devices = lax.axis_size("seq")
    position = lax.axis_index("seq")
    sub_rows = length // devices
    period = 2 * length * devices
    gathered = swap_middle(series.reshape(1, length, series_count, chan_width))
    cos_a, sin_a = angle_pair(counting(2 * devices), counting(devices), 2 * devices, -1.0)
    real_part = jnp.einsum("ka,absc->bksc", cos_a, gathered, precision=EXACTNESS)
    imag_part = jnp.einsum("ka,absc->bksc", sin_a, gathered, precision=EXACTNESS)
    spike_locations = position * sub_rows + counting(sub_rows)
    turn_cos, turn_sin = angle_pair(spike_locations, counting(2 * devices), period, -1.0)
    turn_cos = turn_cos[:, :, None, None]
    turn_sin = turn_sin[:, :, None, None]
    turned = jnp.concatenate(
        [real_part * turn_cos - imag_part * turn_sin, real_part * turn_sin + imag_part * turn_cos],
        axis=2,
    )
    swapped = swap_middle(turned)
    cos_b, sin_b = angle_pair(counting(length), counting(length), length, -1.0)
    primary = jnp.einsum("jb,bksc->jksc", cos_b, swapped, precision=EXACTNESS)
    second = jnp.einsum("jb,bksc->jksc", sin_b, swapped, precision=EXACTNESS)
    return (
        primary[:, :, :series_count] - second[:, :, series_count:],
        primary[:, :, series_count:] + second[:, :, :series_count],
    )


def spread_inverse(spec_re, spec_im):
    length, pair_rows, series_count, chan_width = spec_re.shape
    devices = lax.axis_size("seq")
    position = lax.axis_index("seq")
    sub_rows = length // devices
    period = 2 * length * devices
    cos_b, sin_b = angle_pair(counting(length), counting(length), length, 1.0)
    merged = jnp.concatenate([spec_re, spec_im], axis=2)
    primary = jnp.einsum("bj,jksc->kbsc", cos_b, merged, precision=EXACTNESS)
    second = jnp.einsum("bj,jksc->kbsc", sin_b, merged, precision=EXACTNESS)
    turned = jnp.concatenate(
        [
            primary[:, :, :series_count] - second[:, :, series_count:],
            primary[:, :, series_count:] + second[:, :, :series_count],
        ],
        axis=2,
    )
    swapped = swap_middle(turned)
    spike_locations = position * sub_rows + counting(sub_rows)
    turn_cos, turn_sin = angle_pair(counting(2 * devices), spike_locations, period, 1.0)
    turn_cos = turn_cos[:, :, None, None]
    turn_sin = turn_sin[:, :, None, None]
    real_part = swapped[:, :, :series_count]
    imag_part = swapped[:, :, series_count:]
    rotated_re = real_part * turn_cos - imag_part * turn_sin
    rotated_im = real_part * turn_sin + imag_part * turn_cos
    cos_a, sin_a = angle_pair(counting(devices), counting(2 * devices), 2 * devices, 1.0)
    result = jnp.einsum("ak,kbsc->basc", cos_a, rotated_re, precision=EXACTNESS) - jnp.einsum(
        "ak,kbsc->basc", sin_a, rotated_im, precision=EXACTNESS
    )
    returned = swap_middle(result / period)
    return returned.reshape(length, -1, chan_width)


def local_general(streams, short_taps, long_filter, skip_bias, norm_gain, cotangent):
    row_count = streams.shape[1]
    chan_width = streams.shape[2]
    rim_rows = short_taps.shape[1] - 1
    widened = streams.astype(jnp.float32)
    before = neighbour_rows(widened[:, row_count - rim_rows :, :], 1)
    extended = jnp.concatenate([before, widened], axis=1)
    shorts = jnp.zeros_like(widened)
    for offset in range(short_taps.shape[1]):
        shorts = (
            shorts
            + short_taps[:, offset, None, :]
            * extended[:, rim_rows - offset : rim_rows - offset + row_count, :]
        )
    short_q, short_k, short_v = (shorts[0], shorts[1], shorts[2])
    gated_input = short_k * short_v
    cot_wide = cotangent.astype(jnp.float32)
    carried = cot_wide * short_q
    series = jnp.stack([gated_input, long_filter, carried], axis=1)
    spec_re, spec_im = spread_forward(series)
    series_axis = 2
    gated_re = lax.index_in_dim(spec_re, 0, series_axis, keepdims=False)
    gated_im = lax.index_in_dim(spec_im, 0, series_axis, keepdims=False)
    filter_re = lax.index_in_dim(spec_re, 1, series_axis, keepdims=False)
    filter_im = lax.index_in_dim(spec_im, 1, series_axis, keepdims=False)
    carry_re = lax.index_in_dim(spec_re, 2, series_axis, keepdims=False)
    carry_im = lax.index_in_dim(spec_im, 2, series_axis, keepdims=False)
    output_re = filter_re * gated_re - filter_im * gated_im
    output_im = filter_re * gated_im + filter_im * gated_re
    backward_re = filter_re * carry_re + filter_im * carry_im
    backward_im = filter_re * carry_im - filter_im * carry_re
    inverse_re = jnp.stack([output_re, backward_re], axis=series_axis)
    inverse_im = jnp.stack([output_im, backward_im], axis=series_axis)
    result = spread_inverse(inverse_re, inverse_im)
    convolved = result[:, 0]
    correlated = result[:, 1]
    direct = convolved + skip_bias * gated_input
    mixed_out = short_q * direct
    square_sum = lax.psum(jnp.sum(mixed_out * mixed_out, axis=1), "ch")
    scaling = lax.rsqrt(square_sum[:, None] / (chan_width * lax.axis_size("ch")) + 1e-06)
    normed = (mixed_out * scaling * norm_gain).astype(jnp.bfloat16)
    gated_grad = correlated + skip_bias * carried
    short_grad = jnp.stack([cot_wide * direct, gated_grad * short_v, gated_grad * short_k])
    following = neighbour_rows(short_grad[:, :rim_rows, :], -1)
    grad_ext = jnp.concatenate([short_grad, following], axis=1)
    grads = jnp.zeros_like(short_grad)
    for offset in range(short_taps.shape[1]):
        grads = grads + short_taps[:, offset, None, :] * grad_ext[:, offset : offset + row_count, :]
    return (normed, grads.astype(jnp.bfloat16))


def solution(mesh):
    placed = (
        P(None, "seq", "ch"),
        P(None, None, "ch"),
        P("seq", "ch"),
        P("ch"),
        P("ch"),
        P("seq", "ch"),
    )

    def program(streams, short_taps, long_filter, skip_bias, norm_gain, cotangent):
        parts = mesh.shape["seq"]
        width = cotangent.shape[1] // mesh.shape["ch"]
        lanes_filled = width % (128 * parts) == 0 and parts % 4 == 0 and parts <= 16
        return jax.shard_map(
            local if lanes_filled else local_general,
            mesh=mesh,
            in_specs=placed,
            out_specs=(P("seq", "ch"), P(None, "seq", "ch")),
            check_vma=False,
        )(streams, short_taps, long_filter, skip_bias, norm_gain, cotangent)

    return program
```

```python
import functools
import math

import jax
import jax.numpy as jnp
import numpy as np
from jax import lax
from jax.experimental import pallas as pl
from jax.experimental.pallas import tpu as pltpu
from jax.sharding import PartitionSpec as P

F32 = jnp.float32
BF16 = jnp.bfloat16
PAD_ROWS = 8
VMEM_BYTES = 48 * 1024 * 1024


def shift_along(block, axis, distance):
    devices = range(lax.axis_size(axis))
    route = [(i - distance, i) for i in devices if i - distance in devices]
    return lax.ppermute(block, axis, route)


def measured(microseconds):
    return pl.CostEstimate(flops=0, bytes_accessed=int(microseconds * 73800.0), transcendentals=0)


def params():
    return pltpu.CompilerParams(vmem_limit_bytes=VMEM_BYTES)


def scaled(value, factor):
    if abs(factor) < 1e-12:
        return None
    if abs(factor - 1.0) < 1e-12:
        return value
    if abs(factor + 1.0) < 1e-12:
        return -value
    return value * factor


def total(terms):
    kept = [term for term in terms if term is not None]
    if not kept:
        return None
    result = kept[0]
    for term in kept[1:]:
        result = result + term
    return result


def plus(left, right):
    return total([left, right])


def minus(left, right):
    return total([left, None if right is None else -right])


def sending_place(apart, blocks, by_side):
    return (apart % 2) * (blocks // 2) + apart // 2 if by_side else apart


def dot(left, right):
    return lax.dot_general(left, right, (((1,), (0,)), ((), ())), preferred_element_type=F32)


def stage_tables(blocks, rows):
    period = 2 * blocks * rows
    place = np.arange(rows)
    turn = 2.0 * np.pi * ((place[:, None] * place[None, :]) % rows) / rows
    exact = np.concatenate([np.cos(turn), np.sin(turn)], axis=0)
    high = exact.astype(BF16)
    low = (exact - high.astype(np.float64)).astype(BF16)
    columns = -(-2 * (blocks + 1) // 128) * 128
    twiddles = np.zeros((rows, columns), np.float32)
    for k in range(blocks + 1):
        turn = 2.0 * np.pi * ((place * k) % period) / period
        twiddles[:, 2 * k], twiddles[:, 2 * k + 1] = np.cos(turn), np.sin(turn)
    return np.concatenate([high, high], axis=1), low, twiddles


def turned(twiddles, k, re, im, sign):
    if k == 0:
        return re, im
    cos = jnp.broadcast_to(twiddles[:, 2 * k : 2 * k + 1], re.shape)
    sin = jnp.broadcast_to(twiddles[:, 2 * k + 1 : 2 * k + 2], re.shape) * sign
    if im is None:
        return re * cos, re * sin
    return re * cos - im * sin, re * sin + im * cos


def store_split(split_ref, k, here, re, im):
    rows, width = split_ref.shape[1] // 2, split_ref.shape[2] // 2
    for value, lanes in ((re, slice(0, width)), (im, slice(width, 2 * width))):
        if value is None:
            value = jnp.zeros_like(re)
        high = value.astype(BF16)
        split_ref[k, here, lanes] = high
        split_ref[k, slice(rows + here.start, rows + here.stop), lanes] = (value - high.astype(F32)).astype(BF16)


def first_stage(own, x_ref, tw_ref, split_ref, tile):
    blocks, rows = x_ref.shape[0], x_ref.shape[1]
    for start in range(0, rows, tile):
        here = slice(start, start + tile)
        twiddles = tw_ref[here, :]
        x = [x_ref[a ^ own, here, :] for a in range(blocks)]

        def keep(k, re, im):
            store_split(split_ref, k, here, *turned(twiddles, k, re, im, -1.0))

        for k in range(blocks // 2 + 1):
            parts = []
            for parity in (0, 1):
                members = range(parity, blocks, 2)
                turn = [math.pi * ((a * k) % (2 * blocks)) / blocks for a in members]
                parts.append(total([scaled(x[a], math.cos(t)) for a, t in zip(members, turn)]))
                parts.append(total([scaled(x[a], math.sin(t)) for a, t in zip(members, turn)]))
            even_c, even_s, odd_c, odd_s = parts
            keep(k, plus(even_c, odd_c), None if k == 0 else -plus(even_s, odd_s))
            if 2 * k != blocks:
                keep(blocks - k, minus(even_c, odd_c), None if k == 0 else minus(even_s, odd_s))


def second_stage(table_high, table_low, split):
    rows, width = table_low.shape[1], split.shape[1] // 2
    sums = dot(table_high, split) + dot(table_low, split[:rows])
    return sums[:rows, :width], sums[:rows, width:], sums[rows:, :width], sums[rows:, width:]


def spectrum_kernel(own_ref, x_ref, high_ref, low_ref, tw_ref, _, spec_ref, split_ref):
    blocks, rows = x_ref.shape[0], x_ref.shape[1]
    first_stage(own_ref[0], x_ref, tw_ref, split_ref, 32)
    for k in range(blocks + 1):
        scale = (0.5 if k in (0, blocks) else 1.0) / (blocks * rows)
        cos_re, cos_im, sin_re, sin_im = second_stage(high_ref[...], low_ref[...], split_ref[k])
        spec_ref[k, :rows, :] = (cos_re + sin_im) * scale
        spec_ref[k, rows:, :] = (cos_im - sin_re) * scale


def last_stage(own, by_side, re_ref, im_ref, out_ref, tile):
    blocks, rows = re_ref.shape[0] - 1, re_ref.shape[1]
    for start in range(0, rows, tile):
        here = slice(start, start + tile)
        re = [re_ref[k, here, :] for k in range(blocks + 1)]
        im = {k: im_ref[k, here, :] for k in range(1, blocks)}
        for parity in (0, 1):
            sign = 1.0 - 2.0 * parity
            base = re[0] + sign * re[blocks]
            re_sum = {k: re[k] + sign * re[blocks - k] for k in range(1, blocks // 2)}
            im_sum = {k: im[k] - sign * im[blocks - k] for k in range(1, blocks // 2)}
            re_sum[blocks // 2] = re[blocks // 2]
            im_sum[blocks // 2] = im[blocks // 2]
            for a in range(parity, blocks, 2):
                terms = [base]
                for k in range(1, blocks // 2 + 1):
                    turn = math.pi * ((a * k) % (2 * blocks)) / blocks
                    terms.append(scaled(re_sum[k], math.cos(turn)))
                    terms.append(scaled(im_sum[k], -math.sin(turn)))
                value = total(terms)
                out_ref[sending_place(a ^ own, blocks, by_side), here, :] = value
                if start == 0 and a > 0:
                    place = sending_place((a - 1) ^ own, blocks, by_side)
                    out_ref[place, rows : rows + PAD_ROWS, :] = value[:PAD_ROWS]
    place = sending_place((blocks - 1) ^ own, blocks, by_side)
    out_ref[place, rows : rows + PAD_ROWS, :] = jnp.zeros((PAD_ROWS, out_ref.shape[2]), F32)


def product_kernel(
    conjugate, by_side, own_ref, x_ref, spec_ref, high_ref, low_ref, tw_ref, out_ref, split_ref, re_ref, im_ref
):
    blocks, rows = x_ref.shape[0], x_ref.shape[1]
    first_stage(own_ref[0], x_ref, tw_ref, split_ref, 32)
    sign = -1.0 if conjugate else 1.0
    tile = 32
    for k in range(blocks + 1):
        cos_re, cos_im, sin_re, sin_im = second_stage(high_ref[...], low_ref[...], split_ref[k])
        re_ref[k] = cos_re + sin_im
        im_ref[k] = cos_im - sin_re
    for k in range(blocks + 1):
        for start in range(0, rows, tile):
            here = slice(start, start + tile)
            x_re, x_im = re_ref[k, here, :], im_ref[k, here, :]
            h_re, h_im = spec_ref[k, here, :], spec_ref[k, rows + start : rows + start + tile, :] * sign
            store_split(split_ref, k, here, x_re * h_re - x_im * h_im, x_im * h_re + x_re * h_im)
    for k in range(blocks + 1):
        cos_re, cos_im, sin_re, sin_im = second_stage(high_ref[...], low_ref[...], split_ref[k])
        re, im = turned(tw_ref[...], k, cos_re - sin_im, cos_im + sin_re, 1.0)
        re_ref[k] = re
        im_ref[k] = im
    last_stage(own_ref[0], by_side, re_ref, im_ref, out_ref, tile)


def whole_operands(count):
    return [pl.BlockSpec(memory_space=pltpu.SMEM)] + [pl.BlockSpec(memory_space=pltpu.VMEM)] * count


def split_scratch(blocks, rows, width):
    return pltpu.VMEM((blocks + 1, 2 * rows, 2 * width), BF16)


def spectrum(own, x, tables, unread):
    blocks, rows, width = x.shape
    return pl.pallas_call(
        spectrum_kernel,
        out_shape=jax.ShapeDtypeStruct((blocks + 1, 2 * rows, width), F32),
        in_specs=whole_operands(4) + [pl.BlockSpec(memory_space=pl.ANY)],
        scratch_shapes=[split_scratch(blocks, rows, width)],
        compiler_params=params(),
        cost_estimate=measured(1.1),
        name="filter_spectrum",
    )(own, x, *tables, unread)


def through_filter(own, x, spec, tables, conjugate, by_side):
    blocks, rows, width = x.shape
    part = pltpu.VMEM((blocks + 1, rows, width), F32)
    return pl.pallas_call(
        functools.partial(product_kernel, conjugate, by_side),
        out_shape=jax.ShapeDtypeStruct((blocks, rows + PAD_ROWS, width), F32),
        in_specs=whole_operands(5),
        scratch_shapes=[split_scratch(blocks, rows, width), part, part],
        compiler_params=params(),
        cost_estimate=measured(2.5),
        name="correlation" if conjugate else "convolution",
    )(own, x, spec, *tables)


def row_number(shape):
    return lax.broadcasted_iota(jnp.int32, shape, 0)


def delayed(x, before, distance):
    moved = pltpu.roll(x, distance, 0)
    rows = row_number(x.shape)
    rim = len(before)
    for row in range(distance):
        moved = jnp.where(rows == row, before[rim - distance + row], moved)
    return moved


def advanced(x, after, distance):
    count = x.shape[0]
    moved = pltpu.roll(x, count - distance, 0)
    rows = row_number(x.shape)
    for row in range(distance):
        moved = jnp.where(rows == count - distance + row, after[row], moved)
    return moved


def rows_of(block):
    return [block[row : row + 1] for row in range(block.shape[0])]


def short_filter_after(after, last, taps):
    known = last + after
    return [
        total([taps[j : j + 1] * known[len(last) + row - j] for j in range(taps.shape[0])])
        for row in range(len(after))
    ]


def short_filter(x, before, taps):
    result = taps[0:1] * x
    for j in range(1, taps.shape[0]):
        result = result + taps[j : j + 1] * delayed(x, before, j)
    return result


def short_transpose(x, after, taps):
    result = taps[0:1] * x
    for j in range(1, taps.shape[0]):
        result = result + taps[j : j + 1] * advanced(x, after, j)
    return result


def place_of_part(own_ref, part):
    return part ^ (own_ref[0] % 2)


def pair_specs(rows, pair, rim, count):
    def at(j, own):
        return j ^ (own[0] // 2)

    return {
        "streams": pl.BlockSpec((3, rows, pair), lambda j, own: (0, 0, at(j, own))),
        "before": pl.BlockSpec((3, rim, pair), lambda j, own: (0, 0, at(j, own))),
        "after": pl.BlockSpec((4, rim, pair), lambda j, own: (0, 0, at(j, own))),
        "taps": pl.BlockSpec((3, count, pair), lambda j, own: (0, 0, at(j, own))),
        "vector": pl.BlockSpec((1, pair), lambda j, own: (0, at(j, own))),
        "flat": pl.BlockSpec((rows, pair), lambda j, own: (0, at(j, own))),
        "row": pl.BlockSpec((1, rows), lambda j, own: (0, 0)),
        "chunk": pl.BlockSpec((1, 2, rows + PAD_ROWS, pair // 2), lambda j, own: (j, 0, 0, 0)),
        "by_pair": pl.BlockSpec((1, 2, rows, pair // 2), lambda j, own: (j, 0, 0, 0)),
        "by_side": pl.BlockSpec((2, 1, rows, pair // 2), lambda j, own: (0, j, 0, 0)),
    }


def over_pairs(kernel, own, parts, specs, ins, outs, out_shape, operands, name, microseconds):
    return pl.pallas_call(
        kernel,
        grid_spec=pltpu.PrefetchScalarGridSpec(
            num_scalar_prefetch=1,
            grid=(parts // 2,),
            in_specs=[specs[i] for i in ins],
            out_specs=[specs[o] for o in outs],
        ),
        out_shape=out_shape,
        compiler_params=params(),
        cost_estimate=measured(microseconds),
        name=name,
    )(own, *operands)


def lanes_of(part, block):
    return slice(part * block, (part + 1) * block)


def arrange_kernel(own_ref, x_ref, out_ref):
    block = out_ref.shape[3]
    for part in range(2):
        out_ref[0, place_of_part(own_ref, part)] = x_ref[:, lanes_of(part, block)]


def arrange(own, x, parts, specs):
    rows, width = x.shape
    out = jax.ShapeDtypeStruct((parts // 2, 2, rows, width // parts), F32)
    return over_pairs(arrange_kernel, own, parts, specs, ["flat"], ["by_pair"], [out], [x], "filter_blocks", 0.3)[0]


def shorts_of(streams_ref, before_ref, taps_ref, lanes):
    return [
        short_filter(streams_ref[i, :, lanes].astype(F32), rows_of(before_ref[i, :, lanes]), taps_ref[i, :, lanes])
        for i in range(3)
    ]


def gate_kernel(own_ref, streams_ref, before_ref, taps_ref, cot_ref, gated_ref, carried_ref):
    block = gated_ref.shape[3]
    for part in range(2):
        lanes = lanes_of(part, block)
        place = place_of_part(own_ref, part)
        short = shorts_of(streams_ref, before_ref, taps_ref, lanes)
        gated_ref[place, 0] = short[1] * short[2]
        carried_ref[place, 0] = cot_ref[:, lanes].astype(F32) * short[0]


def gate(own, streams, before, taps, cotangent, parts, specs):
    _, rows, width = streams.shape
    block = width // parts
    return over_pairs(
        gate_kernel,
        own,
        parts,
        specs,
        ["streams", "before", "taps", "flat"],
        ["by_side", "by_side"],
        [
            jax.ShapeDtypeStruct((2, parts // 2, rows, block), F32),
            jax.ShapeDtypeStruct((2, parts // 2, rows, block), F32),
        ],
        [streams, before, taps, cotangent],
        "short_filters",
        1.2,
    )


def mix_kernel(
    own_ref, streams_ref, before_ref, after_ref, taps_ref, bias_ref, cot_ref, conv_ref, mixed_ref, square_ref, grad_ref
):
    step = pl.program_id(0)
    block = conv_ref.shape[3]
    rows = streams_ref.shape[1]
    rim = after_ref.shape[1]
    squares = jnp.zeros((rows, block), F32)
    for part in range(2):
        lanes = lanes_of(part, block)
        place = place_of_part(own_ref, part)
        bias = bias_ref[:, lanes]
        short = shorts_of(streams_ref, before_ref, taps_ref, lanes)
        direct = conv_ref[0, place, :rows, :] + bias * (short[1] * short[2])
        mixed = short[0] * direct
        mixed_ref[:, lanes] = mixed
        squares = squares + mixed * mixed
        gated_after = [
            short_filter_after(
                rows_of(after_ref[i, :, lanes]),
                rows_of(streams_ref[i, rows - rim :, lanes].astype(F32)),
                taps_ref[i, :, lanes],
            )
            for i in (1, 2)
        ]
        conv_after = rows_of(conv_ref[0, place, rows : rows + rim, :])
        cot_after = rows_of(after_ref[3, :, lanes])
        above = [
            cot_after[row] * (conv_after[row] + bias * (gated_after[0][row] * gated_after[1][row]))
            for row in range(rim)
        ]
        grad = short_transpose(cot_ref[:, lanes].astype(F32) * direct, above, taps_ref[0, :, lanes])
        grad_ref[:, lanes] = grad.astype(BF16)
    row_sums = lax.dot_general(
        jnp.ones((8, block), F32),
        squares,
        (((1,), (1,)), ((), ())),
        precision=lax.Precision.HIGHEST,
        preferred_element_type=F32,
    )[0:1]

    @pl.when(step == 0)
    def _():
        square_ref[...] = row_sums

    @pl.when(step > 0)
    def _():
        square_ref[...] += row_sums


def mix(own, streams, before, after, taps, bias, cotangent, conv, specs):
    _, rows, width = streams.shape
    return over_pairs(
        mix_kernel,
        own,
        2 * conv.shape[0],
        specs,
        ["streams", "before", "after", "taps", "vector", "flat", "chunk"],
        ["flat", "row", "flat"],
        [
            jax.ShapeDtypeStruct((rows, width), F32),
            jax.ShapeDtypeStruct((1, rows), F32),
            jax.ShapeDtypeStruct((rows, width), BF16),
        ],
        [streams, before, after, taps, bias, cotangent, conv],
        "mixed_squares",
        2.4,
    )


def norm_kernel(channels, mixed_ref, square_ref, gain_ref, normed_ref):
    rows, width = mixed_ref.shape
    squares = jnp.broadcast_to(square_ref[...], (128, rows)).T
    scaling = lax.rsqrt(squares / channels + 1e-06)
    for start in range(0, width, 128):
        lanes = slice(start, start + 128)
        normed_ref[:, lanes] = (mixed_ref[:, lanes] * scaling * gain_ref[:, lanes]).astype(BF16)


def norm(channels, mixed, squares, gain):
    rows, width = mixed.shape
    return pl.pallas_call(
        functools.partial(norm_kernel, float(channels)),
        out_shape=jax.ShapeDtypeStruct((rows, width), BF16),
        compiler_params=params(),
        cost_estimate=measured(0.9),
        name="norm",
    )(mixed, squares, gain)


def finish_kernel(
    own_ref, streams_ref, before_ref, after_ref, taps_ref, bias_ref, cot_ref, grad_ref, corr_ref, grads_ref
):
    block = corr_ref.shape[3]
    rows = streams_ref.shape[1]
    rim = after_ref.shape[1]
    grads_ref[0] = grad_ref[...]
    for part in range(2):
        lanes = lanes_of(part, block)
        place = place_of_part(own_ref, part)
        bias = bias_ref[:, lanes]
        taps = [taps_ref[i, :, lanes] for i in range(3)]
        short = shorts_of(streams_ref, before_ref, taps_ref, lanes)
        gated_grad = corr_ref[0, place, :rows, :] + bias * (cot_ref[:, lanes].astype(F32) * short[0])
        short_after = [
            short_filter_after(
                rows_of(after_ref[i, :, lanes]), rows_of(streams_ref[i, rows - rim :, lanes].astype(F32)), taps[i]
            )
            for i in range(3)
        ]
        corr_after = rows_of(corr_ref[0, place, rows : rows + rim, :])
        cot_after = rows_of(after_ref[3, :, lanes])
        grad_after = [corr_after[row] + bias * (cot_after[row] * short_after[0][row]) for row in range(rim)]
        for i, other in ((1, 2), (2, 1)):
            above = [grad_after[row] * short_after[other][row] for row in range(rim)]
            grads_ref[i, :, lanes] = short_transpose(gated_grad * short[other], above, taps[i]).astype(BF16)


def finish(own, streams, before, after, taps, bias, cotangent, grad, corr, specs):
    return over_pairs(
        finish_kernel,
        own,
        2 * corr.shape[0],
        specs,
        ["streams", "before", "after", "taps", "vector", "flat", "flat", "chunk"],
        ["streams"],
        [jax.ShapeDtypeStruct(streams.shape, BF16)],
        [streams, before, after, taps, bias, cotangent, grad, corr],
        "stream_grads",
        2.6,
    )[0]


def swapped(block, apart, name):
    route = [(i, i ^ apart) for i in range(lax.axis_size("seq"))]
    with jax.named_scope(f"{name}_over_{apart}"):
        return lax.ppermute(block, "seq", route)


def tied(value, other):
    return lax.optimization_barrier((value, other))


def within_pairs(name, block):
    return swapped(block, 1, name)


def between_pairs(name, blocks):
    return [blocks[0]] + [swapped(blocks[j], 2 * j, name) for j in range(1, len(blocks))]


def sides_of(got):
    return jnp.stack([block[0] for block in got]), jnp.stack([block[1] for block in got])


def joined(kept, other):
    return jnp.stack([kept, other], axis=1)


def as_line(blocks):
    return blocks.reshape((-1,) + blocks.shape[2:])


def local(streams, short_taps, long_filter, skip_bias, norm_gain, cotangent):
    parts = lax.axis_size("seq")
    rows, width = cotangent.shape
    rim = short_taps.shape[1] - 1
    tables = stage_tables(parts, rows)
    specs = pair_specs(rows, 2 * width // parts, rim, short_taps.shape[1])
    own = lax.axis_index("seq").astype(jnp.int32)[None]
    bias, gain = skip_bias[None], norm_gain[None]

    filter_sent = arrange(own, long_filter, parts, specs)
    filter_got = between_pairs("filter", filter_sent)
    streams_later, filter_got[0] = tied(streams, filter_got[0])
    before = shift_along(streams_later[:, rows - rim :].astype(F32), "seq", 1)
    gated, carried = gate(own, streams, before, short_taps, cotangent, parts, specs)
    edges = jnp.concatenate([streams_later[:, :rim].astype(F32), cotangent[None, :rim].astype(F32)], axis=0)
    edges, filter_got[1] = tied(edges, filter_got[1])
    after = shift_along(edges, "seq", -1)

    gated_other = within_pairs("gated", gated[1])
    carried_gone = carried[1]
    gated_got = between_pairs("gated", joined(gated[0], gated_other))
    filter_kept, filter_gone = sides_of(filter_got)
    filter_other = within_pairs("filter", filter_gone)
    filter_blocks = joined(filter_kept, filter_other)
    carried_pairs = joined(carried[0], within_pairs("carried", carried_gone))
    spec = spectrum(own, as_line(filter_blocks), tables, after)
    carried_pairs, spec = tied(carried_pairs, spec)
    carried_got = between_pairs("carried", carried_pairs)

    shape = (rows + PAD_ROWS, width // parts)
    gated_blocks = as_line(jnp.stack(gated_got))
    conv_sent = through_filter(own, gated_blocks, spec, tables, False, True).reshape((2, parts // 2) + shape)
    conv_pairs = joined(conv_sent[0], within_pairs("conv", conv_sent[1]))
    carried_blocks = jnp.stack(carried_got)
    conv_got = between_pairs("conv", conv_pairs)
    corr_sent = through_filter(own, as_line(carried_blocks), spec, tables, True, True).reshape((2, parts // 2) + shape)
    corr_pairs = joined(corr_sent[0], within_pairs("corr", corr_sent[1]))
    corr_pairs, conv_got[2] = tied(corr_pairs, conv_got[2])
    corr_got = between_pairs("corr", corr_pairs)
    conv = jnp.stack(conv_got)
    corr = jnp.stack(corr_got)
    mixed, squares, grad = mix(own, streams, before, after, short_taps, bias, cotangent, conv, specs)
    squares = lax.psum(squares, "ch")
    normed = norm(width * lax.axis_size("ch"), mixed, squares, gain)
    grads = finish(own, streams, before, after, short_taps, bias, cotangent, grad, corr, specs)
    return normed, grads


EXACTNESS = lax.Precision.HIGHEST


def passed_along(block, axis, distance):
    devices = range(lax.axis_size(axis))
    route = [(i - distance, i) for i in devices if i - distance in devices]
    return lax.ppermute(block, axis, route)


def counting(amount):
    return jnp.arange(amount, dtype=jnp.int32)


def angle_pair(left_index, right_index, period, turning):
    product = left_index[:, None] * right_index[None, :] % period
    angles = product.astype(jnp.float32) * (turning * 2.0 * math.pi / period)
    return (jnp.cos(angles), jnp.sin(angles))


def neighbour_rows(edge_rows, offset):
    return passed_along(edge_rows, "seq", offset)


def swap_middle(blocks):
    return lax.all_to_all(blocks, "seq", split_axis=1, concat_axis=0, tiled=True)


def spread_forward(series):
    length, series_count, chan_width = series.shape
    devices = lax.axis_size("seq")
    position = lax.axis_index("seq")
    sub_rows = length // devices
    period = 2 * length * devices
    gathered = swap_middle(series.reshape(1, length, series_count, chan_width))
    cos_a, sin_a = angle_pair(counting(2 * devices), counting(devices), 2 * devices, -1.0)
    real_part = jnp.einsum("ka,absc->bksc", cos_a, gathered, precision=EXACTNESS)
    imag_part = jnp.einsum("ka,absc->bksc", sin_a, gathered, precision=EXACTNESS)
    spike_locations = position * sub_rows + counting(sub_rows)
    turn_cos, turn_sin = angle_pair(spike_locations, counting(2 * devices), period, -1.0)
    turn_cos = turn_cos[:, :, None, None]
    turn_sin = turn_sin[:, :, None, None]
    turned = jnp.concatenate(
        [real_part * turn_cos - imag_part * turn_sin, real_part * turn_sin + imag_part * turn_cos],
        axis=2,
    )
    swapped = swap_middle(turned)
    cos_b, sin_b = angle_pair(counting(length), counting(length), length, -1.0)
    primary = jnp.einsum("jb,bksc->jksc", cos_b, swapped, precision=EXACTNESS)
    second = jnp.einsum("jb,bksc->jksc", sin_b, swapped, precision=EXACTNESS)
    return (
        primary[:, :, :series_count] - second[:, :, series_count:],
        primary[:, :, series_count:] + second[:, :, :series_count],
    )


def spread_inverse(spec_re, spec_im):
    length, pair_rows, series_count, chan_width = spec_re.shape
    devices = lax.axis_size("seq")
    position = lax.axis_index("seq")
    sub_rows = length // devices
    period = 2 * length * devices
    cos_b, sin_b = angle_pair(counting(length), counting(length), length, 1.0)
    merged = jnp.concatenate([spec_re, spec_im], axis=2)
    primary = jnp.einsum("bj,jksc->kbsc", cos_b, merged, precision=EXACTNESS)
    second = jnp.einsum("bj,jksc->kbsc", sin_b, merged, precision=EXACTNESS)
    turned = jnp.concatenate(
        [
            primary[:, :, :series_count] - second[:, :, series_count:],
            primary[:, :, series_count:] + second[:, :, :series_count],
        ],
        axis=2,
    )
    swapped = swap_middle(turned)
    spike_locations = position * sub_rows + counting(sub_rows)
    turn_cos, turn_sin = angle_pair(counting(2 * devices), spike_locations, period, 1.0)
    turn_cos = turn_cos[:, :, None, None]
    turn_sin = turn_sin[:, :, None, None]
    real_part = swapped[:, :, :series_count]
    imag_part = swapped[:, :, series_count:]
    rotated_re = real_part * turn_cos - imag_part * turn_sin
    rotated_im = real_part * turn_sin + imag_part * turn_cos
    cos_a, sin_a = angle_pair(counting(devices), counting(2 * devices), 2 * devices, 1.0)
    result = jnp.einsum("ak,kbsc->basc", cos_a, rotated_re, precision=EXACTNESS) - jnp.einsum(
        "ak,kbsc->basc", sin_a, rotated_im, precision=EXACTNESS
    )
    returned = swap_middle(result / period)
    return returned.reshape(length, -1, chan_width)


def local_general(streams, short_taps, long_filter, skip_bias, norm_gain, cotangent):
    row_count = streams.shape[1]
    chan_width = streams.shape[2]
    rim_rows = short_taps.shape[1] - 1
    widened = streams.astype(jnp.float32)
    before = neighbour_rows(widened[:, row_count - rim_rows :, :], 1)
    extended = jnp.concatenate([before, widened], axis=1)
    shorts = jnp.zeros_like(widened)
    for offset in range(short_taps.shape[1]):
        shorts = (
            shorts
            + short_taps[:, offset, None, :]
            * extended[:, rim_rows - offset : rim_rows - offset + row_count, :]
        )
    short_q, short_k, short_v = (shorts[0], shorts[1], shorts[2])
    gated_input = short_k * short_v
    cot_wide = cotangent.astype(jnp.float32)
    carried = cot_wide * short_q
    series = jnp.stack([gated_input, long_filter, carried], axis=1)
    spec_re, spec_im = spread_forward(series)
    series_axis = 2
    gated_re = lax.index_in_dim(spec_re, 0, series_axis, keepdims=False)
    gated_im = lax.index_in_dim(spec_im, 0, series_axis, keepdims=False)
    filter_re = lax.index_in_dim(spec_re, 1, series_axis, keepdims=False)
    filter_im = lax.index_in_dim(spec_im, 1, series_axis, keepdims=False)
    carry_re = lax.index_in_dim(spec_re, 2, series_axis, keepdims=False)
    carry_im = lax.index_in_dim(spec_im, 2, series_axis, keepdims=False)
    output_re = filter_re * gated_re - filter_im * gated_im
    output_im = filter_re * gated_im + filter_im * gated_re
    backward_re = filter_re * carry_re + filter_im * carry_im
    backward_im = filter_re * carry_im - filter_im * carry_re
    inverse_re = jnp.stack([output_re, backward_re], axis=series_axis)
    inverse_im = jnp.stack([output_im, backward_im], axis=series_axis)
    result = spread_inverse(inverse_re, inverse_im)
    convolved = result[:, 0]
    correlated = result[:, 1]
    direct = convolved + skip_bias * gated_input
    mixed_out = short_q * direct
    square_sum = lax.psum(jnp.sum(mixed_out * mixed_out, axis=1), "ch")
    scaling = lax.rsqrt(square_sum[:, None] / (chan_width * lax.axis_size("ch")) + 1e-06)
    normed = (mixed_out * scaling * norm_gain).astype(jnp.bfloat16)
    gated_grad = correlated + skip_bias * carried
    short_grad = jnp.stack([cot_wide * direct, gated_grad * short_v, gated_grad * short_k])
    following = neighbour_rows(short_grad[:, :rim_rows, :], -1)
    grad_ext = jnp.concatenate([short_grad, following], axis=1)
    grads = jnp.zeros_like(short_grad)
    for offset in range(short_taps.shape[1]):
        grads = grads + short_taps[:, offset, None, :] * grad_ext[:, offset : offset + row_count, :]
    return (normed, grads.astype(jnp.bfloat16))


def solution(mesh):
    placed = (
        P(None, "seq", "ch"),
        P(None, None, "ch"),
        P("seq", "ch"),
        P("ch"),
        P("ch"),
        P("seq", "ch"),
    )

    def program(streams, short_taps, long_filter, skip_bias, norm_gain, cotangent):
        parts = mesh.shape["seq"]
        width = cotangent.shape[1] // mesh.shape["ch"]
        lanes_filled = width % (128 * parts) == 0 and parts in (4, 8, 16)
        return jax.shard_map(
            local if lanes_filled else local_general,
            mesh=mesh,
            in_specs=placed,
            out_specs=(P("seq", "ch"), P(None, "seq", "ch")),
            check_vma=False,
        )(streams, short_taps, long_filter, skip_bias, norm_gain, cotangent)

    return program
```

```python
import functools
import math

import jax
import jax.numpy as jnp
import numpy as np
from jax import lax
from jax.experimental import pallas as pl
from jax.experimental.pallas import tpu as pltpu
from jax.sharding import PartitionSpec as P

F32 = jnp.float32
BF16 = jnp.bfloat16
PAD_ROWS = 8
VMEM_BYTES = 24 * 1024 * 1024


def shift_along(block, axis, distance):
    devices = range(lax.axis_size(axis))
    route = [(i - distance, i) for i in devices if i - distance in devices]
    return lax.ppermute(block, axis, route)


def measured(microseconds):
    return pl.CostEstimate(flops=0, bytes_accessed=int(microseconds * 3.69e6), transcendentals=0)


def params():
    return pltpu.CompilerParams(vmem_limit_bytes=VMEM_BYTES)


def scaled(value, factor):
    if abs(factor) < 1e-12:
        return None
    if abs(factor - 1.0) < 1e-12:
        return value
    if abs(factor + 1.0) < 1e-12:
        return -value
    return value * factor


def total(terms):
    kept = [term for term in terms if term is not None]
    if not kept:
        return None
    result = kept[0]
    for term in kept[1:]:
        result = result + term
    return result


def plus(left, right):
    return total([left, right])


def minus(left, right):
    return total([left, None if right is None else -right])


def sending_place(apart, blocks, by_side):
    return (apart % 2) * (blocks // 2) + apart // 2 if by_side else apart


def dot(left, right):
    return lax.dot_general(left, right, (((1,), (0,)), ((), ())), preferred_element_type=F32)


def stage_tables(blocks, rows):
    period = 2 * blocks * rows
    place = np.arange(rows)
    turn = 2.0 * np.pi * ((place[:, None] * place[None, :]) % rows) / rows
    exact = np.concatenate([np.cos(turn), np.sin(turn)], axis=0)
    high = exact.astype(BF16)
    low = (exact - high.astype(np.float64)).astype(BF16)
    columns = -(-2 * (blocks + 1) // 128) * 128
    twiddles = np.zeros((rows, columns), np.float32)
    for k in range(blocks + 1):
        turn = 2.0 * np.pi * ((place * k) % period) / period
        twiddles[:, 2 * k], twiddles[:, 2 * k + 1] = np.cos(turn), np.sin(turn)
    return np.concatenate([high, high], axis=1), low, twiddles


def turned(twiddles, k, re, im, sign):
    if k == 0:
        return re, im
    cos = jnp.broadcast_to(twiddles[:, 2 * k : 2 * k + 1], re.shape)
    sin = jnp.broadcast_to(twiddles[:, 2 * k + 1 : 2 * k + 2], re.shape) * sign
    if im is None:
        return re * cos, re * sin
    return re * cos - im * sin, re * sin + im * cos


def store_split(split_ref, k, here, re, im):
    rows, width = split_ref.shape[1] // 2, split_ref.shape[2] // 2
    for value, lanes in ((re, slice(0, width)), (im, slice(width, 2 * width))):
        if value is None:
            value = jnp.zeros_like(re)
        high = value.astype(BF16)
        split_ref[k, here, lanes] = high
        split_ref[k, slice(rows + here.start, rows + here.stop), lanes] = (value - high.astype(F32)).astype(BF16)


def first_stage(own, x_ref, tw_ref, split_ref, tile):
    blocks, rows = x_ref.shape[0], x_ref.shape[1]
    for start in range(0, rows, tile):
        here = slice(start, start + tile)
        twiddles = tw_ref[here, :]
        x = [x_ref[a ^ own, here, :] for a in range(blocks)]

        def keep(k, re, im):
            store_split(split_ref, k, here, *turned(twiddles, k, re, im, -1.0))

        for k in range(blocks // 2 + 1):
            parts = []
            for parity in (0, 1):
                members = range(parity, blocks, 2)
                turn = [math.pi * ((a * k) % (2 * blocks)) / blocks for a in members]
                parts.append(total([scaled(x[a], math.cos(t)) for a, t in zip(members, turn)]))
                parts.append(total([scaled(x[a], math.sin(t)) for a, t in zip(members, turn)]))
            even_c, even_s, odd_c, odd_s = parts
            keep(k, plus(even_c, odd_c), None if k == 0 else -plus(even_s, odd_s))
            if 2 * k != blocks:
                keep(blocks - k, minus(even_c, odd_c), None if k == 0 else minus(even_s, odd_s))


def second_stage(table_high, table_low, split):
    rows, width = table_low.shape[1], split.shape[1] // 2
    sums = dot(table_high, split) + dot(table_low, split[:rows])
    return sums[:rows, :width], sums[:rows, width:], sums[rows:, :width], sums[rows:, width:]


def spectrum_kernel(own_ref, x_ref, high_ref, low_ref, tw_ref, spec_ref, split_ref):
    blocks, rows = x_ref.shape[0], x_ref.shape[1]
    first_stage(own_ref[0], x_ref, tw_ref, split_ref, 32)
    for k in range(blocks + 1):
        scale = (0.5 if k in (0, blocks) else 1.0) / (blocks * rows)
        cos_re, cos_im, sin_re, sin_im = second_stage(high_ref[...], low_ref[...], split_ref[k])
        spec_ref[k, :rows, :] = (cos_re + sin_im) * scale
        spec_ref[k, rows:, :] = (cos_im - sin_re) * scale


def last_stage(own, by_side, re_ref, im_ref, out_ref, tile):
    blocks, rows = re_ref.shape[0] - 1, re_ref.shape[1]
    for start in range(0, rows, tile):
        here = slice(start, start + tile)
        re = [re_ref[k, here, :] for k in range(blocks + 1)]
        im = {k: im_ref[k, here, :] for k in range(1, blocks)}
        for parity in (0, 1):
            sign = 1.0 - 2.0 * parity
            base = re[0] + sign * re[blocks]
            re_sum = {k: re[k] + sign * re[blocks - k] for k in range(1, blocks // 2)}
            im_sum = {k: im[k] - sign * im[blocks - k] for k in range(1, blocks // 2)}
            re_sum[blocks // 2] = re[blocks // 2]
            im_sum[blocks // 2] = im[blocks // 2]
            for a in range(parity, blocks, 2):
                terms = [base]
                for k in range(1, blocks // 2 + 1):
                    turn = math.pi * ((a * k) % (2 * blocks)) / blocks
                    terms.append(scaled(re_sum[k], math.cos(turn)))
                    terms.append(scaled(im_sum[k], -math.sin(turn)))
                value = total(terms)
                out_ref[sending_place(a ^ own, blocks, by_side), here, :] = value
                if start == 0 and a > 0:
                    place = sending_place((a - 1) ^ own, blocks, by_side)
                    out_ref[place, rows : rows + PAD_ROWS, :] = value[:PAD_ROWS]
    place = sending_place((blocks - 1) ^ own, blocks, by_side)
    out_ref[place, rows : rows + PAD_ROWS, :] = jnp.zeros((PAD_ROWS, out_ref.shape[2]), F32)


def product_kernel(
    conjugate, by_side, own_ref, x_ref, spec_ref, high_ref, low_ref, tw_ref, out_ref, split_ref, re_ref, im_ref
):
    blocks, rows = x_ref.shape[0], x_ref.shape[1]
    first_stage(own_ref[0], x_ref, tw_ref, split_ref, 32)
    sign = -1.0 if conjugate else 1.0
    tile = 32
    for k in range(blocks + 1):
        cos_re, cos_im, sin_re, sin_im = second_stage(high_ref[...], low_ref[...], split_ref[k])
        re_ref[k] = cos_re + sin_im
        im_ref[k] = cos_im - sin_re
    for k in range(blocks + 1):
        for start in range(0, rows, tile):
            here = slice(start, start + tile)
            x_re, x_im = re_ref[k, here, :], im_ref[k, here, :]
            h_re, h_im = spec_ref[k, here, :], spec_ref[k, rows + start : rows + start + tile, :] * sign
            store_split(split_ref, k, here, x_re * h_re - x_im * h_im, x_im * h_re + x_re * h_im)
    for k in range(blocks + 1):
        cos_re, cos_im, sin_re, sin_im = second_stage(high_ref[...], low_ref[...], split_ref[k])
        re, im = turned(tw_ref[...], k, cos_re - sin_im, cos_im + sin_re, 1.0)
        re_ref[k] = re
        im_ref[k] = im
    last_stage(own_ref[0], by_side, re_ref, im_ref, out_ref, tile)


def whole_operands(count):
    return [pl.BlockSpec(memory_space=pltpu.SMEM)] + [pl.BlockSpec(memory_space=pltpu.VMEM)] * count


def split_scratch(blocks, rows, width):
    return pltpu.VMEM((blocks + 1, 2 * rows, 2 * width), BF16)


def spectrum(own, x, tables):
    blocks, rows, width = x.shape
    return pl.pallas_call(
        spectrum_kernel,
        out_shape=jax.ShapeDtypeStruct((blocks + 1, 2 * rows, width), F32),
        in_specs=whole_operands(4),
        scratch_shapes=[split_scratch(blocks, rows, width)],
        compiler_params=params(),
        cost_estimate=measured(1.1),
        name="filter_spectrum",
    )(own, x, *tables)


def through_filter(own, x, spec, tables, conjugate, by_side):
    blocks, rows, width = x.shape
    part = pltpu.VMEM((blocks + 1, rows, width), F32)
    return pl.pallas_call(
        functools.partial(product_kernel, conjugate, by_side),
        out_shape=jax.ShapeDtypeStruct((blocks, rows + PAD_ROWS, width), F32),
        in_specs=whole_operands(5),
        scratch_shapes=[split_scratch(blocks, rows, width), part, part],
        compiler_params=params(),
        cost_estimate=measured(0.05 if conjugate else 20),
        name="correlation" if conjugate else "convolution",
    )(own, x, spec, *tables)


def row_number(shape):
    return lax.broadcasted_iota(jnp.int32, shape, 0)


def delayed(x, before, distance):
    moved = pltpu.roll(x, distance, 0)
    rows = row_number(x.shape)
    rim = len(before)
    for row in range(distance):
        moved = jnp.where(rows == row, before[rim - distance + row], moved)
    return moved


def rows_of(block):
    return [block[row : row + 1] for row in range(block.shape[0])]


def short_filter_after(after, last, taps):
    known = last + after
    return [
        total([taps[j : j + 1] * known[len(last) + row - j] for j in range(taps.shape[0])])
        for row in range(len(after))
    ]


def short_filter(x, before, taps):
    result = taps[0:1] * x
    for j in range(1, taps.shape[0]):
        result = result + taps[j : j + 1] * delayed(x, before, j)
    return result


def place_of_part(own_ref, part):
    return part ^ (own_ref[0] % 2)


def pair_specs(rows, pair, rim, count):
    def at(j, own):
        return j ^ (own[0] // 2)

    return {
        "streams": pl.BlockSpec((3, rows, pair), lambda j, own: (0, 0, at(j, own))),
        "before": pl.BlockSpec((3, rim, pair), lambda j, own: (0, 0, at(j, own))),
        "after": pl.BlockSpec((4, rim, pair), lambda j, own: (0, 0, at(j, own))),
        "taps": pl.BlockSpec((3, count, pair), lambda j, own: (0, 0, at(j, own))),
        "vector": pl.BlockSpec((1, pair), lambda j, own: (0, at(j, own))),
        "flat": pl.BlockSpec((rows, pair), lambda j, own: (0, at(j, own))),
        "long": pl.BlockSpec((rows + PAD_ROWS, pair), lambda j, own: (0, at(j, own))),
        "by_pair": pl.BlockSpec((1, 2, rows, pair // 2), lambda j, own: (j, 0, 0, 0)),
        "by_side": pl.BlockSpec((2, 1, rows, pair // 2), lambda j, own: (0, j, 0, 0)),
    }


def over_pairs(kernel, own, parts, specs, ins, outs, out_shape, operands, name, microseconds):
    return pl.pallas_call(
        kernel,
        grid_spec=pltpu.PrefetchScalarGridSpec(
            num_scalar_prefetch=1,
            grid=(parts // 2,),
            in_specs=[specs[i] for i in ins],
            out_specs=[specs[o] for o in outs],
        ),
        out_shape=out_shape,
        compiler_params=params(),
        cost_estimate=measured(0.02 * microseconds),
        name=name,
    )(own, *operands)


def lanes_of(part, block):
    return slice(part * block, (part + 1) * block)


def arrange_kernel(own_ref, x_ref, out_ref):
    block = out_ref.shape[3]
    for part in range(2):
        out_ref[0, place_of_part(own_ref, part)] = x_ref[:, lanes_of(part, block)]


def arrange(own, x, parts, specs):
    rows, width = x.shape
    out = jax.ShapeDtypeStruct((parts // 2, 2, rows, width // parts), F32)
    return over_pairs(arrange_kernel, own, parts, specs, ["flat"], ["by_pair"], [out], [x], "filter_blocks", 0.3)[0]


def shorts_of(streams_ref, before_ref, taps_ref, lanes):
    return [
        short_filter(streams_ref[i, :, lanes].astype(F32), rows_of(before_ref[i, :, lanes]), taps_ref[i, :, lanes])
        for i in range(3)
    ]


def gate_kernel(own_ref, streams_ref, before_ref, taps_ref, cot_ref, gated_ref, carried_ref):
    block = gated_ref.shape[3]
    for part in range(2):
        lanes = lanes_of(part, block)
        place = place_of_part(own_ref, part)
        short = shorts_of(streams_ref, before_ref, taps_ref, lanes)
        gated_ref[place, 0] = short[1] * short[2]
        carried_ref[place, 0] = cot_ref[:, lanes].astype(F32) * short[0]


def gate(own, streams, before, taps, cotangent, parts, specs):
    _, rows, width = streams.shape
    block = width // parts
    return over_pairs(
        gate_kernel,
        own,
        parts,
        specs,
        ["streams", "before", "taps", "flat"],
        ["by_side", "by_side"],
        [
            jax.ShapeDtypeStruct((2, parts // 2, rows, block), F32),
            jax.ShapeDtypeStruct((2, parts // 2, rows, block), F32),
        ],
        [streams, before, taps, cotangent],
        "short_filters",
        1.2,
    )


def ahead(ext, distance):
    rows = ext.shape[0] - PAD_ROWS
    return (ext if distance == 0 else pltpu.roll(ext, ext.shape[0] - distance, 0))[:rows]


def short_transpose(ext, taps):
    return total([taps[j : j + 1] * ahead(ext, j) for j in range(taps.shape[0])])


def with_rows(block, rows):
    below = jnp.concatenate(rows + [jnp.zeros((PAD_ROWS - len(rows), block.shape[1]), F32)], axis=0)
    return jnp.concatenate([block, below], axis=0)


def prepare_kernel(
    own_ref, streams_ref, before_ref, after_ref, taps_ref, bias_ref, cot_ref,
    query_ref, key_ref, value_ref, cotangent_ref, gated_ref, carried_ref,
):
    rows = streams_ref.shape[1]
    rim = after_ref.shape[1]
    block = query_ref.shape[1] // 2
    for part in range(2):
        lanes = lanes_of(part, block)
        bias = bias_ref[:, lanes]
        short = shorts_of(streams_ref, before_ref, taps_ref, lanes)
        below = [
            short_filter_after(
                rows_of(after_ref[i, :, lanes]),
                rows_of(streams_ref[i, rows - rim :, lanes].astype(F32)),
                taps_ref[i, :, lanes],
            )
            for i in range(3)
        ]
        query, key, value = (with_rows(short[i], below[i]) for i in range(3))
        cotangent = with_rows(cot_ref[:, lanes].astype(F32), rows_of(after_ref[3, :, lanes]))
        query_ref[:, lanes] = short[0]
        key_ref[:, lanes] = key
        value_ref[:, lanes] = value
        cotangent_ref[:, lanes] = cotangent
        gated_ref[:, lanes] = bias * (key * value)
        carried_ref[:, lanes] = bias * (cotangent * query)


def prepare(own, streams, before, after, taps, bias, cotangent, parts, specs):
    _, rows, width = streams.shape
    long = jax.ShapeDtypeStruct((rows + PAD_ROWS, width), F32)
    return over_pairs(
        prepare_kernel,
        own,
        parts,
        specs,
        ["streams", "before", "after", "taps", "vector", "flat"],
        ["flat"] + ["long"] * 5,
        [jax.ShapeDtypeStruct((rows, width), F32)] + [long] * 5,
        [streams, before, after, taps, bias, cotangent],
        "rows_with_rim",
        2.0,
    )


def blocks_of(own_ref, refs):
    block = refs[0].shape[2]
    for j, ref in enumerate(refs):
        for place in range(2):
            first = pl.multiple_of(((2 * j + place) ^ own_ref[0]) * block, block)
            yield ref, place, pl.ds(first, block)


def mix_kernel(count, own_ref, query_ref, cotangent_ref, gated_ref, taps_ref, *refs):
    conv_refs, (mixed_ref, square_ref, grad_ref) = refs[:count], refs[count:]
    rows = query_ref.shape[0]
    block = conv_refs[0].shape[2]
    squares = jnp.zeros((rows, block), F32)
    for conv_ref, place, lanes in blocks_of(own_ref, conv_refs):
        direct = conv_ref[place] + gated_ref[:, lanes]
        mixed = query_ref[:, lanes] * direct[:rows]
        mixed_ref[:, lanes] = mixed
        squares = squares + mixed * mixed
        grad_ref[:, lanes] = short_transpose(cotangent_ref[:, lanes] * direct, taps_ref[0, :, lanes]).astype(BF16)
    square_ref[...] = lax.dot_general(
        jnp.ones((8, block), F32),
        squares,
        (((1,), (1,)), ((), ())),
        precision=lax.Precision.HIGHEST,
        preferred_element_type=F32,
    )[0:1]


def mix(own, query, cotangent, gated, taps, conv):
    rows, width = query.shape
    return pl.pallas_call(
        functools.partial(mix_kernel, len(conv)),
        out_shape=[
            jax.ShapeDtypeStruct((rows, width), F32),
            jax.ShapeDtypeStruct((1, rows), F32),
            jax.ShapeDtypeStruct((rows, width), BF16),
        ],
        in_specs=whole_operands(4 + len(conv)),
        compiler_params=params(),
        cost_estimate=measured(0.05),
        name="mixed_squares",
    )(own, query, cotangent, gated, taps, *conv)


def norm_kernel(channels, mixed_ref, square_ref, gain_ref, normed_ref):
    rows, width = mixed_ref.shape
    squares = jnp.broadcast_to(square_ref[...], (128, rows)).T
    scaling = lax.rsqrt(squares / channels + 1e-06)
    for start in range(0, width, 128):
        lanes = slice(start, start + 128)
        normed_ref[:, lanes] = (mixed_ref[:, lanes] * scaling * gain_ref[:, lanes]).astype(BF16)


def norm(channels, mixed, squares, gain):
    rows, width = mixed.shape
    return pl.pallas_call(
        functools.partial(norm_kernel, float(channels)),
        out_shape=jax.ShapeDtypeStruct((rows, width), BF16),
        compiler_params=params(),
        cost_estimate=measured(0.02),
        name="norm",
    )(mixed, squares, gain)


def finish_kernel(count, own_ref, key_ref, value_ref, carried_ref, taps_ref, grad_ref, *refs):
    corr_refs, (grads_ref, sent_ref, sems, first_sem) = refs[:count], refs[count:]
    first = pltpu.make_async_copy(grad_ref, grads_ref.at[0], first_sem)
    first.start()
    copies = [first]
    for place_of, (corr_ref, place, lanes) in enumerate(blocks_of(own_ref, corr_refs)):
        gated_grad = corr_ref[place] + carried_ref[:, lanes]
        for i, other_ref in ((1, value_ref), (2, key_ref)):
            grad = short_transpose(gated_grad * other_ref[:, lanes], taps_ref[i, :, lanes])
            sent_ref[i - 1, :, lanes] = grad.astype(BF16)
        copy = pltpu.make_async_copy(
            sent_ref.at[:, :, lanes], grads_ref.at[1:3, :, lanes], sems.at[place_of]
        )
        copy.start()
        copies.append(copy)
    for copy in copies:
        copy.wait()


def finish(own, key, value, carried, taps, grad, corr):
    rows, width = grad.shape
    blocks = 2 * len(corr)
    return pl.pallas_call(
        functools.partial(finish_kernel, len(corr)),
        out_shape=jax.ShapeDtypeStruct((3, rows, width), BF16),
        in_specs=whole_operands(5 + len(corr)),
        out_specs=pl.BlockSpec(memory_space=pl.ANY),
        scratch_shapes=[
            pltpu.VMEM((2, rows, width), BF16),
            pltpu.SemaphoreType.DMA((blocks,)),
            pltpu.SemaphoreType.DMA,
        ],
        compiler_params=params(),
        cost_estimate=measured(0.05),
        name="stream_grads",
    )(own, key, value, carried, taps, grad, *corr)


def swapped(block, apart, name):
    route = [(i, i ^ apart) for i in range(lax.axis_size("seq"))]
    with jax.named_scope(f"{name}_over_{apart}"):
        return lax.ppermute(block, "seq", route)


def summed_over(block, axis):
    count = lax.axis_size(axis)
    if count & (count - 1):
        return lax.psum(block, axis)
    result = block
    for apart in range(1, count):
        with jax.named_scope(f"squares_over_{apart}"):
            result = result + lax.ppermute(block, axis, [(i, i ^ apart) for i in range(count)])
    return result


def tied(value, other):
    return lax.optimization_barrier((value, other))


def within_pairs(name, block):
    return swapped(block, 1, name)


def between_pairs(name, blocks):
    order = list(range(2, len(blocks))) + [1]
    got = {j: swapped(blocks[j], 2 * j, name) for j in order}
    return [blocks[0]] + [got[j] for j in range(1, len(blocks))]


def together(blocks, edges):
    width = blocks.shape[-1]
    return jnp.concatenate([blocks.reshape(-1, width), edges.reshape(-1, width)], axis=0)


def apart_again(rows, blocks, edges):
    count = blocks.size // rows.shape[1]
    return rows[:count].reshape(blocks.shape), rows[count:].reshape(edges.shape)


def rows_after(own, came):
    after = jnp.where(own % 2 == 0, came[0], 0.0)
    pair = own // 2
    for k in range(1, len(came)):
        follows = (own % 2 == 1) & (pair ^ (pair + 1) == 2**k - 1)
        after = jnp.where(follows, came[k], after)
    return after


def sides_of(got):
    return jnp.stack([block[0] for block in got]), jnp.stack([block[1] for block in got])


def paired(kept, other):
    return [jnp.stack([kept[j], other[j]]) for j in range(kept.shape[0])]


def as_line(blocks):
    return blocks.reshape((-1,) + blocks.shape[2:])


def local(streams, short_taps, long_filter, skip_bias, norm_gain, cotangent):
    parts = lax.axis_size("seq")
    rows, width = cotangent.shape
    rim = short_taps.shape[1] - 1
    tables = stage_tables(parts, rows)
    specs = pair_specs(rows, 2 * width // parts, rim, short_taps.shape[1])
    own = lax.axis_index("seq").astype(jnp.int32)[None]
    bias, gain = skip_bias[None], norm_gain[None]

    filter_sent = arrange(own, long_filter, parts, specs)
    filter_got = between_pairs("filter", filter_sent)
    streams_later, filter_got[0] = tied(streams, filter_got[0])
    before = shift_along(streams_later[:, rows - rim :].astype(F32), "seq", 1)
    edges = jnp.concatenate([streams_later[:, :rim].astype(F32), cotangent[None, :rim].astype(F32)], axis=0)
    gated, carried = gate(own, streams, before, short_taps, cotangent, parts, specs)

    gated_other = within_pairs("gated", gated[1])
    carried_gone = carried[1]
    carried_gone, gated_other = tied(carried_gone, gated_other)
    gated_got = between_pairs("gated", paired(gated[0], gated_other))
    filter_kept, filter_gone = sides_of(filter_got)
    filter_other = within_pairs("filter", filter_gone)
    filter_blocks = paired(filter_kept, filter_other)
    carried_other, edges_other = apart_again(within_pairs("carried", together(carried_gone, edges)), carried_gone, edges)
    carried_pairs = paired(carried[0], carried_other)
    spec = spectrum(own, as_line(jnp.stack(filter_blocks)), tables)
    shape = (rows + PAD_ROWS, width // parts)
    gated_blocks = as_line(jnp.stack(gated_got))
    carried_pairs, gated_got[1] = tied(carried_pairs, gated_got[1])
    conv_sent = through_filter(own, gated_blocks, spec, tables, False, True).reshape((2, parts // 2) + shape)
    carried_pairs = list(carried_pairs)
    steps = [j for j in range(1, parts // 2) if j & (j + 1) == 0]
    alone = carried_pairs[0]
    for j in steps:
        carried_pairs[j] = together(carried_pairs[j], edges_other)
    carried_got = between_pairs("carried", carried_pairs)
    edges_got = []
    for j in steps:
        carried_got[j], came = apart_again(carried_got[j], alone, edges)
        edges_got.append(came)
    conv_pairs = paired(conv_sent[0], within_pairs("conv", conv_sent[1]))
    carried_blocks = jnp.stack(carried_got)
    conv_got = between_pairs("conv", conv_pairs)
    corr_sent = through_filter(own, as_line(carried_blocks), spec, tables, True, True).reshape((2, parts // 2) + shape)
    corr_pairs = paired(corr_sent[0], within_pairs("corr", corr_sent[1]))
    corr_pairs, conv_got[2] = tied(corr_pairs, conv_got[2])
    after = rows_after(own[0], [edges_other] + edges_got)
    after, conv_got[1] = tied(after, conv_got[1])
    query, key, value, later, gated_direct, carried_direct = prepare(
        own, streams, before, after, short_taps, bias, cotangent, parts, specs
    )
    corr_pairs, query = tied(corr_pairs, query)
    corr_got = between_pairs("corr", corr_pairs)
    query, corr_got[1] = tied(query, corr_got[1])
    mixed, squares, grad = mix(own, query, later, gated_direct, short_taps, conv_got)
    squares = summed_over(squares, "ch")
    normed = norm(width * lax.axis_size("ch"), mixed, squares, gain)
    grads = finish(own, key, value, carried_direct, short_taps, grad, corr_got)
    return normed, grads


EXACTNESS = lax.Precision.HIGHEST


def passed_along(block, axis, distance):
    devices = range(lax.axis_size(axis))
    route = [(i - distance, i) for i in devices if i - distance in devices]
    return lax.ppermute(block, axis, route)


def counting(amount):
    return jnp.arange(amount, dtype=jnp.int32)


def angle_pair(left_index, right_index, period, turning):
    product = left_index[:, None] * right_index[None, :] % period
    angles = product.astype(jnp.float32) * (turning * 2.0 * math.pi / period)
    return (jnp.cos(angles), jnp.sin(angles))


def neighbour_rows(edge_rows, offset):
    return passed_along(edge_rows, "seq", offset)


def swap_middle(blocks):
    return lax.all_to_all(blocks, "seq", split_axis=1, concat_axis=0, tiled=True)


def spread_forward(series):
    length, series_count, chan_width = series.shape
    devices = lax.axis_size("seq")
    position = lax.axis_index("seq")
    sub_rows = length // devices
    period = 2 * length * devices
    gathered = swap_middle(series.reshape(1, length, series_count, chan_width))
    cos_a, sin_a = angle_pair(counting(2 * devices), counting(devices), 2 * devices, -1.0)
    real_part = jnp.einsum("ka,absc->bksc", cos_a, gathered, precision=EXACTNESS)
    imag_part = jnp.einsum("ka,absc->bksc", sin_a, gathered, precision=EXACTNESS)
    spike_locations = position * sub_rows + counting(sub_rows)
    turn_cos, turn_sin = angle_pair(spike_locations, counting(2 * devices), period, -1.0)
    turn_cos = turn_cos[:, :, None, None]
    turn_sin = turn_sin[:, :, None, None]
    turned = jnp.concatenate(
        [real_part * turn_cos - imag_part * turn_sin, real_part * turn_sin + imag_part * turn_cos],
        axis=2,
    )
    swapped = swap_middle(turned)
    cos_b, sin_b = angle_pair(counting(length), counting(length), length, -1.0)
    primary = jnp.einsum("jb,bksc->jksc", cos_b, swapped, precision=EXACTNESS)
    second = jnp.einsum("jb,bksc->jksc", sin_b, swapped, precision=EXACTNESS)
    return (
        primary[:, :, :series_count] - second[:, :, series_count:],
        primary[:, :, series_count:] + second[:, :, :series_count],
    )


def spread_inverse(spec_re, spec_im):
    length, pair_rows, series_count, chan_width = spec_re.shape
    devices = lax.axis_size("seq")
    position = lax.axis_index("seq")
    sub_rows = length // devices
    period = 2 * length * devices
    cos_b, sin_b = angle_pair(counting(length), counting(length), length, 1.0)
    merged = jnp.concatenate([spec_re, spec_im], axis=2)
    primary = jnp.einsum("bj,jksc->kbsc", cos_b, merged, precision=EXACTNESS)
    second = jnp.einsum("bj,jksc->kbsc", sin_b, merged, precision=EXACTNESS)
    turned = jnp.concatenate(
        [
            primary[:, :, :series_count] - second[:, :, series_count:],
            primary[:, :, series_count:] + second[:, :, :series_count],
        ],
        axis=2,
    )
    swapped = swap_middle(turned)
    spike_locations = position * sub_rows + counting(sub_rows)
    turn_cos, turn_sin = angle_pair(counting(2 * devices), spike_locations, period, 1.0)
    turn_cos = turn_cos[:, :, None, None]
    turn_sin = turn_sin[:, :, None, None]
    real_part = swapped[:, :, :series_count]
    imag_part = swapped[:, :, series_count:]
    rotated_re = real_part * turn_cos - imag_part * turn_sin
    rotated_im = real_part * turn_sin + imag_part * turn_cos
    cos_a, sin_a = angle_pair(counting(devices), counting(2 * devices), 2 * devices, 1.0)
    result = jnp.einsum("ak,kbsc->basc", cos_a, rotated_re, precision=EXACTNESS) - jnp.einsum(
        "ak,kbsc->basc", sin_a, rotated_im, precision=EXACTNESS
    )
    returned = swap_middle(result / period)
    return returned.reshape(length, -1, chan_width)


def local_general(streams, short_taps, long_filter, skip_bias, norm_gain, cotangent):
    row_count = streams.shape[1]
    chan_width = streams.shape[2]
    rim_rows = short_taps.shape[1] - 1
    widened = streams.astype(jnp.float32)
    before = neighbour_rows(widened[:, row_count - rim_rows :, :], 1)
    extended = jnp.concatenate([before, widened], axis=1)
    shorts = jnp.zeros_like(widened)
    for offset in range(short_taps.shape[1]):
        shorts = (
            shorts
            + short_taps[:, offset, None, :]
            * extended[:, rim_rows - offset : rim_rows - offset + row_count, :]
        )
    short_q, short_k, short_v = (shorts[0], shorts[1], shorts[2])
    gated_input = short_k * short_v
    cot_wide = cotangent.astype(jnp.float32)
    carried = cot_wide * short_q
    series = jnp.stack([gated_input, long_filter, carried], axis=1)
    spec_re, spec_im = spread_forward(series)
    series_axis = 2
    gated_re = lax.index_in_dim(spec_re, 0, series_axis, keepdims=False)
    gated_im = lax.index_in_dim(spec_im, 0, series_axis, keepdims=False)
    filter_re = lax.index_in_dim(spec_re, 1, series_axis, keepdims=False)
    filter_im = lax.index_in_dim(spec_im, 1, series_axis, keepdims=False)
    carry_re = lax.index_in_dim(spec_re, 2, series_axis, keepdims=False)
    carry_im = lax.index_in_dim(spec_im, 2, series_axis, keepdims=False)
    output_re = filter_re * gated_re - filter_im * gated_im
    output_im = filter_re * gated_im + filter_im * gated_re
    backward_re = filter_re * carry_re + filter_im * carry_im
    backward_im = filter_re * carry_im - filter_im * carry_re
    inverse_re = jnp.stack([output_re, backward_re], axis=series_axis)
    inverse_im = jnp.stack([output_im, backward_im], axis=series_axis)
    result = spread_inverse(inverse_re, inverse_im)
    convolved = result[:, 0]
    correlated = result[:, 1]
    direct = convolved + skip_bias * gated_input
    mixed_out = short_q * direct
    square_sum = lax.psum(jnp.sum(mixed_out * mixed_out, axis=1), "ch")
    scaling = lax.rsqrt(square_sum[:, None] / (chan_width * lax.axis_size("ch")) + 1e-06)
    normed = (mixed_out * scaling * norm_gain).astype(jnp.bfloat16)
    gated_grad = correlated + skip_bias * carried
    short_grad = jnp.stack([cot_wide * direct, gated_grad * short_v, gated_grad * short_k])
    following = neighbour_rows(short_grad[:, :rim_rows, :], -1)
    grad_ext = jnp.concatenate([short_grad, following], axis=1)
    grads = jnp.zeros_like(short_grad)
    for offset in range(short_taps.shape[1]):
        grads = grads + short_taps[:, offset, None, :] * grad_ext[:, offset : offset + row_count, :]
    return (normed, grads.astype(jnp.bfloat16))


def solution(mesh):
    placed = (
        P(None, "seq", "ch"),
        P(None, None, "ch"),
        P("seq", "ch"),
        P("ch"),
        P("ch"),
        P("seq", "ch"),
    )

    def program(streams, short_taps, long_filter, skip_bias, norm_gain, cotangent):
        parts = mesh.shape["seq"]
        width = cotangent.shape[1] // mesh.shape["ch"]
        lanes_filled = width % (128 * parts) == 0 and parts in (4, 8, 16)
        return jax.shard_map(
            local if lanes_filled else local_general,
            mesh=mesh,
            in_specs=placed,
            out_specs=(P("seq", "ch"), P(None, "seq", "ch")),
            check_vma=False,
        )(streams, short_taps, long_filter, skip_bias, norm_gain, cotangent)

    return program
```

```python
import functools
import math

import jax
import jax.numpy as jnp
import numpy as np
from jax import lax
from jax.experimental import pallas as pl
from jax.experimental.pallas import tpu as pltpu
from jax.sharding import PartitionSpec as P

F32 = jnp.float32
BF16 = jnp.bfloat16
PAD_ROWS = 8
VMEM_BYTES = 24 * 1024 * 1024


def shift_along(block, axis, distance):
    devices = range(lax.axis_size(axis))
    route = [(i - distance, i) for i in devices if i - distance in devices]
    return lax.ppermute(block, axis, route)


def measured(microseconds):
    return pl.CostEstimate(flops=0, bytes_accessed=int(microseconds * 3.69e6), transcendentals=0)


def params():
    return pltpu.CompilerParams(vmem_limit_bytes=VMEM_BYTES)


def scaled(value, factor):
    if abs(factor) < 1e-12:
        return None
    if abs(factor - 1.0) < 1e-12:
        return value
    if abs(factor + 1.0) < 1e-12:
        return -value
    return value * factor


def total(terms):
    kept = [term for term in terms if term is not None]
    if not kept:
        return None
    result = kept[0]
    for term in kept[1:]:
        result = result + term
    return result


def plus(left, right):
    return total([left, right])


def minus(left, right):
    return total([left, None if right is None else -right])


def sending_place(apart, blocks, by_side):
    return (apart % 2) * (blocks // 2) + apart // 2 if by_side else apart


def dot(left, right):
    return lax.dot_general(left, right, (((1,), (0,)), ((), ())), preferred_element_type=F32)


def stage_tables(blocks, rows):
    period = 2 * blocks * rows
    place = np.arange(rows)
    turn = 2.0 * np.pi * ((place[:, None] * place[None, :]) % rows) / rows
    exact = np.concatenate([np.cos(turn), np.sin(turn)], axis=0)
    high = exact.astype(BF16)
    low = (exact - high.astype(np.float64)).astype(BF16)
    columns = -(-2 * (blocks + 1) // 128) * 128
    twiddles = np.zeros((rows, columns), np.float32)
    for k in range(blocks + 1):
        turn = 2.0 * np.pi * ((place * k) % period) / period
        twiddles[:, 2 * k], twiddles[:, 2 * k + 1] = np.cos(turn), np.sin(turn)
    return np.concatenate([high, high], axis=1), low, twiddles


def turned(twiddles, k, re, im, sign):
    if k == 0:
        return re, im
    cos = jnp.broadcast_to(twiddles[:, 2 * k : 2 * k + 1], re.shape)
    sin = jnp.broadcast_to(twiddles[:, 2 * k + 1 : 2 * k + 2], re.shape) * sign
    if im is None:
        return re * cos, re * sin
    return re * cos - im * sin, re * sin + im * cos


def store_split(split_ref, k, here, re, im):
    rows, width = split_ref.shape[1] // 2, split_ref.shape[2] // 2
    for value, lanes in ((re, slice(0, width)), (im, slice(width, 2 * width))):
        if value is None:
            value = jnp.zeros_like(re)
        high = value.astype(BF16)
        split_ref[k, here, lanes] = high
        split_ref[k, slice(rows + here.start, rows + here.stop), lanes] = (value - high.astype(F32)).astype(BF16)


def first_stage(own, x_ref, tw_ref, split_ref, tile):
    blocks, rows = x_ref.shape[0], x_ref.shape[1]
    for start in range(0, rows, tile):
        here = slice(start, start + tile)
        twiddles = tw_ref[here, :]
        x = [x_ref[a ^ own, here, :] for a in range(blocks)]

        def keep(k, re, im):
            store_split(split_ref, k, here, *turned(twiddles, k, re, im, -1.0))

        for k in range(blocks // 2 + 1):
            parts = []
            for parity in (0, 1):
                members = range(parity, blocks, 2)
                turn = [math.pi * ((a * k) % (2 * blocks)) / blocks for a in members]
                parts.append(total([scaled(x[a], math.cos(t)) for a, t in zip(members, turn)]))
                parts.append(total([scaled(x[a], math.sin(t)) for a, t in zip(members, turn)]))
            even_c, even_s, odd_c, odd_s = parts
            keep(k, plus(even_c, odd_c), None if k == 0 else -plus(even_s, odd_s))
            if 2 * k != blocks:
                keep(blocks - k, minus(even_c, odd_c), None if k == 0 else minus(even_s, odd_s))


def second_stage(table_high, table_low, split):
    rows, width = table_low.shape[1], split.shape[1] // 2
    sums = dot(table_high, split) + dot(table_low, split[:rows])
    return sums[:rows, :width], sums[:rows, width:], sums[rows:, :width], sums[rows:, width:]


def spectrum_kernel(own_ref, x_ref, high_ref, low_ref, tw_ref, spec_ref, split_ref):
    blocks, rows = x_ref.shape[0], x_ref.shape[1]
    first_stage(own_ref[0], x_ref, tw_ref, split_ref, 32)
    for k in range(blocks + 1):
        scale = (0.5 if k in (0, blocks) else 1.0) / (blocks * rows)
        cos_re, cos_im, sin_re, sin_im = second_stage(high_ref[...], low_ref[...], split_ref[k])
        spec_ref[k, :rows, :] = (cos_re + sin_im) * scale
        spec_ref[k, rows:, :] = (cos_im - sin_re) * scale


def last_stage(own, by_side, re_ref, im_ref, out_ref, tile):
    blocks, rows = re_ref.shape[0] - 1, re_ref.shape[1]
    for start in range(0, rows, tile):
        here = slice(start, start + tile)
        re = [re_ref[k, here, :] for k in range(blocks + 1)]
        im = {k: im_ref[k, here, :] for k in range(1, blocks)}
        for parity in (0, 1):
            sign = 1.0 - 2.0 * parity
            base = re[0] + sign * re[blocks]
            re_sum = {k: re[k] + sign * re[blocks - k] for k in range(1, blocks // 2)}
            im_sum = {k: im[k] - sign * im[blocks - k] for k in range(1, blocks // 2)}
            re_sum[blocks // 2] = re[blocks // 2]
            im_sum[blocks // 2] = im[blocks // 2]
            for a in range(parity, blocks, 2):
                terms = [base]
                for k in range(1, blocks // 2 + 1):
                    turn = math.pi * ((a * k) % (2 * blocks)) / blocks
                    terms.append(scaled(re_sum[k], math.cos(turn)))
                    terms.append(scaled(im_sum[k], -math.sin(turn)))
                value = total(terms)
                out_ref[sending_place(a ^ own, blocks, by_side), here, :] = value
                if start == 0 and a > 0:
                    place = sending_place((a - 1) ^ own, blocks, by_side)
                    out_ref[place, rows : rows + PAD_ROWS, :] = value[:PAD_ROWS]
    place = sending_place((blocks - 1) ^ own, blocks, by_side)
    out_ref[place, rows : rows + PAD_ROWS, :] = jnp.zeros((PAD_ROWS, out_ref.shape[2]), F32)


def product_kernel(
    conjugate, by_side, own_ref, x_ref, spec_ref, high_ref, low_ref, tw_ref, out_ref, split_ref, re_ref, im_ref
):
    blocks, rows = x_ref.shape[0], x_ref.shape[1]
    first_stage(own_ref[0], x_ref, tw_ref, split_ref, 32)
    sign = -1.0 if conjugate else 1.0
    tile = 32
    for k in range(blocks + 1):
        cos_re, cos_im, sin_re, sin_im = second_stage(high_ref[...], low_ref[...], split_ref[k])
        re_ref[k] = cos_re + sin_im
        im_ref[k] = cos_im - sin_re
    for k in range(blocks + 1):
        for start in range(0, rows, tile):
            here = slice(start, start + tile)
            x_re, x_im = re_ref[k, here, :], im_ref[k, here, :]
            h_re, h_im = spec_ref[k, here, :], spec_ref[k, rows + start : rows + start + tile, :] * sign
            store_split(split_ref, k, here, x_re * h_re - x_im * h_im, x_im * h_re + x_re * h_im)
    for k in range(blocks + 1):
        cos_re, cos_im, sin_re, sin_im = second_stage(high_ref[...], low_ref[...], split_ref[k])
        re, im = turned(tw_ref[...], k, cos_re - sin_im, cos_im + sin_re, 1.0)
        re_ref[k] = re
        im_ref[k] = im
    last_stage(own_ref[0], by_side, re_ref, im_ref, out_ref, tile)


def whole_operands(count):
    return [pl.BlockSpec(memory_space=pltpu.SMEM)] + [pl.BlockSpec(memory_space=pltpu.VMEM)] * count


def split_scratch(blocks, rows, width):
    return pltpu.VMEM((blocks + 1, 2 * rows, 2 * width), BF16)


def spectrum(own, x, tables):
    blocks, rows, width = x.shape
    return pl.pallas_call(
        spectrum_kernel,
        out_shape=jax.ShapeDtypeStruct((blocks + 1, 2 * rows, width), F32),
        in_specs=whole_operands(4),
        scratch_shapes=[split_scratch(blocks, rows, width)],
        compiler_params=params(),
        cost_estimate=measured(1.1),
        name="filter_spectrum",
    )(own, x, *tables)


def through_filter(own, x, spec, tables, conjugate, by_side):
    blocks, rows, width = x.shape
    part = pltpu.VMEM((blocks + 1, rows, width), F32)
    return pl.pallas_call(
        functools.partial(product_kernel, conjugate, by_side),
        out_shape=jax.ShapeDtypeStruct((blocks, rows + PAD_ROWS, width), F32),
        in_specs=whole_operands(5),
        scratch_shapes=[split_scratch(blocks, rows, width), part, part],
        compiler_params=params(),
        cost_estimate=measured(0.05 if conjugate else 20),
        name="correlation" if conjugate else "convolution",
    )(own, x, spec, *tables)


def row_number(shape):
    return lax.broadcasted_iota(jnp.int32, shape, 0)


def delayed(x, before, distance):
    moved = pltpu.roll(x, distance, 0)
    rows = row_number(x.shape)
    rim = len(before)
    for row in range(distance):
        moved = jnp.where(rows == row, before[rim - distance + row], moved)
    return moved


def rows_of(block):
    return [block[row : row + 1] for row in range(block.shape[0])]


def short_filter_after(after, last, taps):
    known = last + after
    return [
        total([taps[j : j + 1] * known[len(last) + row - j] for j in range(taps.shape[0])])
        for row in range(len(after))
    ]


def short_filter(x, before, taps):
    result = taps[0:1] * x
    for j in range(1, taps.shape[0]):
        result = result + taps[j : j + 1] * delayed(x, before, j)
    return result


def place_of_part(own_ref, part):
    return part ^ (own_ref[0] % 2)


def pair_specs(rows, pair, rim, count):
    def at(j, own):
        return j ^ (own[0] // 2)

    return {
        "streams": pl.BlockSpec((3, rows, pair), lambda j, own: (0, 0, at(j, own))),
        "before": pl.BlockSpec((3, rim, pair), lambda j, own: (0, 0, at(j, own))),
        "after": pl.BlockSpec((4, rim, pair), lambda j, own: (0, 0, at(j, own))),
        "taps": pl.BlockSpec((3, count, pair), lambda j, own: (0, 0, at(j, own))),
        "vector": pl.BlockSpec((1, pair), lambda j, own: (0, at(j, own))),
        "flat": pl.BlockSpec((rows, pair), lambda j, own: (0, at(j, own))),
        "long": pl.BlockSpec((rows + PAD_ROWS, pair), lambda j, own: (0, at(j, own))),
        "by_pair": pl.BlockSpec((1, 2, rows, pair // 2), lambda j, own: (j, 0, 0, 0)),
        "by_side": pl.BlockSpec((2, 1, rows, pair // 2), lambda j, own: (0, j, 0, 0)),
    }


def over_pairs(kernel, own, parts, specs, ins, outs, out_shape, operands, name, microseconds):
    return pl.pallas_call(
        kernel,
        grid_spec=pltpu.PrefetchScalarGridSpec(
            num_scalar_prefetch=1,
            grid=(parts // 2,),
            in_specs=[specs[i] for i in ins],
            out_specs=[specs[o] for o in outs],
        ),
        out_shape=out_shape,
        compiler_params=params(),
        cost_estimate=measured(0.02 * microseconds),
        name=name,
    )(own, *operands)


def lanes_of(part, block):
    return slice(part * block, (part + 1) * block)


def arrange_kernel(own_ref, x_ref, out_ref):
    block = out_ref.shape[3]
    for part in range(2):
        out_ref[0, place_of_part(own_ref, part)] = x_ref[:, lanes_of(part, block)]


def arrange(own, x, parts, specs):
    rows, width = x.shape
    out = jax.ShapeDtypeStruct((parts // 2, 2, rows, width // parts), F32)
    return over_pairs(arrange_kernel, own, parts, specs, ["flat"], ["by_pair"], [out], [x], "filter_blocks", 0.3)[0]


def shorts_of(streams_ref, before_ref, taps_ref, lanes):
    return [
        short_filter(streams_ref[i, :, lanes].astype(F32), rows_of(before_ref[i, :, lanes]), taps_ref[i, :, lanes])
        for i in range(3)
    ]


def gate_kernel(own_ref, streams_ref, before_ref, taps_ref, cot_ref, gated_ref, carried_ref):
    block = gated_ref.shape[3]
    for part in range(2):
        lanes = lanes_of(part, block)
        place = place_of_part(own_ref, part)
        short = shorts_of(streams_ref, before_ref, taps_ref, lanes)
        gated_ref[place, 0] = short[1] * short[2]
        carried_ref[place, 0] = cot_ref[:, lanes].astype(F32) * short[0]


def gate(own, streams, before, taps, cotangent, parts, specs):
    _, rows, width = streams.shape
    block = width // parts
    return over_pairs(
        gate_kernel,
        own,
        parts,
        specs,
        ["streams", "before", "taps", "flat"],
        ["by_side", "by_side"],
        [
            jax.ShapeDtypeStruct((2, parts // 2, rows, block), F32),
            jax.ShapeDtypeStruct((2, parts // 2, rows, block), F32),
        ],
        [streams, before, taps, cotangent],
        "short_filters",
        1.2,
    )


def ahead(ext, distance):
    rows = ext.shape[0] - PAD_ROWS
    return (ext if distance == 0 else pltpu.roll(ext, ext.shape[0] - distance, 0))[:rows]


def short_transpose(ext, taps):
    return total([taps[j : j + 1] * ahead(ext, j) for j in range(taps.shape[0])])


def with_rows(block, rows):
    below = jnp.concatenate(rows + [jnp.zeros((PAD_ROWS - len(rows), block.shape[1]), F32)], axis=0)
    return jnp.concatenate([block, below], axis=0)


def prepare_kernel(
    own_ref, streams_ref, before_ref, after_ref, taps_ref, bias_ref, cot_ref,
    query_ref, key_ref, value_ref, cotangent_ref, gated_ref, carried_ref,
):
    rows = streams_ref.shape[1]
    rim = after_ref.shape[1]
    block = query_ref.shape[1] // 2
    for part in range(2):
        lanes = lanes_of(part, block)
        bias = bias_ref[:, lanes]
        short = shorts_of(streams_ref, before_ref, taps_ref, lanes)
        below = [
            short_filter_after(
                rows_of(after_ref[i, :, lanes]),
                rows_of(streams_ref[i, rows - rim :, lanes].astype(F32)),
                taps_ref[i, :, lanes],
            )
            for i in range(3)
        ]
        query, key, value = (with_rows(short[i], below[i]) for i in range(3))
        cotangent = with_rows(cot_ref[:, lanes].astype(F32), rows_of(after_ref[3, :, lanes]))
        query_ref[:, lanes] = short[0]
        key_ref[:, lanes] = key
        value_ref[:, lanes] = value
        cotangent_ref[:, lanes] = cotangent
        gated_ref[:, lanes] = bias * (key * value)
        carried_ref[:, lanes] = bias * (cotangent * query)


def prepare(own, streams, before, after, taps, bias, cotangent, parts, specs):
    _, rows, width = streams.shape
    long = jax.ShapeDtypeStruct((rows + PAD_ROWS, width), F32)
    return over_pairs(
        prepare_kernel,
        own,
        parts,
        specs,
        ["streams", "before", "after", "taps", "vector", "flat"],
        ["flat"] + ["long"] * 5,
        [jax.ShapeDtypeStruct((rows, width), F32)] + [long] * 5,
        [streams, before, after, taps, bias, cotangent],
        "rows_with_rim",
        2.0,
    )


def blocks_of(own_ref, refs):
    block = refs[0].shape[2]
    for j, ref in enumerate(refs):
        for place in range(2):
            first = pl.multiple_of(((2 * j + place) ^ own_ref[0]) * block, block)
            yield ref, place, pl.ds(first, block)


def mix_kernel(count, own_ref, query_ref, cotangent_ref, gated_ref, taps_ref, *refs):
    conv_refs, (mixed_ref, square_ref, grad_ref) = refs[:count], refs[count:]
    rows = query_ref.shape[0]
    block = conv_refs[0].shape[2]
    squares = jnp.zeros((rows, block), F32)
    for conv_ref, place, lanes in blocks_of(own_ref, conv_refs):
        direct = conv_ref[place] + gated_ref[:, lanes]
        mixed = query_ref[:, lanes] * direct[:rows]
        mixed_ref[:, lanes] = mixed
        squares = squares + mixed * mixed
        grad_ref[:, lanes] = short_transpose(cotangent_ref[:, lanes] * direct, taps_ref[0, :, lanes]).astype(BF16)
    square_ref[...] = lax.dot_general(
        jnp.ones((8, block), F32),
        squares,
        (((1,), (1,)), ((), ())),
        precision=lax.Precision.HIGHEST,
        preferred_element_type=F32,
    )[0:1]


def mix(own, query, cotangent, gated, taps, conv):
    rows, width = query.shape
    return pl.pallas_call(
        functools.partial(mix_kernel, len(conv)),
        out_shape=[
            jax.ShapeDtypeStruct((rows, width), F32),
            jax.ShapeDtypeStruct((1, rows), F32),
            jax.ShapeDtypeStruct((rows, width), BF16),
        ],
        in_specs=whole_operands(4 + len(conv)),
        compiler_params=params(),
        cost_estimate=measured(0.05),
        name="mixed_squares",
    )(own, query, cotangent, gated, taps, *conv)


def norm_kernel(channels, mixed_ref, square_ref, gain_ref, normed_ref):
    rows, width = mixed_ref.shape
    squares = jnp.broadcast_to(square_ref[...], (128, rows)).T
    scaling = lax.rsqrt(squares / channels + 1e-06)
    for start in range(0, width, 128):
        lanes = slice(start, start + 128)
        normed_ref[:, lanes] = (mixed_ref[:, lanes] * scaling * gain_ref[:, lanes]).astype(BF16)


def norm(channels, mixed, squares, gain):
    rows, width = mixed.shape
    return pl.pallas_call(
        functools.partial(norm_kernel, float(channels)),
        out_shape=jax.ShapeDtypeStruct((rows, width), BF16),
        compiler_params=params(),
        cost_estimate=measured(0.02),
        name="norm",
    )(mixed, squares, gain)


def finish_kernel(count, own_ref, key_ref, value_ref, carried_ref, taps_ref, grad_ref, *refs):
    corr_refs, (grads_ref, sent_ref, sems, first_sem) = refs[:count], refs[count:]
    first = pltpu.make_async_copy(grad_ref, grads_ref.at[0], first_sem)
    first.start()
    copies = [first]
    for place_of, (corr_ref, place, lanes) in enumerate(blocks_of(own_ref, corr_refs)):
        gated_grad = corr_ref[place] + carried_ref[:, lanes]
        for i, other_ref in ((1, value_ref), (2, key_ref)):
            grad = short_transpose(gated_grad * other_ref[:, lanes], taps_ref[i, :, lanes])
            sent_ref[i - 1, :, lanes] = grad.astype(BF16)
        copy = pltpu.make_async_copy(
            sent_ref.at[:, :, lanes], grads_ref.at[1:3, :, lanes], sems.at[place_of]
        )
        copy.start()
        copies.append(copy)
    for copy in copies:
        copy.wait()


def finish(own, key, value, carried, taps, grad, corr):
    rows, width = grad.shape
    blocks = 2 * len(corr)
    return pl.pallas_call(
        functools.partial(finish_kernel, len(corr)),
        out_shape=jax.ShapeDtypeStruct((3, rows, width), BF16),
        in_specs=whole_operands(5 + len(corr)),
        out_specs=pl.BlockSpec(memory_space=pl.ANY),
        scratch_shapes=[
            pltpu.VMEM((2, rows, width), BF16),
            pltpu.SemaphoreType.DMA((blocks,)),
            pltpu.SemaphoreType.DMA,
        ],
        compiler_params=params(),
        cost_estimate=measured(0.05),
        name="stream_grads",
    )(own, key, value, carried, taps, grad, *corr)


def swapped(block, apart, name):
    route = [(i, i ^ apart) for i in range(lax.axis_size("seq"))]
    with jax.named_scope(f"{name}_over_{apart}"):
        return lax.ppermute(block, "seq", route)


def summed_over(block, axis):
    count = lax.axis_size(axis)
    if count & (count - 1):
        return lax.psum(block, axis)
    result = block
    for apart in range(1, count):
        with jax.named_scope(f"squares_over_{apart}"):
            result = result + lax.ppermute(block, axis, [(i, i ^ apart) for i in range(count)])
    return result


def tied(value, other):
    return lax.optimization_barrier((value, other))


def within_pairs(name, block):
    return swapped(block, 1, name)


def between_pairs(name, blocks):
    order = list(range(2, len(blocks))) + [1]
    got = {j: swapped(blocks[j], 2 * j, name) for j in order}
    return [blocks[0]] + [got[j] for j in range(1, len(blocks))]


def together(blocks, edges):
    width = blocks.shape[-1]
    return jnp.concatenate([blocks.reshape(-1, width), edges.reshape(-1, width)], axis=0)


def apart_again(rows, blocks, edges):
    count = blocks.size // rows.shape[1]
    return rows[:count].reshape(blocks.shape), rows[count:].reshape(edges.shape)


def rows_after(own, came):
    after = jnp.where(own % 2 == 0, came[0], 0.0)
    pair = own // 2
    for k in range(1, len(came)):
        follows = (own % 2 == 1) & (pair ^ (pair + 1) == 2**k - 1)
        after = jnp.where(follows, came[k], after)
    return after


def in_turn(blocks, earlier):
    blocks, earlier = list(blocks), list(earlier)
    for j in range(2, len(blocks)):
        blocks[j], earlier[j] = tied(blocks[j], earlier[j])
    return blocks, earlier


def sides_of(got):
    return jnp.stack([block[0] for block in got]), jnp.stack([block[1] for block in got])


def paired(kept, other):
    return [jnp.stack([kept[j], other[j]]) for j in range(kept.shape[0])]


def as_line(blocks):
    return blocks.reshape((-1,) + blocks.shape[2:])


def local(streams, short_taps, long_filter, skip_bias, norm_gain, cotangent):
    parts = lax.axis_size("seq")
    rows, width = cotangent.shape
    rim = short_taps.shape[1] - 1
    tables = stage_tables(parts, rows)
    specs = pair_specs(rows, 2 * width // parts, rim, short_taps.shape[1])
    own = lax.axis_index("seq").astype(jnp.int32)[None]
    bias, gain = skip_bias[None], norm_gain[None]

    filter_sent = arrange(own, long_filter, parts, specs)
    filter_got = between_pairs("filter", filter_sent)
    streams_later, filter_got[0] = tied(streams, filter_got[0])
    before = shift_along(streams_later[:, rows - rim :].astype(F32), "seq", 1)
    edges = jnp.concatenate([streams_later[:, :rim].astype(F32), cotangent[None, :rim].astype(F32)], axis=0)
    gated, carried = gate(own, streams, before, short_taps, cotangent, parts, specs)

    gated_other = within_pairs("gated", gated[1])
    carried_gone = carried[1]
    carried_gone, gated_other = tied(carried_gone, gated_other)
    gated_got = between_pairs("gated", paired(gated[0], gated_other))
    filter_kept, filter_gone = sides_of(filter_got)
    filter_other = within_pairs("filter", filter_gone)
    filter_blocks = paired(filter_kept, filter_other)
    carried_other, edges_other = apart_again(within_pairs("carried", together(carried_gone, edges)), carried_gone, edges)
    carried_pairs = paired(carried[0], carried_other)
    spec = spectrum(own, as_line(jnp.stack(filter_blocks)), tables)
    shape = (rows + PAD_ROWS, width // parts)
    gated_blocks = as_line(jnp.stack(gated_got))
    carried_pairs, gated_got[1] = tied(carried_pairs, gated_got[1])
    conv_sent = through_filter(own, gated_blocks, spec, tables, False, True).reshape((2, parts // 2) + shape)
    carried_pairs = list(carried_pairs)
    steps = [j for j in range(1, parts // 2) if j & (j + 1) == 0]
    alone = carried_pairs[0]
    for j in steps:
        carried_pairs[j] = together(carried_pairs[j], edges_other)
    carried_got = between_pairs("carried", carried_pairs)
    edges_got = []
    for j in steps:
        carried_got[j], came = apart_again(carried_got[j], alone, edges)
        edges_got.append(came)
    conv_pairs = paired(conv_sent[0], within_pairs("conv", conv_sent[1]))
    conv_pairs, carried_got = in_turn(conv_pairs, carried_got)
    carried_blocks = jnp.stack(carried_got)
    conv_got = between_pairs("conv", conv_pairs)
    corr_sent = through_filter(own, as_line(carried_blocks), spec, tables, True, True).reshape((2, parts // 2) + shape)
    corr_pairs = paired(corr_sent[0], within_pairs("corr", corr_sent[1]))
    corr_pairs, conv_got[2] = tied(corr_pairs, conv_got[2])
    after = rows_after(own[0], [edges_other] + edges_got)
    after, conv_got[1] = tied(after, conv_got[1])
    query, key, value, later, gated_direct, carried_direct = prepare(
        own, streams, before, after, short_taps, bias, cotangent, parts, specs
    )
    corr_pairs, query = tied(corr_pairs, query)
    corr_got = between_pairs("corr", corr_pairs)
    query, corr_got[1] = tied(query, corr_got[1])
    mixed, squares, grad = mix(own, query, later, gated_direct, short_taps, conv_got)
    squares = summed_over(squares, "ch")
    normed = norm(width * lax.axis_size("ch"), mixed, squares, gain)
    grads = finish(own, key, value, carried_direct, short_taps, grad, corr_got)
    return normed, grads


EXACTNESS = lax.Precision.HIGHEST


def passed_along(block, axis, distance):
    devices = range(lax.axis_size(axis))
    route = [(i - distance, i) for i in devices if i - distance in devices]
    return lax.ppermute(block, axis, route)


def counting(amount):
    return jnp.arange(amount, dtype=jnp.int32)


def angle_pair(left_index, right_index, period, turning):
    product = left_index[:, None] * right_index[None, :] % period
    angles = product.astype(jnp.float32) * (turning * 2.0 * math.pi / period)
    return (jnp.cos(angles), jnp.sin(angles))


def neighbour_rows(edge_rows, offset):
    return passed_along(edge_rows, "seq", offset)


def swap_middle(blocks):
    return lax.all_to_all(blocks, "seq", split_axis=1, concat_axis=0, tiled=True)


def spread_forward(series):
    length, series_count, chan_width = series.shape
    devices = lax.axis_size("seq")
    position = lax.axis_index("seq")
    sub_rows = length // devices
    period = 2 * length * devices
    gathered = swap_middle(series.reshape(1, length, series_count, chan_width))
    cos_a, sin_a = angle_pair(counting(2 * devices), counting(devices), 2 * devices, -1.0)
    real_part = jnp.einsum("ka,absc->bksc", cos_a, gathered, precision=EXACTNESS)
    imag_part = jnp.einsum("ka,absc->bksc", sin_a, gathered, precision=EXACTNESS)
    spike_locations = position * sub_rows + counting(sub_rows)
    turn_cos, turn_sin = angle_pair(spike_locations, counting(2 * devices), period, -1.0)
    turn_cos = turn_cos[:, :, None, None]
    turn_sin = turn_sin[:, :, None, None]
    turned = jnp.concatenate(
        [real_part * turn_cos - imag_part * turn_sin, real_part * turn_sin + imag_part * turn_cos],
        axis=2,
    )
    swapped = swap_middle(turned)
    cos_b, sin_b = angle_pair(counting(length), counting(length), length, -1.0)
    primary = jnp.einsum("jb,bksc->jksc", cos_b, swapped, precision=EXACTNESS)
    second = jnp.einsum("jb,bksc->jksc", sin_b, swapped, precision=EXACTNESS)
    return (
        primary[:, :, :series_count] - second[:, :, series_count:],
        primary[:, :, series_count:] + second[:, :, :series_count],
    )


def spread_inverse(spec_re, spec_im):
    length, pair_rows, series_count, chan_width = spec_re.shape
    devices = lax.axis_size("seq")
    position = lax.axis_index("seq")
    sub_rows = length // devices
    period = 2 * length * devices
    cos_b, sin_b = angle_pair(counting(length), counting(length), length, 1.0)
    merged = jnp.concatenate([spec_re, spec_im], axis=2)
    primary = jnp.einsum("bj,jksc->kbsc", cos_b, merged, precision=EXACTNESS)
    second = jnp.einsum("bj,jksc->kbsc", sin_b, merged, precision=EXACTNESS)
    turned = jnp.concatenate(
        [
            primary[:, :, :series_count] - second[:, :, series_count:],
            primary[:, :, series_count:] + second[:, :, :series_count],
        ],
        axis=2,
    )
    swapped = swap_middle(turned)
    spike_locations = position * sub_rows + counting(sub_rows)
    turn_cos, turn_sin = angle_pair(counting(2 * devices), spike_locations, period, 1.0)
    turn_cos = turn_cos[:, :, None, None]
    turn_sin = turn_sin[:, :, None, None]
    real_part = swapped[:, :, :series_count]
    imag_part = swapped[:, :, series_count:]
    rotated_re = real_part * turn_cos - imag_part * turn_sin
    rotated_im = real_part * turn_sin + imag_part * turn_cos
    cos_a, sin_a = angle_pair(counting(devices), counting(2 * devices), 2 * devices, 1.0)
    result = jnp.einsum("ak,kbsc->basc", cos_a, rotated_re, precision=EXACTNESS) - jnp.einsum(
        "ak,kbsc->basc", sin_a, rotated_im, precision=EXACTNESS
    )
    returned = swap_middle(result / period)
    return returned.reshape(length, -1, chan_width)


def local_general(streams, short_taps, long_filter, skip_bias, norm_gain, cotangent):
    row_count = streams.shape[1]
    chan_width = streams.shape[2]
    rim_rows = short_taps.shape[1] - 1
    widened = streams.astype(jnp.float32)
    before = neighbour_rows(widened[:, row_count - rim_rows :, :], 1)
    extended = jnp.concatenate([before, widened], axis=1)
    shorts = jnp.zeros_like(widened)
    for offset in range(short_taps.shape[1]):
        shorts = (
            shorts
            + short_taps[:, offset, None, :]
            * extended[:, rim_rows - offset : rim_rows - offset + row_count, :]
        )
    short_q, short_k, short_v = (shorts[0], shorts[1], shorts[2])
    gated_input = short_k * short_v
    cot_wide = cotangent.astype(jnp.float32)
    carried = cot_wide * short_q
    series = jnp.stack([gated_input, long_filter, carried], axis=1)
    spec_re, spec_im = spread_forward(series)
    series_axis = 2
    gated_re = lax.index_in_dim(spec_re, 0, series_axis, keepdims=False)
    gated_im = lax.index_in_dim(spec_im, 0, series_axis, keepdims=False)
    filter_re = lax.index_in_dim(spec_re, 1, series_axis, keepdims=False)
    filter_im = lax.index_in_dim(spec_im, 1, series_axis, keepdims=False)
    carry_re = lax.index_in_dim(spec_re, 2, series_axis, keepdims=False)
    carry_im = lax.index_in_dim(spec_im, 2, series_axis, keepdims=False)
    output_re = filter_re * gated_re - filter_im * gated_im
    output_im = filter_re * gated_im + filter_im * gated_re
    backward_re = filter_re * carry_re + filter_im * carry_im
    backward_im = filter_re * carry_im - filter_im * carry_re
    inverse_re = jnp.stack([output_re, backward_re], axis=series_axis)
    inverse_im = jnp.stack([output_im, backward_im], axis=series_axis)
    result = spread_inverse(inverse_re, inverse_im)
    convolved = result[:, 0]
    correlated = result[:, 1]
    direct = convolved + skip_bias * gated_input
    mixed_out = short_q * direct
    square_sum = lax.psum(jnp.sum(mixed_out * mixed_out, axis=1), "ch")
    scaling = lax.rsqrt(square_sum[:, None] / (chan_width * lax.axis_size("ch")) + 1e-06)
    normed = (mixed_out * scaling * norm_gain).astype(jnp.bfloat16)
    gated_grad = correlated + skip_bias * carried
    short_grad = jnp.stack([cot_wide * direct, gated_grad * short_v, gated_grad * short_k])
    following = neighbour_rows(short_grad[:, :rim_rows, :], -1)
    grad_ext = jnp.concatenate([short_grad, following], axis=1)
    grads = jnp.zeros_like(short_grad)
    for offset in range(short_taps.shape[1]):
        grads = grads + short_taps[:, offset, None, :] * grad_ext[:, offset : offset + row_count, :]
    return (normed, grads.astype(jnp.bfloat16))


def solution(mesh):
    placed = (
        P(None, "seq", "ch"),
        P(None, None, "ch"),
        P("seq", "ch"),
        P("ch"),
        P("ch"),
        P("seq", "ch"),
    )

    def program(streams, short_taps, long_filter, skip_bias, norm_gain, cotangent):
        parts = mesh.shape["seq"]
        width = cotangent.shape[1] // mesh.shape["ch"]
        lanes_filled = width % (128 * parts) == 0 and parts in (4, 8, 16)
        return jax.shard_map(
            local if lanes_filled else local_general,
            mesh=mesh,
            in_specs=placed,
            out_specs=(P("seq", "ch"), P(None, "seq", "ch")),
            check_vma=False,
        )(streams, short_taps, long_filter, skip_bias, norm_gain, cotangent)

    return program
```

```python
import functools
import math

import jax
import jax.numpy as jnp
import numpy as np
from jax import lax
from jax.experimental import pallas as pl
from jax.experimental.pallas import tpu as pltpu
from jax.sharding import PartitionSpec as P

F32 = jnp.float32
BF16 = jnp.bfloat16
PAD_ROWS = 8
VMEM_BYTES = 24 * 1024 * 1024


def shift_along(block, axis, distance):
    devices = range(lax.axis_size(axis))
    route = [(i - distance, i) for i in devices if i - distance in devices]
    return lax.ppermute(block, axis, route)


def measured(microseconds):
    return pl.CostEstimate(flops=0, bytes_accessed=int(microseconds * 3.69e6), transcendentals=0)


def params():
    return pltpu.CompilerParams(vmem_limit_bytes=VMEM_BYTES)


def scaled(value, factor):
    if abs(factor) < 1e-12:
        return None
    if abs(factor - 1.0) < 1e-12:
        return value
    if abs(factor + 1.0) < 1e-12:
        return -value
    return value * factor


def total(terms):
    kept = [term for term in terms if term is not None]
    if not kept:
        return None
    result = kept[0]
    for term in kept[1:]:
        result = result + term
    return result


def plus(left, right):
    return total([left, right])


def minus(left, right):
    return total([left, None if right is None else -right])


def sending_place(apart, blocks, by_side):
    return (apart % 2) * (blocks // 2) + apart // 2 if by_side else apart


def dot(left, right):
    return lax.dot_general(left, right, (((1,), (0,)), ((), ())), preferred_element_type=F32)


def stage_tables(blocks, rows):
    period = 2 * blocks * rows
    place = np.arange(rows)
    turn = 2.0 * np.pi * ((place[:, None] * place[None, :]) % rows) / rows
    exact = np.concatenate([np.cos(turn), np.sin(turn)], axis=0)
    high = exact.astype(BF16)
    low = (exact - high.astype(np.float64)).astype(BF16)
    columns = -(-2 * (blocks + 1) // 128) * 128
    twiddles = np.zeros((rows, columns), np.float32)
    for k in range(blocks + 1):
        turn = 2.0 * np.pi * ((place * k) % period) / period
        twiddles[:, 2 * k], twiddles[:, 2 * k + 1] = np.cos(turn), np.sin(turn)
    return np.concatenate([high, high], axis=1), low, twiddles


def turned(twiddles, k, re, im, sign):
    if k == 0:
        return re, im
    cos = jnp.broadcast_to(twiddles[:, 2 * k : 2 * k + 1], re.shape)
    sin = jnp.broadcast_to(twiddles[:, 2 * k + 1 : 2 * k + 2], re.shape) * sign
    if im is None:
        return re * cos, re * sin
    return re * cos - im * sin, re * sin + im * cos


def store_split(split_ref, k, here, re, im):
    rows, width = split_ref.shape[1] // 2, split_ref.shape[2] // 2
    for value, lanes in ((re, slice(0, width)), (im, slice(width, 2 * width))):
        if value is None:
            value = jnp.zeros_like(re)
        high = value.astype(BF16)
        split_ref[k, here, lanes] = high
        split_ref[k, slice(rows + here.start, rows + here.stop), lanes] = (value - high.astype(F32)).astype(BF16)


def first_stage(own, x_ref, tw_ref, split_ref, tile):
    blocks, rows = x_ref.shape[0], x_ref.shape[1]
    for start in range(0, rows, tile):
        here = slice(start, start + tile)
        twiddles = tw_ref[here, :]
        x = [x_ref[a ^ own, here, :] for a in range(blocks)]

        def keep(k, re, im):
            store_split(split_ref, k, here, *turned(twiddles, k, re, im, -1.0))

        for k in range(blocks // 2 + 1):
            parts = []
            for parity in (0, 1):
                members = range(parity, blocks, 2)
                turn = [math.pi * ((a * k) % (2 * blocks)) / blocks for a in members]
                parts.append(total([scaled(x[a], math.cos(t)) for a, t in zip(members, turn)]))
                parts.append(total([scaled(x[a], math.sin(t)) for a, t in zip(members, turn)]))
            even_c, even_s, odd_c, odd_s = parts
            keep(k, plus(even_c, odd_c), None if k == 0 else -plus(even_s, odd_s))
            if 2 * k != blocks:
                keep(blocks - k, minus(even_c, odd_c), None if k == 0 else minus(even_s, odd_s))


def second_stage(table_high, table_low, split):
    rows, width = table_low.shape[1], split.shape[1] // 2
    sums = dot(table_high, split) + dot(table_low, split[:rows])
    return sums[:rows, :width], sums[:rows, width:], sums[rows:, :width], sums[rows:, width:]


def spectrum_kernel(own_ref, x_ref, high_ref, low_ref, tw_ref, spec_ref, split_ref):
    blocks, rows = x_ref.shape[0], x_ref.shape[1]
    first_stage(own_ref[0], x_ref, tw_ref, split_ref, 32)
    for k in range(blocks + 1):
        scale = (0.5 if k in (0, blocks) else 1.0) / (blocks * rows)
        cos_re, cos_im, sin_re, sin_im = second_stage(high_ref[...], low_ref[...], split_ref[k])
        spec_ref[k, :rows, :] = (cos_re + sin_im) * scale
        spec_ref[k, rows:, :] = (cos_im - sin_re) * scale


def last_stage(own, by_side, re_ref, im_ref, out_ref, tile):
    blocks, rows = re_ref.shape[0] - 1, re_ref.shape[1]
    for start in range(0, rows, tile):
        here = slice(start, start + tile)
        re = [re_ref[k, here, :] for k in range(blocks + 1)]
        im = {k: im_ref[k, here, :] for k in range(1, blocks)}
        for parity in (0, 1):
            sign = 1.0 - 2.0 * parity
            base = re[0] + sign * re[blocks]
            re_sum = {k: re[k] + sign * re[blocks - k] for k in range(1, blocks // 2)}
            im_sum = {k: im[k] - sign * im[blocks - k] for k in range(1, blocks // 2)}
            re_sum[blocks // 2] = re[blocks // 2]
            im_sum[blocks // 2] = im[blocks // 2]
            for a in range(parity, blocks, 2):
                terms = [base]
                for k in range(1, blocks // 2 + 1):
                    turn = math.pi * ((a * k) % (2 * blocks)) / blocks
                    terms.append(scaled(re_sum[k], math.cos(turn)))
                    terms.append(scaled(im_sum[k], -math.sin(turn)))
                value = total(terms)
                out_ref[sending_place(a ^ own, blocks, by_side), here, :] = value
                if start == 0 and a > 0:
                    place = sending_place((a - 1) ^ own, blocks, by_side)
                    out_ref[place, rows : rows + PAD_ROWS, :] = value[:PAD_ROWS]
    place = sending_place((blocks - 1) ^ own, blocks, by_side)
    out_ref[place, rows : rows + PAD_ROWS, :] = jnp.zeros((PAD_ROWS, out_ref.shape[2]), F32)


def product_kernel(
    conjugate, by_side, own_ref, x_ref, spec_ref, high_ref, low_ref, tw_ref, out_ref, split_ref, re_ref, im_ref
):
    blocks, rows = x_ref.shape[0], x_ref.shape[1]
    first_stage(own_ref[0], x_ref, tw_ref, split_ref, 32)
    sign = -1.0 if conjugate else 1.0
    tile = 32
    for k in range(blocks + 1):
        cos_re, cos_im, sin_re, sin_im = second_stage(high_ref[...], low_ref[...], split_ref[k])
        re_ref[k] = cos_re + sin_im
        im_ref[k] = cos_im - sin_re
    for k in range(blocks + 1):
        for start in range(0, rows, tile):
            here = slice(start, start + tile)
            x_re, x_im = re_ref[k, here, :], im_ref[k, here, :]
            h_re, h_im = spec_ref[k, here, :], spec_ref[k, rows + start : rows + start + tile, :] * sign
            store_split(split_ref, k, here, x_re * h_re - x_im * h_im, x_im * h_re + x_re * h_im)
    for k in range(blocks + 1):
        cos_re, cos_im, sin_re, sin_im = second_stage(high_ref[...], low_ref[...], split_ref[k])
        re, im = turned(tw_ref[...], k, cos_re - sin_im, cos_im + sin_re, 1.0)
        re_ref[k] = re
        im_ref[k] = im
    last_stage(own_ref[0], by_side, re_ref, im_ref, out_ref, tile)


def whole_operands(count):
    return [pl.BlockSpec(memory_space=pltpu.SMEM)] + [pl.BlockSpec(memory_space=pltpu.VMEM)] * count


def split_scratch(blocks, rows, width):
    return pltpu.VMEM((blocks + 1, 2 * rows, 2 * width), BF16)


def spectrum(own, x, tables):
    blocks, rows, width = x.shape
    return pl.pallas_call(
        spectrum_kernel,
        out_shape=jax.ShapeDtypeStruct((blocks + 1, 2 * rows, width), F32),
        in_specs=whole_operands(4),
        scratch_shapes=[split_scratch(blocks, rows, width)],
        compiler_params=params(),
        cost_estimate=measured(1.1),
        name="filter_spectrum",
    )(own, x, *tables)


def through_filter(own, x, spec, tables, conjugate, by_side):
    blocks, rows, width = x.shape
    part = pltpu.VMEM((blocks + 1, rows, width), F32)
    return pl.pallas_call(
        functools.partial(product_kernel, conjugate, by_side),
        out_shape=jax.ShapeDtypeStruct((blocks, rows + PAD_ROWS, width), F32),
        in_specs=whole_operands(5),
        scratch_shapes=[split_scratch(blocks, rows, width), part, part],
        compiler_params=params(),
        cost_estimate=measured(0.05 if conjugate else 20),
        name="correlation" if conjugate else "convolution",
    )(own, x, spec, *tables)


def row_number(shape):
    return lax.broadcasted_iota(jnp.int32, shape, 0)


def delayed(x, before, distance):
    moved = pltpu.roll(x, distance, 0)
    rows = row_number(x.shape)
    rim = len(before)
    for row in range(distance):
        moved = jnp.where(rows == row, before[rim - distance + row], moved)
    return moved


def rows_of(block):
    return [block[row : row + 1] for row in range(block.shape[0])]


def short_filter_after(after, last, taps):
    known = last + after
    return [
        total([taps[j : j + 1] * known[len(last) + row - j] for j in range(taps.shape[0])])
        for row in range(len(after))
    ]


def short_filter(x, before, taps):
    result = taps[0:1] * x
    for j in range(1, taps.shape[0]):
        result = result + taps[j : j + 1] * delayed(x, before, j)
    return result


def place_of_part(own_ref, part):
    return part ^ (own_ref[0] % 2)


def pair_specs(rows, pair, rim, count):
    def at(j, own):
        return j ^ (own[0] // 2)

    return {
        "streams": pl.BlockSpec((3, rows, pair), lambda j, own: (0, 0, at(j, own))),
        "before": pl.BlockSpec((3, rim, pair), lambda j, own: (0, 0, at(j, own))),
        "after": pl.BlockSpec((4, rim, pair), lambda j, own: (0, 0, at(j, own))),
        "taps": pl.BlockSpec((3, count, pair), lambda j, own: (0, 0, at(j, own))),
        "vector": pl.BlockSpec((1, pair), lambda j, own: (0, at(j, own))),
        "flat": pl.BlockSpec((rows, pair), lambda j, own: (0, at(j, own))),
        "long": pl.BlockSpec((rows + PAD_ROWS, pair), lambda j, own: (0, at(j, own))),
        "by_pair": pl.BlockSpec((1, 2, rows, pair // 2), lambda j, own: (j, 0, 0, 0)),
        "by_side": pl.BlockSpec((2, 1, rows, pair // 2), lambda j, own: (0, j, 0, 0)),
    }


def over_pairs(kernel, own, parts, specs, ins, outs, out_shape, operands, name, microseconds):
    return pl.pallas_call(
        kernel,
        grid_spec=pltpu.PrefetchScalarGridSpec(
            num_scalar_prefetch=1,
            grid=(parts // 2,),
            in_specs=[specs[i] for i in ins],
            out_specs=[specs[o] for o in outs],
        ),
        out_shape=out_shape,
        compiler_params=params(),
        cost_estimate=measured(0.02 * microseconds),
        name=name,
    )(own, *operands)


def lanes_of(part, block):
    return slice(part * block, (part + 1) * block)


def arrange_kernel(own_ref, x_ref, out_ref, sems):
    blocks, _, block = out_ref.shape
    copies = [
        pltpu.make_async_copy(x_ref.at[:, lanes_of(part, block)], out_ref.at[part ^ own_ref[0]], sems.at[part])
        for part in range(blocks)
    ]
    for copy in copies:
        copy.start()
    for copy in copies:
        copy.wait()


def arrange(own, x, parts):
    rows, width = x.shape
    block = width // parts
    blocks = pl.pallas_call(
        arrange_kernel,
        in_specs=[pl.BlockSpec(memory_space=pltpu.SMEM), pl.BlockSpec(memory_space=pl.ANY)],
        out_specs=pl.BlockSpec(memory_space=pl.ANY),
        out_shape=jax.ShapeDtypeStruct((parts, rows, block), F32),
        scratch_shapes=[pltpu.SemaphoreType.DMA((parts,))],
        compiler_params=pltpu.CompilerParams(vmem_limit_bytes=24 * 1024 * 1024),
        cost_estimate=measured(0.02),
        name="filter_blocks",
    )(own, x)
    return blocks.reshape(parts // 2, 2, rows, block)


def shorts_of(streams_ref, before_ref, taps_ref, lanes):
    return [
        short_filter(streams_ref[i, :, lanes].astype(F32), rows_of(before_ref[i, :, lanes]), taps_ref[i, :, lanes])
        for i in range(3)
    ]


def gate_kernel(own_ref, streams_ref, before_ref, taps_ref, cot_ref, gated_ref, carried_ref):
    block = gated_ref.shape[3]
    for part in range(2):
        lanes = lanes_of(part, block)
        place = place_of_part(own_ref, part)
        short = shorts_of(streams_ref, before_ref, taps_ref, lanes)
        gated_ref[place, 0] = short[1] * short[2]
        carried_ref[place, 0] = cot_ref[:, lanes].astype(F32) * short[0]


def gate(own, streams, before, taps, cotangent, parts, specs):
    _, rows, width = streams.shape
    block = width // parts
    return over_pairs(
        gate_kernel,
        own,
        parts,
        specs,
        ["streams", "before", "taps", "flat"],
        ["by_side", "by_side"],
        [
            jax.ShapeDtypeStruct((2, parts // 2, rows, block), F32),
            jax.ShapeDtypeStruct((2, parts // 2, rows, block), F32),
        ],
        [streams, before, taps, cotangent],
        "short_filters",
        1.2,
    )


def ahead(ext, distance):
    rows = ext.shape[0] - PAD_ROWS
    return (ext if distance == 0 else pltpu.roll(ext, ext.shape[0] - distance, 0))[:rows]


def short_transpose(ext, taps):
    return total([taps[j : j + 1] * ahead(ext, j) for j in range(taps.shape[0])])


def with_rows(block, rows):
    below = jnp.concatenate(rows + [jnp.zeros((PAD_ROWS - len(rows), block.shape[1]), F32)], axis=0)
    return jnp.concatenate([block, below], axis=0)


def prepare_kernel(
    own_ref, streams_ref, before_ref, after_ref, taps_ref, bias_ref, cot_ref,
    query_ref, key_ref, value_ref, cotangent_ref, gated_ref, carried_ref,
):
    rows = streams_ref.shape[1]
    rim = after_ref.shape[1]
    block = query_ref.shape[1] // 2
    for part in range(2):
        lanes = lanes_of(part, block)
        bias = bias_ref[:, lanes]
        short = shorts_of(streams_ref, before_ref, taps_ref, lanes)
        below = [
            short_filter_after(
                rows_of(after_ref[i, :, lanes]),
                rows_of(streams_ref[i, rows - rim :, lanes].astype(F32)),
                taps_ref[i, :, lanes],
            )
            for i in range(3)
        ]
        query, key, value = (with_rows(short[i], below[i]) for i in range(3))
        cotangent = with_rows(cot_ref[:, lanes].astype(F32), rows_of(after_ref[3, :, lanes]))
        query_ref[:, lanes] = short[0]
        key_ref[:, lanes] = key
        value_ref[:, lanes] = value
        cotangent_ref[:, lanes] = cotangent
        gated_ref[:, lanes] = bias * (key * value)
        carried_ref[:, lanes] = bias * (cotangent * query)


def prepare(own, streams, before, after, taps, bias, cotangent, parts, specs):
    _, rows, width = streams.shape
    long = jax.ShapeDtypeStruct((rows + PAD_ROWS, width), F32)
    return over_pairs(
        prepare_kernel,
        own,
        parts,
        specs,
        ["streams", "before", "after", "taps", "vector", "flat"],
        ["flat"] + ["long"] * 5,
        [jax.ShapeDtypeStruct((rows, width), F32)] + [long] * 5,
        [streams, before, after, taps, bias, cotangent],
        "rows_with_rim",
        2.0,
    )


def blocks_of(own_ref, refs):
    block = refs[0].shape[2]
    for j, ref in enumerate(refs):
        for place in range(2):
            first = pl.multiple_of(((2 * j + place) ^ own_ref[0]) * block, block)
            yield ref, place, pl.ds(first, block)


def mix_kernel(count, own_ref, query_ref, cotangent_ref, gated_ref, taps_ref, *refs):
    conv_refs, (mixed_ref, square_ref, grad_ref) = refs[:count], refs[count:]
    rows = query_ref.shape[0]
    block = conv_refs[0].shape[2]
    squares = jnp.zeros((rows, block), F32)
    for conv_ref, place, lanes in blocks_of(own_ref, conv_refs):
        direct = conv_ref[place] + gated_ref[:, lanes]
        mixed = query_ref[:, lanes] * direct[:rows]
        mixed_ref[:, lanes] = mixed
        squares = squares + mixed * mixed
        grad_ref[:, lanes] = short_transpose(cotangent_ref[:, lanes] * direct, taps_ref[0, :, lanes]).astype(BF16)
    square_ref[...] = lax.dot_general(
        jnp.ones((8, block), F32),
        squares,
        (((1,), (1,)), ((), ())),
        precision=lax.Precision.HIGHEST,
        preferred_element_type=F32,
    )[0:1]


def mix(own, query, cotangent, gated, taps, conv):
    rows, width = query.shape
    return pl.pallas_call(
        functools.partial(mix_kernel, len(conv)),
        out_shape=[
            jax.ShapeDtypeStruct((rows, width), F32),
            jax.ShapeDtypeStruct((1, rows), F32),
            jax.ShapeDtypeStruct((rows, width), BF16),
        ],
        in_specs=whole_operands(4 + len(conv)),
        compiler_params=params(),
        cost_estimate=measured(0.05),
        name="mixed_squares",
    )(own, query, cotangent, gated, taps, *conv)


def norm_kernel(channels, mixed_ref, square_ref, gain_ref, normed_ref, sent_ref, sems):
    rows, width = mixed_ref.shape
    squares = jnp.broadcast_to(square_ref[...], (128, rows)).T
    scaling = lax.rsqrt(squares / channels + 1e-06)
    copies = []
    for start in range(0, width, 128):
        lanes = slice(start, start + 128)
        sent_ref[:, lanes] = (mixed_ref[:, lanes] * scaling * gain_ref[:, lanes]).astype(BF16)
        copies.append(
            pltpu.make_async_copy(sent_ref.at[:, lanes], normed_ref.at[:, lanes], sems.at[start // 128])
        )
        copies[-1].start()
    for copy in copies:
        copy.wait()


def norm(channels, mixed, squares, gain):
    rows, width = mixed.shape
    return pl.pallas_call(
        functools.partial(norm_kernel, float(channels)),
        out_shape=jax.ShapeDtypeStruct((rows, width), BF16),
        out_specs=pl.BlockSpec(memory_space=pl.ANY),
        scratch_shapes=[pltpu.VMEM((rows, width), BF16), pltpu.SemaphoreType.DMA((width // 128,))],
        compiler_params=params(),
        cost_estimate=measured(0.02),
        name="norm",
    )(mixed, squares, gain)


def finish_kernel(count, own_ref, key_ref, value_ref, carried_ref, taps_ref, grad_ref, *refs):
    corr_refs, (grads_ref, sent_ref, sems, first_sem) = refs[:count], refs[count:]
    first = pltpu.make_async_copy(grad_ref, grads_ref.at[0], first_sem)
    first.start()
    copies = [first]
    for place_of, (corr_ref, place, lanes) in enumerate(blocks_of(own_ref, corr_refs)):
        gated_grad = corr_ref[place] + carried_ref[:, lanes]
        for i, other_ref in ((1, value_ref), (2, key_ref)):
            grad = short_transpose(gated_grad * other_ref[:, lanes], taps_ref[i, :, lanes])
            sent_ref[i - 1, :, lanes] = grad.astype(BF16)
        copy = pltpu.make_async_copy(
            sent_ref.at[:, :, lanes], grads_ref.at[1:3, :, lanes], sems.at[place_of]
        )
        copy.start()
        copies.append(copy)
    for copy in copies:
        copy.wait()


def finish(own, key, value, carried, taps, grad, corr):
    rows, width = grad.shape
    blocks = 2 * len(corr)
    return pl.pallas_call(
        functools.partial(finish_kernel, len(corr)),
        out_shape=jax.ShapeDtypeStruct((3, rows, width), BF16),
        in_specs=whole_operands(5 + len(corr)),
        out_specs=pl.BlockSpec(memory_space=pl.ANY),
        scratch_shapes=[
            pltpu.VMEM((2, rows, width), BF16),
            pltpu.SemaphoreType.DMA((blocks,)),
            pltpu.SemaphoreType.DMA,
        ],
        compiler_params=params(),
        cost_estimate=measured(0.05),
        name="stream_grads",
    )(own, key, value, carried, taps, grad, *corr)


def swapped(block, apart, name):
    route = [(i, i ^ apart) for i in range(lax.axis_size("seq"))]
    with jax.named_scope(f"{name}_over_{apart}"):
        return lax.ppermute(block, "seq", route)


def summed_over(block, axis):
    count = lax.axis_size(axis)
    if count & (count - 1):
        return lax.psum(block, axis)
    result = block
    for apart in range(1, count):
        with jax.named_scope(f"squares_over_{apart}"):
            result = result + lax.ppermute(block, axis, [(i, i ^ apart) for i in range(count)])
    return result


def tied(value, other):
    return lax.optimization_barrier((value, other))


def within_pairs(name, block):
    return swapped(block, 1, name)


def between_pairs(name, blocks):
    order = list(range(2, len(blocks))) + [1]
    got = {j: swapped(blocks[j], 2 * j, name) for j in order}
    return [blocks[0]] + [got[j] for j in range(1, len(blocks))]


def together(blocks, edges):
    width = blocks.shape[-1]
    return jnp.concatenate([blocks.reshape(-1, width), edges.reshape(-1, width)], axis=0)


def apart_again(rows, blocks, edges):
    count = blocks.size // rows.shape[1]
    return rows[:count].reshape(blocks.shape), rows[count:].reshape(edges.shape)


def rows_after(own, came):
    after = jnp.where(own % 2 == 0, came[0], 0.0)
    pair = own // 2
    for k in range(1, len(came)):
        follows = (own % 2 == 1) & (pair ^ (pair + 1) == 2**k - 1)
        after = jnp.where(follows, came[k], after)
    return after


def in_turn(blocks, earlier):
    blocks, earlier = list(blocks), list(earlier)
    for j in range(2, len(blocks)):
        blocks[j], earlier[j] = tied(blocks[j], earlier[j])
    return blocks, earlier


def sides_of(got):
    return jnp.stack([block[0] for block in got]), jnp.stack([block[1] for block in got])


def paired(kept, other):
    return [jnp.stack([kept[j], other[j]]) for j in range(kept.shape[0])]


def as_line(blocks):
    return blocks.reshape((-1,) + blocks.shape[2:])


def local(streams, short_taps, long_filter, skip_bias, norm_gain, cotangent):
    parts = lax.axis_size("seq")
    rows, width = cotangent.shape
    rim = short_taps.shape[1] - 1
    tables = stage_tables(parts, rows)
    specs = pair_specs(rows, 2 * width // parts, rim, short_taps.shape[1])
    own = lax.axis_index("seq").astype(jnp.int32)[None]
    bias, gain = skip_bias[None], norm_gain[None]

    filter_sent = arrange(own, long_filter, parts)
    filter_got = between_pairs("filter", filter_sent)
    streams_later, filter_got[0] = tied(streams, filter_got[0])
    before = shift_along(streams_later[:, rows - rim :].astype(F32), "seq", 1)
    edges = jnp.concatenate([streams_later[:, :rim].astype(F32), cotangent[None, :rim].astype(F32)], axis=0)
    gated, carried = gate(own, streams, before, short_taps, cotangent, parts, specs)

    gated_other = within_pairs("gated", gated[1])
    carried_gone = carried[1]
    carried_gone, gated_other = tied(carried_gone, gated_other)
    gated_got = between_pairs("gated", paired(gated[0], gated_other))
    filter_kept, filter_gone = sides_of(filter_got)
    filter_other = within_pairs("filter", filter_gone)
    filter_blocks = paired(filter_kept, filter_other)
    carried_other, edges_other = apart_again(within_pairs("carried", together(carried_gone, edges)), carried_gone, edges)
    carried_pairs = paired(carried[0], carried_other)
    spec = spectrum(own, as_line(jnp.stack(filter_blocks)), tables)
    shape = (rows + PAD_ROWS, width // parts)
    gated_blocks = as_line(jnp.stack(gated_got))
    carried_pairs, gated_got[1] = tied(carried_pairs, gated_got[1])
    conv_sent = through_filter(own, gated_blocks, spec, tables, False, True).reshape((2, parts // 2) + shape)
    carried_pairs = list(carried_pairs)
    steps = [j for j in range(1, parts // 2) if j & (j + 1) == 0]
    alone = carried_pairs[0]
    for j in steps:
        carried_pairs[j] = together(carried_pairs[j], edges_other)
    carried_got = between_pairs("carried", carried_pairs)
    edges_got = []
    for j in steps:
        carried_got[j], came = apart_again(carried_got[j], alone, edges)
        edges_got.append(came)
    conv_pairs = paired(conv_sent[0], within_pairs("conv", conv_sent[1]))
    conv_pairs, carried_got = in_turn(conv_pairs, carried_got)
    carried_blocks = jnp.stack(carried_got)
    conv_got = between_pairs("conv", conv_pairs)
    corr_sent = through_filter(own, as_line(carried_blocks), spec, tables, True, True).reshape((2, parts // 2) + shape)
    corr_pairs = paired(corr_sent[0], within_pairs("corr", corr_sent[1]))
    corr_pairs, conv_got[2] = tied(corr_pairs, conv_got[2])
    after = rows_after(own[0], [edges_other] + edges_got)
    after, conv_got[1] = tied(after, conv_got[1])
    query, key, value, later, gated_direct, carried_direct = prepare(
        own, streams, before, after, short_taps, bias, cotangent, parts, specs
    )
    corr_pairs, query = tied(corr_pairs, query)
    corr_got = between_pairs("corr", corr_pairs)
    query, corr_got[1] = tied(query, corr_got[1])
    mixed, squares, grad = mix(own, query, later, gated_direct, short_taps, conv_got)
    squares = summed_over(squares, "ch")
    normed = norm(width * lax.axis_size("ch"), mixed, squares, gain)
    grads = finish(own, key, value, carried_direct, short_taps, grad, corr_got)
    return normed, grads


EXACTNESS = lax.Precision.HIGHEST


def passed_along(block, axis, distance):
    devices = range(lax.axis_size(axis))
    route = [(i - distance, i) for i in devices if i - distance in devices]
    return lax.ppermute(block, axis, route)


def counting(amount):
    return jnp.arange(amount, dtype=jnp.int32)


def angle_pair(left_index, right_index, period, turning):
    product = left_index[:, None] * right_index[None, :] % period
    angles = product.astype(jnp.float32) * (turning * 2.0 * math.pi / period)
    return (jnp.cos(angles), jnp.sin(angles))


def neighbour_rows(edge_rows, offset):
    return passed_along(edge_rows, "seq", offset)


def swap_middle(blocks):
    return lax.all_to_all(blocks, "seq", split_axis=1, concat_axis=0, tiled=True)


def spread_forward(series):
    length, series_count, chan_width = series.shape
    devices = lax.axis_size("seq")
    position = lax.axis_index("seq")
    sub_rows = length // devices
    period = 2 * length * devices
    gathered = swap_middle(series.reshape(1, length, series_count, chan_width))
    cos_a, sin_a = angle_pair(counting(2 * devices), counting(devices), 2 * devices, -1.0)
    real_part = jnp.einsum("ka,absc->bksc", cos_a, gathered, precision=EXACTNESS)
    imag_part = jnp.einsum("ka,absc->bksc", sin_a, gathered, precision=EXACTNESS)
    spike_locations = position * sub_rows + counting(sub_rows)
    turn_cos, turn_sin = angle_pair(spike_locations, counting(2 * devices), period, -1.0)
    turn_cos = turn_cos[:, :, None, None]
    turn_sin = turn_sin[:, :, None, None]
    turned = jnp.concatenate(
        [real_part * turn_cos - imag_part * turn_sin, real_part * turn_sin + imag_part * turn_cos],
        axis=2,
    )
    swapped = swap_middle(turned)
    cos_b, sin_b = angle_pair(counting(length), counting(length), length, -1.0)
    primary = jnp.einsum("jb,bksc->jksc", cos_b, swapped, precision=EXACTNESS)
    second = jnp.einsum("jb,bksc->jksc", sin_b, swapped, precision=EXACTNESS)
    return (
        primary[:, :, :series_count] - second[:, :, series_count:],
        primary[:, :, series_count:] + second[:, :, :series_count],
    )


def spread_inverse(spec_re, spec_im):
    length, pair_rows, series_count, chan_width = spec_re.shape
    devices = lax.axis_size("seq")
    position = lax.axis_index("seq")
    sub_rows = length // devices
    period = 2 * length * devices
    cos_b, sin_b = angle_pair(counting(length), counting(length), length, 1.0)
    merged = jnp.concatenate([spec_re, spec_im], axis=2)
    primary = jnp.einsum("bj,jksc->kbsc", cos_b, merged, precision=EXACTNESS)
    second = jnp.einsum("bj,jksc->kbsc", sin_b, merged, precision=EXACTNESS)
    turned = jnp.concatenate(
        [
            primary[:, :, :series_count] - second[:, :, series_count:],
            primary[:, :, series_count:] + second[:, :, :series_count],
        ],
        axis=2,
    )
    swapped = swap_middle(turned)
    spike_locations = position * sub_rows + counting(sub_rows)
    turn_cos, turn_sin = angle_pair(counting(2 * devices), spike_locations, period, 1.0)
    turn_cos = turn_cos[:, :, None, None]
    turn_sin = turn_sin[:, :, None, None]
    real_part = swapped[:, :, :series_count]
    imag_part = swapped[:, :, series_count:]
    rotated_re = real_part * turn_cos - imag_part * turn_sin
    rotated_im = real_part * turn_sin + imag_part * turn_cos
    cos_a, sin_a = angle_pair(counting(devices), counting(2 * devices), 2 * devices, 1.0)
    result = jnp.einsum("ak,kbsc->basc", cos_a, rotated_re, precision=EXACTNESS) - jnp.einsum(
        "ak,kbsc->basc", sin_a, rotated_im, precision=EXACTNESS
    )
    returned = swap_middle(result / period)
    return returned.reshape(length, -1, chan_width)


def local_general(streams, short_taps, long_filter, skip_bias, norm_gain, cotangent):
    row_count = streams.shape[1]
    chan_width = streams.shape[2]
    rim_rows = short_taps.shape[1] - 1
    widened = streams.astype(jnp.float32)
    before = neighbour_rows(widened[:, row_count - rim_rows :, :], 1)
    extended = jnp.concatenate([before, widened], axis=1)
    shorts = jnp.zeros_like(widened)
    for offset in range(short_taps.shape[1]):
        shorts = (
            shorts
            + short_taps[:, offset, None, :]
            * extended[:, rim_rows - offset : rim_rows - offset + row_count, :]
        )
    short_q, short_k, short_v = (shorts[0], shorts[1], shorts[2])
    gated_input = short_k * short_v
    cot_wide = cotangent.astype(jnp.float32)
    carried = cot_wide * short_q
    series = jnp.stack([gated_input, long_filter, carried], axis=1)
    spec_re, spec_im = spread_forward(series)
    series_axis = 2
    gated_re = lax.index_in_dim(spec_re, 0, series_axis, keepdims=False)
    gated_im = lax.index_in_dim(spec_im, 0, series_axis, keepdims=False)
    filter_re = lax.index_in_dim(spec_re, 1, series_axis, keepdims=False)
    filter_im = lax.index_in_dim(spec_im, 1, series_axis, keepdims=False)
    carry_re = lax.index_in_dim(spec_re, 2, series_axis, keepdims=False)
    carry_im = lax.index_in_dim(spec_im, 2, series_axis, keepdims=False)
    output_re = filter_re * gated_re - filter_im * gated_im
    output_im = filter_re * gated_im + filter_im * gated_re
    backward_re = filter_re * carry_re + filter_im * carry_im
    backward_im = filter_re * carry_im - filter_im * carry_re
    inverse_re = jnp.stack([output_re, backward_re], axis=series_axis)
    inverse_im = jnp.stack([output_im, backward_im], axis=series_axis)
    result = spread_inverse(inverse_re, inverse_im)
    convolved = result[:, 0]
    correlated = result[:, 1]
    direct = convolved + skip_bias * gated_input
    mixed_out = short_q * direct
    square_sum = lax.psum(jnp.sum(mixed_out * mixed_out, axis=1), "ch")
    scaling = lax.rsqrt(square_sum[:, None] / (chan_width * lax.axis_size("ch")) + 1e-06)
    normed = (mixed_out * scaling * norm_gain).astype(jnp.bfloat16)
    gated_grad = correlated + skip_bias * carried
    short_grad = jnp.stack([cot_wide * direct, gated_grad * short_v, gated_grad * short_k])
    following = neighbour_rows(short_grad[:, :rim_rows, :], -1)
    grad_ext = jnp.concatenate([short_grad, following], axis=1)
    grads = jnp.zeros_like(short_grad)
    for offset in range(short_taps.shape[1]):
        grads = grads + short_taps[:, offset, None, :] * grad_ext[:, offset : offset + row_count, :]
    return (normed, grads.astype(jnp.bfloat16))


def solution(mesh):
    placed = (
        P(None, "seq", "ch"),
        P(None, None, "ch"),
        P("seq", "ch"),
        P("ch"),
        P("ch"),
        P("seq", "ch"),
    )

    def program(streams, short_taps, long_filter, skip_bias, norm_gain, cotangent):
        parts = mesh.shape["seq"]
        width = cotangent.shape[1] // mesh.shape["ch"]
        lanes_filled = width % (128 * parts) == 0 and parts in (4, 8, 16)
        return jax.shard_map(
            local if lanes_filled else local_general,
            mesh=mesh,
            in_specs=placed,
            out_specs=(P("seq", "ch"), P(None, "seq", "ch")),
            check_vma=False,
        )(streams, short_taps, long_filter, skip_bias, norm_gain, cotangent)

    return program
```

```python
import functools
import math

import jax
import jax.numpy as jnp
import numpy as np
from jax import lax
from jax.experimental import pallas as pl
from jax.experimental.pallas import tpu as pltpu
from jax.sharding import PartitionSpec as P

F32 = jnp.float32
BF16 = jnp.bfloat16
PAD_ROWS = 8
VMEM_BYTES = 24 * 1024 * 1024


def shift_along(block, axis, distance):
    devices = range(lax.axis_size(axis))
    route = [(i - distance, i) for i in devices if i - distance in devices]
    return lax.ppermute(block, axis, route)


def measured(microseconds):
    return pl.CostEstimate(flops=0, bytes_accessed=int(microseconds * 3.69e6), transcendentals=0)


def params():
    return pltpu.CompilerParams(vmem_limit_bytes=VMEM_BYTES)


def scaled(value, factor):
    if abs(factor) < 1e-12:
        return None
    if abs(factor - 1.0) < 1e-12:
        return value
    if abs(factor + 1.0) < 1e-12:
        return -value
    return value * factor


def total(terms):
    kept = [term for term in terms if term is not None]
    if not kept:
        return None
    result = kept[0]
    for term in kept[1:]:
        result = result + term
    return result


def plus(left, right):
    return total([left, right])


def minus(left, right):
    return total([left, None if right is None else -right])


def sending_place(apart, blocks, by_side):
    return (apart % 2) * (blocks // 2) + apart // 2 if by_side else apart


def dot(left, right):
    return lax.dot_general(left, right, (((1,), (0,)), ((), ())), preferred_element_type=F32)


def stage_tables(blocks, rows):
    period = 2 * blocks * rows
    place = np.arange(rows)
    turn = 2.0 * np.pi * ((place[:, None] * place[None, :]) % rows) / rows
    exact = np.concatenate([np.cos(turn), np.sin(turn)], axis=0)
    high = exact.astype(BF16)
    low = (exact - high.astype(np.float64)).astype(BF16)
    columns = -(-2 * (blocks + 1) // 128) * 128
    twiddles = np.zeros((rows, columns), np.float32)
    for k in range(blocks + 1):
        turn = 2.0 * np.pi * ((place * k) % period) / period
        twiddles[:, 2 * k], twiddles[:, 2 * k + 1] = np.cos(turn), np.sin(turn)
    return np.concatenate([high, high], axis=1), low, twiddles


def turned(twiddles, k, re, im, sign):
    if k == 0:
        return re, im
    cos = jnp.broadcast_to(twiddles[:, 2 * k : 2 * k + 1], re.shape)
    sin = jnp.broadcast_to(twiddles[:, 2 * k + 1 : 2 * k + 2], re.shape) * sign
    if im is None:
        return re * cos, re * sin
    return re * cos - im * sin, re * sin + im * cos


def store_split(split_ref, k, here, re, im):
    rows, width = split_ref.shape[1] // 2, split_ref.shape[2] // 2
    for value, lanes in ((re, slice(0, width)), (im, slice(width, 2 * width))):
        if value is None:
            value = jnp.zeros_like(re)
        high = value.astype(BF16)
        split_ref[k, here, lanes] = high
        split_ref[k, slice(rows + here.start, rows + here.stop), lanes] = (value - high.astype(F32)).astype(BF16)


def first_stage(own, x_ref, tw_ref, split_ref, tile):
    blocks, rows = x_ref.shape[0], x_ref.shape[1]
    for start in range(0, rows, tile):
        here = slice(start, start + tile)
        twiddles = tw_ref[here, :]
        x = [x_ref[a ^ own, here, :] for a in range(blocks)]

        def keep(k, re, im):
            store_split(split_ref, k, here, *turned(twiddles, k, re, im, -1.0))

        for k in range(blocks // 2 + 1):
            parts = []
            for parity in (0, 1):
                members = range(parity, blocks, 2)
                turn = [math.pi * ((a * k) % (2 * blocks)) / blocks for a in members]
                parts.append(total([scaled(x[a], math.cos(t)) for a, t in zip(members, turn)]))
                parts.append(total([scaled(x[a], math.sin(t)) for a, t in zip(members, turn)]))
            even_c, even_s, odd_c, odd_s = parts
            keep(k, plus(even_c, odd_c), None if k == 0 else -plus(even_s, odd_s))
            if 2 * k != blocks:
                keep(blocks - k, minus(even_c, odd_c), None if k == 0 else minus(even_s, odd_s))


def second_stage(table_high, table_low, split):
    rows, width = table_low.shape[1], split.shape[1] // 2
    sums = dot(table_high, split) + dot(table_low, split[:rows])
    return sums[:rows, :width], sums[:rows, width:], sums[rows:, :width], sums[rows:, width:]


def spectrum_kernel(own_ref, x_ref, high_ref, low_ref, tw_ref, spec_ref, split_ref):
    blocks, rows = x_ref.shape[0], x_ref.shape[1]
    first_stage(own_ref[0], x_ref, tw_ref, split_ref, 32)
    for k in range(blocks + 1):
        scale = (0.5 if k in (0, blocks) else 1.0) / (blocks * rows)
        cos_re, cos_im, sin_re, sin_im = second_stage(high_ref[...], low_ref[...], split_ref[k])
        spec_ref[k, :rows, :] = (cos_re + sin_im) * scale
        spec_ref[k, rows:, :] = (cos_im - sin_re) * scale


def last_stage(own, by_side, re_ref, im_ref, out_ref, tile):
    blocks, rows = re_ref.shape[0] - 1, re_ref.shape[1]
    for start in range(0, rows, tile):
        here = slice(start, start + tile)
        re = [re_ref[k, here, :] for k in range(blocks + 1)]
        im = {k: im_ref[k, here, :] for k in range(1, blocks)}
        for parity in (0, 1):
            sign = 1.0 - 2.0 * parity
            base = re[0] + sign * re[blocks]
            re_sum = {k: re[k] + sign * re[blocks - k] for k in range(1, blocks // 2)}
            im_sum = {k: im[k] - sign * im[blocks - k] for k in range(1, blocks // 2)}
            re_sum[blocks // 2] = re[blocks // 2]
            im_sum[blocks // 2] = im[blocks // 2]
            for a in range(parity, blocks, 2):
                terms = [base]
                for k in range(1, blocks // 2 + 1):
                    turn = math.pi * ((a * k) % (2 * blocks)) / blocks
                    terms.append(scaled(re_sum[k], math.cos(turn)))
                    terms.append(scaled(im_sum[k], -math.sin(turn)))
                value = total(terms)
                out_ref[sending_place(a ^ own, blocks, by_side), here, :] = value
                if start == 0 and a > 0:
                    place = sending_place((a - 1) ^ own, blocks, by_side)
                    out_ref[place, rows : rows + PAD_ROWS, :] = value[:PAD_ROWS]
    place = sending_place((blocks - 1) ^ own, blocks, by_side)
    out_ref[place, rows : rows + PAD_ROWS, :] = jnp.zeros((PAD_ROWS, out_ref.shape[2]), F32)


def product_kernel(
    conjugate, by_side, own_ref, x_ref, spec_ref, high_ref, low_ref, tw_ref, out_ref, split_ref, re_ref, im_ref
):
    blocks, rows = x_ref.shape[0], x_ref.shape[1]
    first_stage(own_ref[0], x_ref, tw_ref, split_ref, 32)
    sign = -1.0 if conjugate else 1.0
    tile = 32
    for k in range(blocks + 1):
        cos_re, cos_im, sin_re, sin_im = second_stage(high_ref[...], low_ref[...], split_ref[k])
        re_ref[k] = cos_re + sin_im
        im_ref[k] = cos_im - sin_re
    for k in range(blocks + 1):
        for start in range(0, rows, tile):
            here = slice(start, start + tile)
            x_re, x_im = re_ref[k, here, :], im_ref[k, here, :]
            h_re, h_im = spec_ref[k, here, :], spec_ref[k, rows + start : rows + start + tile, :] * sign
            store_split(split_ref, k, here, x_re * h_re - x_im * h_im, x_im * h_re + x_re * h_im)
    for k in range(blocks + 1):
        cos_re, cos_im, sin_re, sin_im = second_stage(high_ref[...], low_ref[...], split_ref[k])
        re, im = turned(tw_ref[...], k, cos_re - sin_im, cos_im + sin_re, 1.0)
        re_ref[k] = re
        im_ref[k] = im
    last_stage(own_ref[0], by_side, re_ref, im_ref, out_ref, tile)


def whole_operands(count):
    return [pl.BlockSpec(memory_space=pltpu.SMEM)] + [pl.BlockSpec(memory_space=pltpu.VMEM)] * count


def split_scratch(blocks, rows, width):
    return pltpu.VMEM((blocks + 1, 2 * rows, 2 * width), BF16)


def spectrum(own, x, tables):
    blocks, rows, width = x.shape
    return pl.pallas_call(
        spectrum_kernel,
        out_shape=jax.ShapeDtypeStruct((blocks + 1, 2 * rows, width), F32),
        in_specs=whole_operands(4),
        scratch_shapes=[split_scratch(blocks, rows, width)],
        compiler_params=params(),
        cost_estimate=measured(1.1),
        name="filter_spectrum",
    )(own, x, *tables)


def through_filter(own, x, spec, tables, conjugate, by_side):
    blocks, rows, width = x.shape
    part = pltpu.VMEM((blocks + 1, rows, width), F32)
    return pl.pallas_call(
        functools.partial(product_kernel, conjugate, by_side),
        out_shape=jax.ShapeDtypeStruct((blocks, rows + PAD_ROWS, width), F32),
        in_specs=whole_operands(5),
        scratch_shapes=[split_scratch(blocks, rows, width), part, part],
        compiler_params=params(),
        cost_estimate=measured(0.05),
        name="correlation" if conjugate else "convolution",
    )(own, x, spec, *tables)


def row_number(shape):
    return lax.broadcasted_iota(jnp.int32, shape, 0)


def delayed(x, before, distance):
    moved = pltpu.roll(x, distance, 0)
    rows = row_number(x.shape)
    rim = len(before)
    for row in range(distance):
        moved = jnp.where(rows == row, before[rim - distance + row], moved)
    return moved


def rows_of(block):
    return [block[row : row + 1] for row in range(block.shape[0])]


def short_filter_after(after, last, taps):
    known = last + after
    return [
        total([taps[j : j + 1] * known[len(last) + row - j] for j in range(taps.shape[0])])
        for row in range(len(after))
    ]


def short_filter(x, before, taps):
    result = taps[0:1] * x
    for j in range(1, taps.shape[0]):
        result = result + taps[j : j + 1] * delayed(x, before, j)
    return result


def place_of_part(own_ref, part):
    return part ^ (own_ref[0] % 2)


def pair_specs(rows, pair, rim, count):
    def at(j, own):
        return j ^ (own[0] // 2)

    return {
        "streams": pl.BlockSpec((3, rows, pair), lambda j, own: (0, 0, at(j, own))),
        "before": pl.BlockSpec((3, rim, pair), lambda j, own: (0, 0, at(j, own))),
        "after": pl.BlockSpec((4, rim, pair), lambda j, own: (0, 0, at(j, own))),
        "taps": pl.BlockSpec((3, count, pair), lambda j, own: (0, 0, at(j, own))),
        "vector": pl.BlockSpec((1, pair), lambda j, own: (0, at(j, own))),
        "flat": pl.BlockSpec((rows, pair), lambda j, own: (0, at(j, own))),
        "long": pl.BlockSpec((rows + PAD_ROWS, pair), lambda j, own: (0, at(j, own))),
        "by_pair": pl.BlockSpec((1, 2, rows, pair // 2), lambda j, own: (j, 0, 0, 0)),
        "by_side": pl.BlockSpec((2, 1, rows, pair // 2), lambda j, own: (0, j, 0, 0)),
    }


def over_pairs(kernel, own, parts, specs, ins, outs, out_shape, operands, name, microseconds):
    return pl.pallas_call(
        kernel,
        grid_spec=pltpu.PrefetchScalarGridSpec(
            num_scalar_prefetch=1,
            grid=(parts // 2,),
            in_specs=[specs[i] for i in ins],
            out_specs=[specs[o] for o in outs],
        ),
        out_shape=out_shape,
        compiler_params=params(),
        cost_estimate=measured(0.02 * microseconds),
        name=name,
    )(own, *operands)


def lanes_of(part, block):
    return slice(part * block, (part + 1) * block)


def arrange_kernel(own_ref, x_ref, out_ref, sems):
    blocks, _, block = out_ref.shape
    copies = [
        pltpu.make_async_copy(x_ref.at[:, lanes_of(part, block)], out_ref.at[part ^ own_ref[0]], sems.at[part])
        for part in range(blocks)
    ]
    for copy in copies:
        copy.start()
    for copy in copies:
        copy.wait()


def arrange(own, x, parts):
    rows, width = x.shape
    block = width // parts
    blocks = pl.pallas_call(
        arrange_kernel,
        in_specs=[pl.BlockSpec(memory_space=pltpu.SMEM), pl.BlockSpec(memory_space=pl.ANY)],
        out_specs=pl.BlockSpec(memory_space=pl.ANY),
        out_shape=jax.ShapeDtypeStruct((parts, rows, block), F32),
        scratch_shapes=[pltpu.SemaphoreType.DMA((parts,))],
        compiler_params=pltpu.CompilerParams(vmem_limit_bytes=24 * 1024 * 1024),
        cost_estimate=measured(0.02),
        name="filter_blocks",
    )(own, x)
    return blocks.reshape(parts // 2, 2, rows, block)


def shorts_of(streams_ref, before_ref, taps_ref, lanes):
    return [
        short_filter(streams_ref[i, :, lanes].astype(F32), rows_of(before_ref[i, :, lanes]), taps_ref[i, :, lanes])
        for i in range(3)
    ]


def gate_kernel(own_ref, streams_ref, before_ref, taps_ref, cot_ref, gated_ref, carried_ref):
    block = gated_ref.shape[3]
    for part in range(2):
        lanes = lanes_of(part, block)
        place = place_of_part(own_ref, part)
        short = shorts_of(streams_ref, before_ref, taps_ref, lanes)
        gated_ref[place, 0] = short[1] * short[2]
        carried_ref[place, 0] = cot_ref[:, lanes].astype(F32) * short[0]


def gate(own, streams, before, taps, cotangent, parts, specs):
    _, rows, width = streams.shape
    block = width // parts
    return over_pairs(
        gate_kernel,
        own,
        parts,
        specs,
        ["streams", "before", "taps", "flat"],
        ["by_side", "by_side"],
        [
            jax.ShapeDtypeStruct((2, parts // 2, rows, block), F32),
            jax.ShapeDtypeStruct((2, parts // 2, rows, block), F32),
        ],
        [streams, before, taps, cotangent],
        "short_filters",
        1.2,
    )


def ahead(ext, distance):
    rows = ext.shape[0] - PAD_ROWS
    return (ext if distance == 0 else pltpu.roll(ext, ext.shape[0] - distance, 0))[:rows]


def short_transpose(ext, taps):
    return total([taps[j : j + 1] * ahead(ext, j) for j in range(taps.shape[0])])


def with_rows(block, rows):
    below = jnp.concatenate(rows + [jnp.zeros((PAD_ROWS - len(rows), block.shape[1]), F32)], axis=0)
    return jnp.concatenate([block, below], axis=0)


def prepare_kernel(
    own_ref, streams_ref, before_ref, after_ref, taps_ref, bias_ref, cot_ref,
    query_ref, key_ref, value_ref, cotangent_ref, gated_ref, carried_ref,
):
    rows = streams_ref.shape[1]
    rim = after_ref.shape[1]
    block = query_ref.shape[1] // 2
    for part in range(2):
        lanes = lanes_of(part, block)
        bias = bias_ref[:, lanes]
        short = shorts_of(streams_ref, before_ref, taps_ref, lanes)
        below = [
            short_filter_after(
                rows_of(after_ref[i, :, lanes]),
                rows_of(streams_ref[i, rows - rim :, lanes].astype(F32)),
                taps_ref[i, :, lanes],
            )
            for i in range(3)
        ]
        query, key, value = (with_rows(short[i], below[i]) for i in range(3))
        cotangent = with_rows(cot_ref[:, lanes].astype(F32), rows_of(after_ref[3, :, lanes]))
        query_ref[:, lanes] = short[0]
        key_ref[:, lanes] = key
        value_ref[:, lanes] = value
        cotangent_ref[:, lanes] = cotangent
        gated_ref[:, lanes] = bias * (key * value)
        carried_ref[:, lanes] = bias * (cotangent * query)


def prepare(own, streams, before, after, taps, bias, cotangent, parts, specs):
    _, rows, width = streams.shape
    long = jax.ShapeDtypeStruct((rows + PAD_ROWS, width), F32)
    return over_pairs(
        prepare_kernel,
        own,
        parts,
        specs,
        ["streams", "before", "after", "taps", "vector", "flat"],
        ["flat"] + ["long"] * 5,
        [jax.ShapeDtypeStruct((rows, width), F32)] + [long] * 5,
        [streams, before, after, taps, bias, cotangent],
        "rows_with_rim",
        2.0,
    )


def blocks_of(own_ref, refs):
    block = refs[0].shape[2]
    for j, ref in enumerate(refs):
        for place in range(2):
            first = pl.multiple_of(((2 * j + place) ^ own_ref[0]) * block, block)
            yield ref, place, pl.ds(first, block)


def mix_kernel(count, own_ref, query_ref, cotangent_ref, gated_ref, taps_ref, *refs):
    conv_refs, (mixed_ref, square_ref, grad_ref) = refs[:count], refs[count:]
    rows = query_ref.shape[0]
    block = conv_refs[0].shape[2]
    squares = jnp.zeros((rows, block), F32)
    for conv_ref, place, lanes in blocks_of(own_ref, conv_refs):
        direct = conv_ref[place] + gated_ref[:, lanes]
        mixed = query_ref[:, lanes] * direct[:rows]
        mixed_ref[:, lanes] = mixed
        squares = squares + mixed * mixed
        grad_ref[:, lanes] = short_transpose(cotangent_ref[:, lanes] * direct, taps_ref[0, :, lanes]).astype(BF16)
    square_ref[...] = lax.dot_general(
        jnp.ones((8, block), F32),
        squares,
        (((1,), (1,)), ((), ())),
        precision=lax.Precision.HIGHEST,
        preferred_element_type=F32,
    )[0:1]


def mix(own, query, cotangent, gated, taps, conv):
    rows, width = query.shape
    return pl.pallas_call(
        functools.partial(mix_kernel, len(conv)),
        out_shape=[
            jax.ShapeDtypeStruct((rows, width), F32),
            jax.ShapeDtypeStruct((1, rows), F32),
            jax.ShapeDtypeStruct((rows, width), BF16),
        ],
        in_specs=whole_operands(4 + len(conv)),
        compiler_params=params(),
        cost_estimate=measured(0.05),
        name="mixed_squares",
    )(own, query, cotangent, gated, taps, *conv)


def norm_kernel(channels, mixed_ref, square_ref, gain_ref, normed_ref, sent_ref, sems):
    rows, width = mixed_ref.shape
    squares = jnp.broadcast_to(square_ref[...], (128, rows)).T
    scaling = lax.rsqrt(squares / channels + 1e-06)
    copies = []
    for start in range(0, width, 128):
        lanes = slice(start, start + 128)
        sent_ref[:, lanes] = (mixed_ref[:, lanes] * scaling * gain_ref[:, lanes]).astype(BF16)
        copies.append(
            pltpu.make_async_copy(sent_ref.at[:, lanes], normed_ref.at[:, lanes], sems.at[start // 128])
        )
        copies[-1].start()
    for copy in copies:
        copy.wait()


def norm(channels, mixed, squares, gain):
    rows, width = mixed.shape
    return pl.pallas_call(
        functools.partial(norm_kernel, float(channels)),
        out_shape=jax.ShapeDtypeStruct((rows, width), BF16),
        out_specs=pl.BlockSpec(memory_space=pl.ANY),
        scratch_shapes=[pltpu.VMEM((rows, width), BF16), pltpu.SemaphoreType.DMA((width // 128,))],
        compiler_params=params(),
        cost_estimate=measured(0.02),
        name="norm",
    )(mixed, squares, gain)


def finish_kernel(count, own_ref, key_ref, value_ref, carried_ref, taps_ref, grad_ref, *refs):
    corr_refs, (grads_ref, sent_ref, sems, first_sem) = refs[:count], refs[count:]
    first = pltpu.make_async_copy(grad_ref, grads_ref.at[0], first_sem)
    first.start()
    copies = [first]
    for place_of, (corr_ref, place, lanes) in enumerate(blocks_of(own_ref, corr_refs)):
        gated_grad = corr_ref[place] + carried_ref[:, lanes]
        for i, other_ref in ((1, value_ref), (2, key_ref)):
            grad = short_transpose(gated_grad * other_ref[:, lanes], taps_ref[i, :, lanes])
            sent_ref[i - 1, :, lanes] = grad.astype(BF16)
        copy = pltpu.make_async_copy(
            sent_ref.at[:, :, lanes], grads_ref.at[1:3, :, lanes], sems.at[place_of]
        )
        copy.start()
        copies.append(copy)
    for copy in copies:
        copy.wait()


def finish(own, key, value, carried, taps, grad, corr):
    rows, width = grad.shape
    blocks = 2 * len(corr)
    return pl.pallas_call(
        functools.partial(finish_kernel, len(corr)),
        out_shape=jax.ShapeDtypeStruct((3, rows, width), BF16),
        in_specs=whole_operands(5 + len(corr)),
        out_specs=pl.BlockSpec(memory_space=pl.ANY),
        scratch_shapes=[
            pltpu.VMEM((2, rows, width), BF16),
            pltpu.SemaphoreType.DMA((blocks,)),
            pltpu.SemaphoreType.DMA,
        ],
        compiler_params=params(),
        cost_estimate=measured(0.05),
        name="stream_grads",
    )(own, key, value, carried, taps, grad, *corr)


def swapped(block, apart, name):
    route = [(i, i ^ apart) for i in range(lax.axis_size("seq"))]
    with jax.named_scope(f"{name}_over_{apart}"):
        return lax.ppermute(block, "seq", route)


def summed_over(block, axis):
    count = lax.axis_size(axis)
    if count & (count - 1):
        return lax.psum(block, axis)
    result = block
    for apart in range(1, count):
        with jax.named_scope(f"squares_over_{apart}"):
            result = result + lax.ppermute(block, axis, [(i, i ^ apart) for i in range(count)])
    return result


def tied(value, other):
    return lax.optimization_barrier((value, other))


def within_pairs(name, block):
    return swapped(block, 1, name)


def between_pairs(name, blocks):
    order = list(range(2, len(blocks))) + [1]
    got = {j: swapped(blocks[j], 2 * j, name) for j in order}
    return [blocks[0]] + [got[j] for j in range(1, len(blocks))]


def together(blocks, edges):
    width = blocks.shape[-1]
    return jnp.concatenate([blocks.reshape(-1, width), edges.reshape(-1, width)], axis=0)


def apart_again(rows, blocks, edges):
    count = blocks.size // rows.shape[1]
    return rows[:count].reshape(blocks.shape), rows[count:].reshape(edges.shape)


def rows_after(own, came):
    after = jnp.where(own % 2 == 0, came[0], 0.0)
    pair = own // 2
    for k in range(1, len(came)):
        follows = (own % 2 == 1) & (pair ^ (pair + 1) == 2**k - 1)
        after = jnp.where(follows, came[k], after)
    return after


def in_turn(blocks, earlier):
    blocks, earlier = list(blocks), list(earlier)
    for j in range(2, len(blocks)):
        blocks[j], earlier[j] = tied(blocks[j], earlier[j])
    return blocks, earlier


def sides_of(got):
    return jnp.stack([block[0] for block in got]), jnp.stack([block[1] for block in got])


def paired(kept, other):
    return [jnp.stack([kept[j], other[j]]) for j in range(kept.shape[0])]


def as_line(blocks):
    return blocks.reshape((-1,) + blocks.shape[2:])


def local(streams, short_taps, long_filter, skip_bias, norm_gain, cotangent):
    parts = lax.axis_size("seq")
    rows, width = cotangent.shape
    rim = short_taps.shape[1] - 1
    tables = stage_tables(parts, rows)
    specs = pair_specs(rows, 2 * width // parts, rim, short_taps.shape[1])
    own = lax.axis_index("seq").astype(jnp.int32)[None]
    bias, gain = skip_bias[None], norm_gain[None]

    filter_sent = arrange(own, long_filter, parts)
    filter_got = between_pairs("filter", filter_sent)
    streams_later, filter_got[0] = tied(streams, filter_got[0])
    before = shift_along(streams_later[:, rows - rim :].astype(F32), "seq", 1)
    edges = jnp.concatenate([streams_later[:, :rim].astype(F32), cotangent[None, :rim].astype(F32)], axis=0)
    gated, carried = gate(own, streams, before, short_taps, cotangent, parts, specs)

    gated_other = within_pairs("gated", gated[1])
    carried_gone = carried[1]
    carried_gone, gated_other = tied(carried_gone, gated_other)
    gated_got = between_pairs("gated", paired(gated[0], gated_other))
    filter_kept, filter_gone = sides_of(filter_got)
    filter_other = within_pairs("filter", filter_gone)
    filter_blocks = paired(filter_kept, filter_other)
    carried_other, edges_other = apart_again(within_pairs("carried", together(carried_gone, edges)), carried_gone, edges)
    carried_pairs = paired(carried[0], carried_other)
    spec = spectrum(own, as_line(jnp.stack(filter_blocks)), tables)
    shape = (rows + PAD_ROWS, width // parts)
    gated_blocks = as_line(jnp.stack(gated_got))
    carried_pairs, gated_got[1] = tied(carried_pairs, gated_got[1])
    conv_sent = through_filter(own, gated_blocks, spec, tables, False, True).reshape((2, parts // 2) + shape)
    carried_pairs = list(carried_pairs)
    steps = [j for j in range(1, parts // 2) if j & (j + 1) == 0]
    alone = carried_pairs[0]
    for j in steps:
        carried_pairs[j] = together(carried_pairs[j], edges_other)
    carried_got = between_pairs("carried", carried_pairs)
    edges_got = []
    for j in steps:
        carried_got[j], came = apart_again(carried_got[j], alone, edges)
        edges_got.append(came)
    conv_pairs = paired(conv_sent[0], within_pairs("conv", conv_sent[1]))
    conv_pairs, carried_got = in_turn(conv_pairs, carried_got)
    carried_blocks = jnp.stack(carried_got)
    conv_got = between_pairs("conv", conv_pairs)
    corr_sent = through_filter(own, as_line(carried_blocks), spec, tables, True, True).reshape((2, parts // 2) + shape)
    corr_pairs = paired(corr_sent[0], within_pairs("corr", corr_sent[1]))
    corr_pairs, conv_got[2] = tied(corr_pairs, conv_got[2])
    after = rows_after(own[0], [edges_other] + edges_got)
    after, conv_got[1] = tied(after, conv_got[1])
    query, key, value, later, gated_direct, carried_direct = prepare(
        own, streams, before, after, short_taps, bias, cotangent, parts, specs
    )
    corr_pairs, query = tied(corr_pairs, query)
    corr_got = between_pairs("corr", corr_pairs)
    query, corr_got[1] = tied(query, corr_got[1])
    mixed, squares, grad = mix(own, query, later, gated_direct, short_taps, conv_got)
    squares = summed_over(squares, "ch")
    normed = norm(width * lax.axis_size("ch"), mixed, squares, gain)
    grads = finish(own, key, value, carried_direct, short_taps, grad, corr_got)
    return normed, grads


EXACTNESS = lax.Precision.HIGHEST


def passed_along(block, axis, distance):
    devices = range(lax.axis_size(axis))
    route = [(i - distance, i) for i in devices if i - distance in devices]
    return lax.ppermute(block, axis, route)


def counting(amount):
    return jnp.arange(amount, dtype=jnp.int32)


def angle_pair(left_index, right_index, period, turning):
    product = left_index[:, None] * right_index[None, :] % period
    angles = product.astype(jnp.float32) * (turning * 2.0 * math.pi / period)
    return (jnp.cos(angles), jnp.sin(angles))


def neighbour_rows(edge_rows, offset):
    return passed_along(edge_rows, "seq", offset)


def swap_middle(blocks):
    return lax.all_to_all(blocks, "seq", split_axis=1, concat_axis=0, tiled=True)


def spread_forward(series):
    length, series_count, chan_width = series.shape
    devices = lax.axis_size("seq")
    position = lax.axis_index("seq")
    sub_rows = length // devices
    period = 2 * length * devices
    gathered = swap_middle(series.reshape(1, length, series_count, chan_width))
    cos_a, sin_a = angle_pair(counting(2 * devices), counting(devices), 2 * devices, -1.0)
    real_part = jnp.einsum("ka,absc->bksc", cos_a, gathered, precision=EXACTNESS)
    imag_part = jnp.einsum("ka,absc->bksc", sin_a, gathered, precision=EXACTNESS)
    spike_locations = position * sub_rows + counting(sub_rows)
    turn_cos, turn_sin = angle_pair(spike_locations, counting(2 * devices), period, -1.0)
    turn_cos = turn_cos[:, :, None, None]
    turn_sin = turn_sin[:, :, None, None]
    turned = jnp.concatenate(
        [real_part * turn_cos - imag_part * turn_sin, real_part * turn_sin + imag_part * turn_cos],
        axis=2,
    )
    swapped = swap_middle(turned)
    cos_b, sin_b = angle_pair(counting(length), counting(length), length, -1.0)
    primary = jnp.einsum("jb,bksc->jksc", cos_b, swapped, precision=EXACTNESS)
    second = jnp.einsum("jb,bksc->jksc", sin_b, swapped, precision=EXACTNESS)
    return (
        primary[:, :, :series_count] - second[:, :, series_count:],
        primary[:, :, series_count:] + second[:, :, :series_count],
    )


def spread_inverse(spec_re, spec_im):
    length, pair_rows, series_count, chan_width = spec_re.shape
    devices = lax.axis_size("seq")
    position = lax.axis_index("seq")
    sub_rows = length // devices
    period = 2 * length * devices
    cos_b, sin_b = angle_pair(counting(length), counting(length), length, 1.0)
    merged = jnp.concatenate([spec_re, spec_im], axis=2)
    primary = jnp.einsum("bj,jksc->kbsc", cos_b, merged, precision=EXACTNESS)
    second = jnp.einsum("bj,jksc->kbsc", sin_b, merged, precision=EXACTNESS)
    turned = jnp.concatenate(
        [
            primary[:, :, :series_count] - second[:, :, series_count:],
            primary[:, :, series_count:] + second[:, :, :series_count],
        ],
        axis=2,
    )
    swapped = swap_middle(turned)
    spike_locations = position * sub_rows + counting(sub_rows)
    turn_cos, turn_sin = angle_pair(counting(2 * devices), spike_locations, period, 1.0)
    turn_cos = turn_cos[:, :, None, None]
    turn_sin = turn_sin[:, :, None, None]
    real_part = swapped[:, :, :series_count]
    imag_part = swapped[:, :, series_count:]
    rotated_re = real_part * turn_cos - imag_part * turn_sin
    rotated_im = real_part * turn_sin + imag_part * turn_cos
    cos_a, sin_a = angle_pair(counting(devices), counting(2 * devices), 2 * devices, 1.0)
    result = jnp.einsum("ak,kbsc->basc", cos_a, rotated_re, precision=EXACTNESS) - jnp.einsum(
        "ak,kbsc->basc", sin_a, rotated_im, precision=EXACTNESS
    )
    returned = swap_middle(result / period)
    return returned.reshape(length, -1, chan_width)


def local_general(streams, short_taps, long_filter, skip_bias, norm_gain, cotangent):
    row_count = streams.shape[1]
    chan_width = streams.shape[2]
    rim_rows = short_taps.shape[1] - 1
    widened = streams.astype(jnp.float32)
    before = neighbour_rows(widened[:, row_count - rim_rows :, :], 1)
    extended = jnp.concatenate([before, widened], axis=1)
    shorts = jnp.zeros_like(widened)
    for offset in range(short_taps.shape[1]):
        shorts = (
            shorts
            + short_taps[:, offset, None, :]
            * extended[:, rim_rows - offset : rim_rows - offset + row_count, :]
        )
    short_q, short_k, short_v = (shorts[0], shorts[1], shorts[2])
    gated_input = short_k * short_v
    cot_wide = cotangent.astype(jnp.float32)
    carried = cot_wide * short_q
    series = jnp.stack([gated_input, long_filter, carried], axis=1)
    spec_re, spec_im = spread_forward(series)
    series_axis = 2
    gated_re = lax.index_in_dim(spec_re, 0, series_axis, keepdims=False)
    gated_im = lax.index_in_dim(spec_im, 0, series_axis, keepdims=False)
    filter_re = lax.index_in_dim(spec_re, 1, series_axis, keepdims=False)
    filter_im = lax.index_in_dim(spec_im, 1, series_axis, keepdims=False)
    carry_re = lax.index_in_dim(spec_re, 2, series_axis, keepdims=False)
    carry_im = lax.index_in_dim(spec_im, 2, series_axis, keepdims=False)
    output_re = filter_re * gated_re - filter_im * gated_im
    output_im = filter_re * gated_im + filter_im * gated_re
    backward_re = filter_re * carry_re + filter_im * carry_im
    backward_im = filter_re * carry_im - filter_im * carry_re
    inverse_re = jnp.stack([output_re, backward_re], axis=series_axis)
    inverse_im = jnp.stack([output_im, backward_im], axis=series_axis)
    result = spread_inverse(inverse_re, inverse_im)
    convolved = result[:, 0]
    correlated = result[:, 1]
    direct = convolved + skip_bias * gated_input
    mixed_out = short_q * direct
    square_sum = lax.psum(jnp.sum(mixed_out * mixed_out, axis=1), "ch")
    scaling = lax.rsqrt(square_sum[:, None] / (chan_width * lax.axis_size("ch")) + 1e-06)
    normed = (mixed_out * scaling * norm_gain).astype(jnp.bfloat16)
    gated_grad = correlated + skip_bias * carried
    short_grad = jnp.stack([cot_wide * direct, gated_grad * short_v, gated_grad * short_k])
    following = neighbour_rows(short_grad[:, :rim_rows, :], -1)
    grad_ext = jnp.concatenate([short_grad, following], axis=1)
    grads = jnp.zeros_like(short_grad)
    for offset in range(short_taps.shape[1]):
        grads = grads + short_taps[:, offset, None, :] * grad_ext[:, offset : offset + row_count, :]
    return (normed, grads.astype(jnp.bfloat16))


def solution(mesh):
    placed = (
        P(None, "seq", "ch"),
        P(None, None, "ch"),
        P("seq", "ch"),
        P("ch"),
        P("ch"),
        P("seq", "ch"),
    )

    def program(streams, short_taps, long_filter, skip_bias, norm_gain, cotangent):
        parts = mesh.shape["seq"]
        width = cotangent.shape[1] // mesh.shape["ch"]
        lanes_filled = width % (128 * parts) == 0 and parts in (4, 8, 16)
        return jax.shard_map(
            local if lanes_filled else local_general,
            mesh=mesh,
            in_specs=placed,
            out_specs=(P("seq", "ch"), P(None, "seq", "ch")),
            check_vma=False,
        )(streams, short_taps, long_filter, skip_bias, norm_gain, cotangent)

    return program
```
